32 devices in a mesh: dp: 16 (over z, y, core), seq: 2 (over x).
Axes of the slice: x: 2, y: 2, z: 4, core: 2. Of those that a mesh axis runs over, the one named last changes fastest.
Arguments:
- tokens: bfloat16 [16, 1024, 512], P('dp', 'seq')
- cell_starts: int32 [16, 4], P('dp'), may hold values from 0 to 1023, as said below
- generate_flags: int32 [16, 1024], P('dp'), may hold values 0 or 1
- valid_mask: int32 [16, 1024], P('dp'), may hold values from 0 to 1
- in_weight: bfloat16 [2, 512, 1536], replicated, may hold values from -0.25 to 0.25
- out_weight: bfloat16 [2, 512, 512], replicated, may hold values from -2 to 2
- up_weight: bfloat16 [2, 512, 512], replicated, may hold values from -0.25 to 0.25
- down_weight: bfloat16 [2, 512, 512], replicated, may hold values from -0.25 to 0.25
- norm_gains: float32 [2, 2, 512], replicated, may hold values from 0.25 to 1.75
- biases: float32 [2, 7, 512], replicated, may hold values from -3 to 3
- out_grad: bfloat16 [16, 1024, 512], P('dp', 'seq'), may hold values from -6 to 6
Outputs:
- layer_output: bfloat16 [16, 1024, 512], P('dp', 'seq')
- input_grad: float32 [16, 1024, 512], P('dp', 'seq')
- in_weight_grad: float32 [2, 512, 1536], replicated
- out_weight_grad: float32 [2, 512, 512], replicated
- up_weight_grad: float32 [2, 512, 512], replicated
- down_weight_grad: float32 [2, 512, 512], replicated
- norm_gains_grad: float32 [2, 2, 512], replicated
- biases_grad: float32 [2, 7, 512], replicated
- stream_rms: float32 [2, 3], replicated
The draws below stay inside these ranges and needn't reach their ends.
Inputs may be any that keep to these rules, and one draw needn't show every extreme that they name: `cell_starts`: in each row the 4 starts rise strictly from 0; one cell of each row, which one drawn from the seed, begins within the first 512 positions and ends within the last 512.
All inputs are finite; a program needn't handle non-finite values. No bound on the sum of `generate_flags` on one device may be relied on, other than what follows from the above.
Results may differ from the reference program's by a relative error of at most 0.035.
Values may be sent and summed in bfloat16 or wider, within the bound.
A program may use at most 192 MiB of HBM per device.

```python
import math
import jax
import jax.numpy as jnp
from jax import lax

D = 512
FF = 512
HEADS = 8
HEAD_DIM = 64
LAYERS = 2
CELLS = 4
SEQ_LEN = 1024
DEV_TOK = 512
ROWS = 16


def draw_tokens(key, part):
    key = jax.random.fold_in(key, 11)
    row_place = jnp.arange(ROWS, dtype=jnp.float32)[:, None, None] / ROWS
    token_place = jnp.arange(SEQ_LEN, dtype=jnp.float32)[None, :, None] / SEQ_LEN
    scale = jnp.exp(row_place * jnp.log(2.0) + token_place * (0.25 * jnp.log(3.0)))
    base = jax.random.normal(key, (ROWS, SEQ_LEN, D), jnp.float32)
    return (base * scale).astype(jnp.bfloat16)


def draw_valid_mask(key, part):
    key = jax.random.fold_in(key, 37)
    threshold = 35 + 60 * jnp.arange(ROWS, dtype=jnp.int32)[:, None] // ROWS
    roll = jax.random.randint(key, (ROWS, SEQ_LEN), 0, 100)
    return (roll < threshold).astype(jnp.int32)


def draw_cell_starts(key, part):
    key = jax.random.fold_in(key, 23)
    pick_key, first_key, last_key = jax.random.split(key, 3)
    slack = max(DEV_TOK // 2 - CELLS, 1)
    chosen = jax.random.randint(pick_key, (ROWS, 1), 0, CELLS)
    leading = jax.random.randint(first_key, (ROWS, 1), 0, slack)
    trailing = jax.random.randint(last_key, (ROWS, 1), 0, slack)
    after = CELLS - 1 - chosen
    begin = jnp.where(chosen > 0, chosen + leading, 0)
    finish = SEQ_LEN - after - jnp.where(after > 0, trailing, 0)
    index = jnp.arange(CELLS, dtype=jnp.int32)[None, :]
    before_start = index * begin // jnp.maximum(chosen, 1)
    after_start = finish + (index - chosen - 1) * (SEQ_LEN - finish) // jnp.maximum(after, 1)
    return jnp.where(index < chosen, before_start, jnp.where(index == chosen, begin, after_start)).astype(jnp.int32)


def with_ends(values, key, low, largest):
    shape = values.shape
    index_at = [jax.random.randint(jax.random.fold_in(key, axis), (), 0, shape[axis]) for axis in range(len(shape))]
    values = values.at[tuple(index_at)].set(low)
    longest = shape.index(max(shape))
    index_at[longest] = (index_at[longest] + 1) % shape[longest]
    return values.at[tuple(index_at)].set(largest)


def block_scale(own_key, extent, shards, least, high):
    level = 1.0
    for dim, parts in shards:
        steps = jax.random.uniform(jax.random.fold_in(jax.random.fold_in(own_key, 6), dim), (parts,), jnp.float32, least / len(shards), high / len(shards))
        level = level * jnp.repeat(jnp.exp(steps), extent[dim] // parts).reshape((-1,) + (1,) * (len(extent) - 1 - dim))
    return level


def normal_values(stream_key, dims, scale, reach, pieces=(), held_as=jnp.bfloat16):
    loudness = block_scale(stream_key, dims, pieces, -0.22, 0.18) if pieces else 1.0
    entries = jax.random.normal(stream_key, dims, jnp.float32) * scale * loudness
    return jnp.minimum(jnp.maximum(entries, -reach), reach).astype(held_as)


def setup_inputs(seed: int = 0) -> dict:
    seeds = jax.random.split(jax.random.key(seed), 12)
    tokens = draw_tokens(jax.random.fold_in(seeds[11], 71), 0)
    cell_starts = draw_cell_starts(jax.random.fold_in(seeds[11], 71), 0)
    generate_flags = with_ends((jax.random.randint(seeds[2], (ROWS, SEQ_LEN), 0, 4) < 1).astype(jnp.int32), jax.random.fold_in(seeds[2], 1), 0, 1)
    valid_mask = draw_valid_mask(jax.random.fold_in(seeds[11], 71), 0)
    in_weight = normal_values(seeds[4], (LAYERS, D, 3 * D), D ** -0.5, 0.25)
    out_weight = normal_values(seeds[5], (LAYERS, D, D), (D // 64) ** -0.5, 2.0)
    up_weight = normal_values(seeds[6], (LAYERS, D, FF), D ** -0.5, 0.25)
    down_weight = normal_values(seeds[7], (LAYERS, FF, D), FF ** -0.5, 0.25)
    norm_gains = jnp.clip(1.0 + 0.15 * jax.random.normal(seeds[8], (LAYERS, 2, D), jnp.float32), 0.25, 1.75)
    biases = normal_values(seeds[9], (LAYERS, 7, D), 0.5, 3.0, (), jnp.float32)
    out_grad = normal_values(seeds[10], (ROWS, SEQ_LEN, D), 1.0, 6.0, ((0, 16), (1, 2)))
    return {"tokens": tokens, "cell_starts": cell_starts, "generate_flags": generate_flags, "valid_mask": valid_mask, "in_weight": in_weight, "out_weight": out_weight, "up_weight": up_weight, "down_weight": down_weight, "norm_gains": norm_gains, "biases": biases, "out_grad": out_grad}


@jax.custom_vjp
def low(v):
    return lax.optimization_barrier(v.astype(jnp.bfloat16)).astype(jnp.float32)

@jax.custom_vjp
def low_back(v):
    return v

def low_keep(v):
    return (low(v), None)

def low_pass(kept, grad):
    return (grad,)

def back_keep(v):
    return (v, None)

def back_low(kept, grad):
    return (low(grad),)
low.defvjp(low_keep, low_pass)
low_back.defvjp(back_keep, back_low)
HIGH = lax.Precision.HIGHEST
EPS = 1e-05
NEG = -1e+30

def product(left, right):
    return jnp.dot(left, right, precision=HIGH)

def block_width(count):
    for option in range(1024, 255, -1):
        if count % option == 0:
            return option
    return count

def segment_ids(starts_row, positions):
    return lax.optimization_barrier(jnp.sum((positions[:, None] >= starts_row[None, :]).astype(jnp.int32), axis=1)) - 1

def norm_rows(total, gain, shift):
    mean = lax.optimization_barrier(jnp.mean(total, axis=-1, keepdims=True))
    centred = total - mean
    spread = lax.optimization_barrier(jnp.mean(centred * centred, axis=-1, keepdims=True))
    return centred * lax.rsqrt(spread + EPS) * gain + shift

def attention(queries, keys, values, segments, key_good):
    length = queries.shape[0]
    width = block_width(length)
    scale = 1.0 / math.sqrt(HEAD_DIM)
    query_heads = queries.reshape(length, HEADS, HEAD_DIM)
    key_heads = keys.reshape(length, HEADS, HEAD_DIM)
    value_heads = values.reshape(length, HEADS, HEAD_DIM)
    key_pos = jnp.arange(length, dtype=jnp.int32)

    def one_block(index):
        begin = index * width
        query_rows = lax.dynamic_slice_in_dim(query_heads, begin, width, 0)
        query_pos = begin + jnp.arange(width, dtype=jnp.int32)
        query_seg = lax.dynamic_slice_in_dim(segments, begin, width, 0)
        allowed = (query_seg[:, None] == segments[None, :]) & (key_good[None, :] | (query_pos[:, None] == key_pos[None, :]))
        scores = low_back(jnp.einsum('qhd,khd->hqk', query_rows, key_heads, precision=HIGH) * scale)
        masked = jnp.where(allowed[None], scores, NEG)
        top = lax.optimization_barrier(jnp.max(masked, axis=-1, keepdims=True))
        weights = jnp.where(allowed[None], jnp.exp(masked - top), 0.0)
        total = lax.optimization_barrier(jnp.sum(weights, axis=-1))
        summed = jnp.einsum('hqk,khd->qhd', low(weights), value_heads, precision=HIGH)
        return (summed / total.T[:, :, None]).reshape(width, HEADS * HEAD_DIM)
    blocks = lax.map(jax.checkpoint(one_block), jnp.arange(length // width, dtype=jnp.int32))
    return blocks.reshape(length, HEADS * HEAD_DIM)

def layer(stream, in_matrix, out_matrix, up_matrix, down_matrix, gain_pair, bias_rows, segments, key_good, valid_f):
    model = stream.shape[1]
    zeros = jnp.zeros((model,), jnp.float32)
    mixed = product(low(stream), in_matrix) + jnp.concatenate([bias_rows[0], zeros, bias_rows[1]])
    mixed = low(low_back(mixed))
    attended = attention(mixed[:, :model], mixed[:, model:2 * model], mixed[:, 2 * model:], segments, key_good)
    branch = low_back(product(low(low_back(attended)), out_matrix) + bias_rows[2])
    hidden = norm_rows(stream + branch, gain_pair[0], bias_rows[5])
    inner = low_back(product(low(hidden), up_matrix) + bias_rows[3])
    ff_out = low_back(product(low(jax.nn.gelu(inner, approximate=False)), down_matrix) + bias_rows[4])
    result = norm_rows(hidden + ff_out, gain_pair[1], bias_rows[6])
    squares = jnp.stack([jnp.sum(valid_f * lax.optimization_barrier(jnp.sum(part * part, axis=-1))) for part in (stream, branch, ff_out)])
    return (result, squares)

def reference(tokens, cell_starts, generate_flags, valid_mask, in_weight, out_weight, up_weight, down_weight, norm_gains, biases, out_grad):
    params = tuple((weight_arg.astype(jnp.float32) for weight_arg in (in_weight, out_weight, up_weight, down_weight, norm_gains, biases)))
    positions = jnp.arange(SEQ_LEN, dtype=jnp.int32)

    def row_step(carry, row):
        sums, square_sums, count = carry
        row_tokens, row_grad, row_starts, row_flags, row_valid = row
        segments = segment_ids(row_starts, positions)
        key_good = row_valid * (1 - row_flags) > 0
        valid_f = row_valid.astype(jnp.float32)

        def forward(stream, in_all, out_all, up_all, down_all, gains_all, biases_all):
            stats = []
            for layer_index in range(LAYERS):
                stream, squares = layer(stream, in_all[layer_index], out_all[layer_index], up_all[layer_index], down_all[layer_index], gains_all[layer_index], biases_all[layer_index], segments, key_good, valid_f)
                stats.append(squares)
            return (stream, jnp.stack(stats))
        result, pull, squares = jax.vjp(forward, row_tokens.astype(jnp.float32), *params, has_aux=True)
        grads = pull(row_grad.astype(jnp.float32))
        sums = tuple((older + newer for older, newer in zip(sums, grads[1:])))
        return ((sums, square_sums + squares, count + jnp.sum(valid_f)), (result.astype(jnp.bfloat16), grads[0]))
    start_carry = (tuple((jnp.zeros_like(weight_arg) for weight_arg in params)), jnp.zeros((LAYERS, 3), jnp.float32), jnp.zeros((), jnp.float32))
    final, outputs = lax.scan(row_step, start_carry, (tokens, out_grad, cell_starts, generate_flags, valid_mask))
    sums, square_sums, count = final
    stream_rms = jnp.sqrt(square_sums / (count * D))
    return (outputs[0], outputs[1], sums[0], sums[1], sums[2], sums[3], sums[4], sums[5], stream_rms)
```

```python
import functools
import math

import jax
import jax.numpy as jnp
from jax import lax
from jax.experimental import pallas as pl
from jax.experimental.pallas import tpu as pltpu
from jax.sharding import PartitionSpec as P

HEADS = 8
HEAD_DIM = 64
LAYERS = 2


EPS = 1e-05
NEG = -1e30


def block_width(count):
    for option in range(1024, 255, -1):
        if count % option == 0:
            return option
    return count


def segment_ids(starts_row, positions):
    return jnp.sum((positions[:, None] >= starts_row[None, :]).astype(jnp.int32), axis=1) - 1


def norm_rows(total, gain, shift):
    mean = jnp.mean(total, axis=-1, keepdims=True)
    centred = total - mean
    spread = jnp.mean(centred * centred, axis=-1, keepdims=True)
    inverse = lax.rsqrt(spread + EPS)
    normed = centred * inverse
    return (normed * gain + shift, normed, inverse)


def norm_back(grad, normed, inverse, gain):
    scaled = grad * gain
    return inverse * (
        scaled
        - jnp.mean(scaled, axis=-1, keepdims=True)
        - normed * jnp.mean(scaled * normed, axis=-1, keepdims=True)
    )


def gelu_slope(inner):
    return (
        0.5 * (1.0 + jax.scipy.special.erf(inner * 0.7071067811865476))
        + inner * jnp.exp(-0.5 * inner * inner) * 0.3989422804014327
    )


def make_mask(query_pos, query_seg, starts_row, key_ok_row):

    def mask_for(begin, width):
        key_pos = begin + jnp.arange(width, dtype=jnp.int32)
        key_seg = segment_ids(starts_row, key_pos)
        key_good = lax.dynamic_slice_in_dim(key_ok_row, begin, width, 0) > 0
        return (query_seg[:, None] == key_seg[None, :]) & (
            key_good[None, :] | (query_pos[:, None] == key_pos[None, :])
        )

    return mask_for


def make_attend(query_heads, mask_for, scale):

    def attend(carry, piece, start):
        count = piece.shape[0]
        width = block_width(count)
        model = piece.shape[1] // 2

        def attend_one_block(step, state):
            best, total, summed = state
            begin = step * width
            block = lax.dynamic_slice_in_dim(piece, begin, width, 0)
            key_heads = block[:, :model].reshape(width, HEADS, HEAD_DIM)
            value_heads = block[:, model:].reshape(width, HEADS, HEAD_DIM)
            allowed = mask_for(start + begin, width)[None]
            scores = (
                jnp.einsum(
                    "qhd,khd->hqk", query_heads, key_heads, preferred_element_type=jnp.float32
                )
                * scale
            )
            scores = jnp.where(allowed, scores, NEG)
            new_best = jnp.maximum(best, jnp.max(scores, axis=-1))
            factor = jnp.exp(best - new_best)
            weights = jnp.where(allowed, jnp.exp(scores - new_best[:, :, None]), 0.0)
            total = total * factor + jnp.sum(weights, axis=-1)
            update = jnp.einsum(
                "hqk,khd->qhd",
                weights.astype(jnp.bfloat16),
                value_heads,
                preferred_element_type=jnp.float32,
            )
            summed = summed * factor.T[:, :, None] + update
            return (new_best, total, summed)

        return lax.fori_loop(0, count // width, attend_one_block, carry)

    return attend


def make_back(query_heads, grad_heads, log_total, delta, mask_for, scale):

    def back(carry, piece, start):
        count = piece.shape[0]
        width = block_width(count)
        model = piece.shape[1] // 2

        def back_one_block(step, state):
            query_grad, full_grad = state
            begin = step * width
            block = lax.dynamic_slice_in_dim(piece, begin, width, 0)
            key_heads = block[:, :model].reshape(width, HEADS, HEAD_DIM)
            value_heads = block[:, model:].reshape(width, HEADS, HEAD_DIM)
            allowed = mask_for(start + begin, width)[None]
            scores = (
                jnp.einsum(
                    "qhd,khd->hqk", query_heads, key_heads, preferred_element_type=jnp.float32
                )
                * scale
            )
            probs = jnp.where(allowed, jnp.exp(scores - log_total[:, :, None]), 0.0)
            prob_grad = jnp.einsum(
                "qhd,khd->hqk", grad_heads, value_heads, preferred_element_type=jnp.float32
            )
            score_grad = (probs * (prob_grad - delta[:, :, None])).astype(jnp.bfloat16)
            query_grad = (
                query_grad
                + jnp.einsum(
                    "hqk,khd->qhd", score_grad, key_heads, preferred_element_type=jnp.float32
                )
                * scale
            )
            key_grad = (
                jnp.einsum(
                    "hqk,qhd->khd", score_grad, query_heads, preferred_element_type=jnp.float32
                )
                * scale
            )
            value_grad = jnp.einsum(
                "hqk,qhd->khd",
                probs.astype(jnp.bfloat16),
                grad_heads,
                preferred_element_type=jnp.float32,
            )
            update = jnp.concatenate(
                [key_grad.reshape(width, model), value_grad.reshape(width, model)], axis=1
            )
            place = start + begin
            current = lax.dynamic_slice_in_dim(full_grad, place, width, 0)
            full_grad = lax.dynamic_update_slice_in_dim(full_grad, current + update, place, 0)
            return (query_grad, full_grad)

        return lax.fori_loop(0, count // width, back_one_block, carry)

    return back


def local(
    tokens,
    cell_starts,
    generate_flags,
    valid_mask,
    in_weight,
    out_weight,
    up_weight,
    down_weight,
    norm_gains,
    biases,
    out_grad,
):
    rows = tokens.shape[1]
    model = tokens.shape[2]
    scale = 1.0 / math.sqrt(HEAD_DIM)
    first = lax.axis_index("seq") * rows
    query_pos = first + jnp.arange(rows, dtype=jnp.int32)
    starts_row = cell_starts[0]
    key_ok_row = valid_mask[0] * (1 - generate_flags[0])
    mask_for = make_mask(query_pos, segment_ids(starts_row, query_pos), starts_row, key_ok_row)
    valid_here = lax.dynamic_slice_in_dim(valid_mask[0], first, rows, 0).astype(jnp.float32)
    stream = tokens[0].astype(jnp.float32)
    stream_low = tokens[0]
    kept = []
    squares = []
    for layer in range(LAYERS):
        bias_rows = biases[layer]
        gains_pair = norm_gains[layer]
        mixed = jnp.dot(
            stream_low, in_weight[layer], preferred_element_type=jnp.float32
        ) + jnp.concatenate([bias_rows[0], jnp.zeros((model,), jnp.float32), bias_rows[1]])
        mixed_low = mixed.astype(jnp.bfloat16)
        query_heads = mixed_low[:, :model].reshape(rows, HEADS, HEAD_DIM)
        key_value = mixed_low[:, model:]
        attend = make_attend(query_heads, mask_for, scale)
        state = (
            jnp.full((HEADS, rows), NEG, jnp.float32),
            jnp.zeros((HEADS, rows), jnp.float32),
            jnp.zeros((rows, HEADS, HEAD_DIM), jnp.float32),
        )
        gathered = key_value
        best, total, summed = attend(
            state, lax.all_gather(key_value, "seq", axis=0, tiled=True), jnp.int32(0)
        )
        attended = (summed / total.T[:, :, None]).reshape(rows, model)
        log_total = best + jnp.log(total)
        attended_low = attended.astype(jnp.bfloat16)
        branch = (
            jnp.dot(attended_low, out_weight[layer], preferred_element_type=jnp.float32)
            + bias_rows[2]
        )
        hidden, normed_one, inverse_one = norm_rows(stream + branch, gains_pair[0], bias_rows[5])
        hidden_low = hidden.astype(jnp.bfloat16)
        inner = (
            jnp.dot(hidden_low, up_weight[layer], preferred_element_type=jnp.float32) + bias_rows[3]
        )
        active_low = jax.nn.gelu(inner, approximate=False).astype(jnp.bfloat16)
        ff_out = (
            jnp.dot(active_low, down_weight[layer], preferred_element_type=jnp.float32)
            + bias_rows[4]
        )
        result, normed_two, inverse_two = norm_rows(hidden + ff_out, gains_pair[1], bias_rows[6])
        squares.append(
            jnp.stack(
                [
                    jnp.sum(valid_here * jnp.sum(part * part, axis=-1))
                    for part in (stream, branch, ff_out)
                ]
            )
        )
        kept.append(
            (
                stream_low,
                query_heads,
                gathered,
                attended,
                attended_low,
                log_total,
                normed_one,
                inverse_one,
                hidden_low,
                inner,
                active_low,
                normed_two,
                inverse_two,
            )
        )
        stream = result
        stream_low = result.astype(jnp.bfloat16)
    layer_output = stream.astype(jnp.bfloat16)[None]
    square_local = jnp.stack(squares)
    count_local = jnp.sum(valid_here)
    square_total, count_total = lax.psum((square_local, count_local), ("dp", "seq"))
    grad = out_grad[0].astype(jnp.float32)
    length = rows * lax.axis_size("seq")
    collected = [None] * LAYERS
    for layer in reversed(range(LAYERS)):
        (
            stream_low,
            query_heads,
            gathered,
            attended,
            attended_low,
            log_total,
            normed_one,
            inverse_one,
            hidden_low,
            inner,
            active_low,
            normed_two,
            inverse_two,
        ) = kept[layer]
        gains_pair = norm_gains[layer]
        gain_two = jnp.sum(grad * normed_two, axis=0)
        shift_two = jnp.sum(grad, axis=0)
        second_grad = norm_back(grad, normed_two, inverse_two, gains_pair[1])
        down_grad_low = second_grad.astype(jnp.bfloat16)
        down_bias = jnp.sum(down_grad_low.astype(jnp.float32), axis=0)
        down_matrix_grad = jnp.einsum(
            "tf,td->fd", active_low, down_grad_low, preferred_element_type=jnp.float32
        )
        active_grad = jnp.einsum(
            "td,fd->tf", down_grad_low, down_weight[layer], preferred_element_type=jnp.float32
        )
        inner_grad_low = (active_grad * gelu_slope(inner)).astype(jnp.bfloat16)
        up_bias = jnp.sum(inner_grad_low.astype(jnp.float32), axis=0)
        up_matrix_grad = jnp.einsum(
            "td,tf->df", hidden_low, inner_grad_low, preferred_element_type=jnp.float32
        )
        hidden_grad = second_grad + jnp.einsum(
            "tf,df->td", inner_grad_low, up_weight[layer], preferred_element_type=jnp.float32
        )
        gain_one = jnp.sum(hidden_grad * normed_one, axis=0)
        shift_one = jnp.sum(hidden_grad, axis=0)
        first_grad = norm_back(hidden_grad, normed_one, inverse_one, gains_pair[0])
        branch_grad_low = first_grad.astype(jnp.bfloat16)
        out_bias = jnp.sum(branch_grad_low.astype(jnp.float32), axis=0)
        out_matrix_grad = jnp.einsum(
            "td,te->de", attended_low, branch_grad_low, preferred_element_type=jnp.float32
        )
        attended_grad_low = jnp.einsum(
            "te,de->td", branch_grad_low, out_weight[layer], preferred_element_type=jnp.float32
        ).astype(jnp.bfloat16)
        grad_heads = attended_grad_low.reshape(rows, HEADS, HEAD_DIM)
        delta = jnp.sum(
            (attended_grad_low.astype(jnp.float32) * attended).reshape(rows, HEADS, HEAD_DIM),
            axis=-1,
        ).T
        back = make_back(query_heads, grad_heads, log_total, delta, mask_for, scale)
        state = (
            jnp.zeros((rows, HEADS, HEAD_DIM), jnp.float32),
            jnp.zeros((length, 2 * model), jnp.float32),
        )
        query_grad, full_grad = back(
            state, lax.all_gather(gathered, "seq", axis=0, tiled=True), jnp.int32(0)
        )
        key_value_grad = lax.psum_scatter(
            full_grad.astype(jnp.bfloat16), "seq", scatter_dimension=0, tiled=True
        ).astype(jnp.float32)
        mixed_grad_low = jnp.concatenate(
            [query_grad.reshape(rows, model), key_value_grad], axis=1
        ).astype(jnp.bfloat16)
        query_bias = jnp.sum(mixed_grad_low[:, :model].astype(jnp.float32), axis=0)
        value_bias = jnp.sum(mixed_grad_low[:, 2 * model :].astype(jnp.float32), axis=0)
        in_matrix_grad = jnp.einsum(
            "td,tm->dm", stream_low, mixed_grad_low, preferred_element_type=jnp.float32
        )
        grad = first_grad + jnp.einsum(
            "tm,dm->td", mixed_grad_low, in_weight[layer], preferred_element_type=jnp.float32
        )
        collected[layer] = (
            in_matrix_grad,
            out_matrix_grad,
            up_matrix_grad,
            down_matrix_grad,
            jnp.stack([gain_one, gain_two]),
            jnp.stack([query_bias, value_bias, out_bias, up_bias, down_bias, shift_one, shift_two]),
        )
    in_stack = jnp.stack([collected[layer][0] for layer in range(LAYERS)])
    out_stack = jnp.stack([collected[layer][1] for layer in range(LAYERS)])
    up_stack = jnp.stack([collected[layer][2] for layer in range(LAYERS)])
    down_stack = jnp.stack([collected[layer][3] for layer in range(LAYERS)])
    gains_stack = jnp.stack([collected[layer][4] for layer in range(LAYERS)])
    biases_stack = jnp.stack([collected[layer][5] for layer in range(LAYERS)])
    in_total, out_total, up_total, down_total, gains_total, biases_total = lax.psum(
        (in_stack, out_stack, up_stack, down_stack, gains_stack, biases_stack), ("dp", "seq")
    )
    stream_rms = jnp.sqrt(square_total / (count_total * model))
    return (
        layer_output,
        grad[None],
        in_total,
        out_total,
        up_total,
        down_total,
        gains_total,
        biases_total,
        stream_rms,
    )


MESH = pl.DeviceIdType.MESH
LOW = jnp.bfloat16
F32 = jnp.float32
SMALL_ROWS = 32


def nn(left, right):
    return lax.dot_general(left, right, (((1,), (0,)), ((), ())), preferred_element_type=F32)


def nt(left, right):
    return lax.dot_general(left, right, (((1,), (1,)), ((), ())), preferred_element_type=F32)


def tn(left, right):
    return lax.dot_general(left, right, (((0,), (0,)), ((), ())), preferred_element_type=F32)


def column_sum(value):
    return jnp.sum(value.astype(F32), axis=0, keepdims=True)


def pad_head(rows, which):
    blank = jnp.zeros_like(rows)
    return jnp.concatenate([rows, blank] if which == 0 else [blank, rows], axis=0)


class Sems:
    def __init__(self, send, recv, near):
        self.send, self.recv, self.near = send, recv, near
        self.far_used = self.near_used = 0

    def far(self, src, dst, device):
        index = self.far_used
        self.far_used += 1
        return pltpu.make_async_remote_copy(
            src_ref=src,
            dst_ref=dst,
            send_sem=self.send.at[index],
            recv_sem=self.recv.at[index],
            device_id=device,
            device_id_type=MESH,
        )

    def local(self, src, dst):
        index = self.near_used
        self.near_used += 1
        return pltpu.make_async_copy(src, dst, self.near.at[index])


FAR_SEMS = 224
NEAR_SEMS = 64


def fused_kernel(
    levels,
    tok_ref,
    starts_ref,
    flags_ref,
    valid_ref,
    win_hbm,
    wout_hbm,
    wup_hbm,
    wdn_hbm,
    gains_ref,
    biases_ref,
    og_hbm,
    lo_hbm,
    ig_hbm,
    gin_hbm,
    gout_hbm,
    gup_hbm,
    gdn_hbm,
    small_ref,
    kept_hbm,
    win,
    wout,
    wup,
    wdn,
    low,
    outer,
    keys,
    values,
    turned,
    query_t,
    weights_t,
    attended_t,
    attended_low,
    inverse_total,
    normed_one,
    normed_two,
    inverse_norm,
    hidden_low,
    active_low,
    slope_low,
    scores,
    mask,
    flow,
    query_grad_t,
    give_t,
    take_t,
    meta,
    meta_sent,
    small,
    small_in,
    small_z,
    grads,
    whole,
    take_core,
    take_x,
    take_y,
    take_ay,
    take_bx,
    take_z,
    send_sems,
    recv_sems,
    near_sems,
):
    rows, model = low.shape[1], low.shape[2]
    length = 2 * rows
    pairs = HEADS // 2
    d = lax.axis_index("dp")
    x = lax.axis_index("seq")
    core = lax.rem(d, 2)
    y = lax.rem(lax.div(d, 2), 2)
    z = lax.div(d, 4)
    to_core = (d + 1 - 2 * core, x)
    to_x = (d, 1 - x)
    to_y = (d + 2 - 4 * y, x)
    to_diag = (d + 1 - 2 * core, 1 - x)

    def at_z(level):
        return (d + (level - z) * 4, x)

    z_next = [lax.rem(z + step, levels) for step in range(1, levels)]
    sems = Sems(send_sems, recv_sems, near_sems)
    barrier = pltpu.get_barrier_semaphore()
    peers = [to_core, to_x, to_y, to_diag] + [at_z(level) for level in z_next]
    for peer in peers:
        pl.semaphore_signal(barrier, inc=1, device_id=peer, device_id_type=MESH)

    def load(pairs_of):
        copies = [sems.local(src, dst) for src, dst in pairs_of]
        for copy in copies:
            copy.start()
        return copies

    moved = core != x
    away_low = sems.far(tok_ref.at[0], low.at[0], to_diag)
    away_outer = sems.far(og_hbm.at[0], outer, to_diag)
    away_meta = sems.far(meta_sent, meta, to_diag)
    stay_low = sems.local(tok_ref.at[0], low.at[0])
    stay_outer = sems.local(og_hbm.at[0], outer)

    position = lax.broadcasted_iota(jnp.int32, (1, length), 1)
    segment = jnp.zeros((1, length), jnp.int32) - 1
    for cell in range(starts_ref.shape[1]):
        segment = segment + (position >= starts_ref[0:1, cell : cell + 1]).astype(jnp.int32)
    good = valid_ref[...] * (1 - flags_ref[...]) > 0
    meta_sent[...] = jnp.zeros_like(meta_sent)
    meta_sent[0:1, :] = jnp.where(good, segment, -1).astype(F32)
    meta_sent[1:2, :] = segment.astype(F32)
    meta_sent[2:3, :] = valid_ref[...].astype(F32)

    pl.semaphore_wait(barrier, len(peers))

    @pl.when(moved)
    def _():
        away_meta.start()
        away_low.start()

    @pl.when(jnp.logical_not(moved))
    def _():
        stay_low.start()
        meta[...] = meta_sent[...]

    weight_loads = []
    for layer in range(LAYERS):
        weight_loads.append(
            [
                load([(win_hbm.at[layer], win.at[layer])])[0],
                load([(wout_hbm.at[layer], wout.at[layer])])[0],
                load([(wup_hbm.at[layer], wup.at[layer])])[0],
                load([(wdn_hbm.at[layer], wdn.at[layer])])[0],
            ]
        )

    small[...] = jnp.zeros_like(small)

    @pl.when(moved)
    def _():
        away_meta.wait()

    near = meta[:, pl.ds(pl.multiple_of(core * rows, 128), rows)]
    far = meta[:, pl.ds(pl.multiple_of((1 - core) * rows, 128), rows)]
    near_t, far_t = near.T, far.T
    same = lax.broadcasted_iota(jnp.int32, (rows, rows), 0) == lax.broadcasted_iota(
        jnp.int32, (rows, rows), 1
    )
    mask[0:rows, :] = jnp.where((near_t[:, 0:1] == near[1:2, :]) | same, 0.0, NEG)
    mask[rows:length, :] = jnp.where(far_t[:, 0:1] == near[1:2, :], 0.0, NEG)
    valid_column = near_t[:, 2:3]
    small[0, 24:25, :] = near[2:3, :]

    @pl.when(moved)
    def _():
        away_low.wait()
        away_outer.start()

    @pl.when(jnp.logical_not(moved))
    def _():
        stay_low.wait()
        stay_outer.start()

    def note_square(layer, which, value):
        row = 18 + 3 * layer + which
        small[0, row : row + 1, :] = column_sum(value * value * valid_column)

    spills = []
    flow[...] = low[0].astype(F32)
    for layer in range(LAYERS):
        bias = [biases_ref[layer, k : k + 1, :] for k in range(7)]
        gain = [gains_ref[layer, k : k + 1, :] for k in range(2)]
        load_in, load_out, load_up, load_down = weight_loads[layer]
        load_in.wait()
        stream_low = low[layer]
        note_square(layer, 0, flow[...])
        keys[layer, 0:rows, :] = nn(stream_low, win[layer, :, model : 2 * model]).astype(LOW)
        send_keys = sems.far(
            keys.at[layer, pl.ds(0, rows)], keys.at[layer, pl.ds(rows, rows)], to_core
        )
        send_keys.start()
        values[layer, 0:rows, :] = (
            nn(stream_low, win[layer, :, 2 * model : 3 * model]) + bias[1]
        ).astype(LOW)
        send_values = sems.far(
            values.at[layer, pl.ds(0, rows)], values.at[layer, pl.ds(rows, rows)], to_core
        )
        send_values.start()
        query = (nn(stream_low, win[layer, :, 0:model]) + bias[0]).astype(LOW)
        query_t[layer] = (query.astype(F32) * (1.0 / math.sqrt(HEAD_DIM))).T.astype(LOW)
        turned[:, 0:rows] = values[layer, 0:rows, :].T
        send_keys.wait()
        send_values.wait()
        turned[:, rows:length] = values[layer, rows:length, :].T

        def score(head, layer=layer):
            pair = head // 2
            scores[head % 2] = (
                nn(
                    keys[layer, :, 128 * pair : 128 * pair + 128],
                    pad_head(query_t[layer, 64 * head : 64 * head + 64, :], head % 2),
                )
                + mask[...]
            )

        score(0)
        for head in range(HEADS):
            if head + 1 < HEADS:
                score(head + 1)
            if layer > 0:
                spills[layer - 1][head].wait()
            block = scores[head % 2]
            best = jnp.max(block, axis=0, keepdims=True)
            weight = jnp.exp(block - best)
            inverse = 1.0 / jnp.sum(weight, axis=0, keepdims=True)
            weight_low = weight.astype(LOW)
            weights_t[head] = weight_low
            span = slice(64 * head, 64 * head + 64)
            inverse_total[layer, head : head + 1, :] = inverse
            attended_t[layer, span, :] = nn(turned[span, :], weight_low) * inverse
            if layer + 1 < LAYERS:
                if head == 0:
                    spills.append([])
                copy = sems.local(weights_t.at[head], kept_hbm.at[layer, head])
                copy.start()
                spills[layer].append(copy)
        attended_low[layer] = attended_t[layer].T.astype(LOW)
        load_out.wait()
        branch = nn(attended_low[layer], wout[layer]) + bias[2]
        note_square(layer, 1, branch)
        total = flow[...] + branch
        centred = total - jnp.mean(total, axis=-1, keepdims=True)
        inverse = lax.rsqrt(jnp.mean(centred * centred, axis=-1, keepdims=True) + EPS)
        normed = centred * inverse
        normed_one[layer] = normed.astype(LOW)
        inverse_norm[:, 2 * layer : 2 * layer + 1] = inverse
        hidden = normed * gain[0] + bias[5]
        flow[...] = hidden
        hidden_low[layer] = hidden.astype(LOW)
        load_up.wait()
        inner = nn(hidden_low[layer], wup[layer]) + bias[3]
        share = 0.5 * (1.0 + lax.erf(inner * 0.7071067811865476))
        active_low[layer] = (inner * share).astype(LOW)
        slope_low[layer] = (
            share + inner * jnp.exp(-0.5 * inner * inner) * 0.3989422804014327
        ).astype(LOW)
        load_down.wait()
        ff_out = nn(active_low[layer], wdn[layer]) + bias[4]
        note_square(layer, 2, ff_out)
        total = flow[...] + ff_out
        centred = total - jnp.mean(total, axis=-1, keepdims=True)
        inverse = lax.rsqrt(jnp.mean(centred * centred, axis=-1, keepdims=True) + EPS)
        normed = centred * inverse
        normed_two[layer] = normed.astype(LOW)
        inverse_norm[:, 2 * layer + 1 : 2 * layer + 2] = inverse
        result = normed * gain[1] + bias[6]
        if layer + 1 < LAYERS:
            flow[...] = result
            low[layer + 1] = result.astype(LOW)
        else:
            grads[6 * LAYERS - 1] = result.astype(LOW)

    staged = grads.at[6 * LAYERS - 1]
    away_result = sems.far(staged, lo_hbm.at[0], to_diag)
    stay_result = sems.local(staged, lo_hbm.at[0])
    away_grad = sems.far(outer, ig_hbm.at[0], to_diag)
    stay_grad = sems.local(outer, ig_hbm.at[0])

    @pl.when(moved)
    def _():
        away_outer.wait()
        away_result.start()

    @pl.when(jnp.logical_not(moved))
    def _():
        stay_outer.wait()
        stay_result.start()

    half, quarter, eighth = model // 2, model // 4, model // 8
    piece = eighth // levels
    left, right = pl.ds(0, half), pl.ds(half, half)
    core_row = pl.multiple_of(core * half, half)
    core_other = pl.multiple_of((1 - core) * half, half)
    a_row = pl.multiple_of(core_row + x * quarter, quarter)
    a_other = pl.multiple_of(core_row + (1 - x) * quarter, quarter)
    b_row = pl.multiple_of(core_row + y * quarter, quarter)
    b_other = pl.multiple_of(core_row + (1 - y) * quarter, quarter)
    a_deep = pl.multiple_of(a_row + y * eighth, eighth)
    a_deep_other = pl.multiple_of(a_row + (1 - y) * eighth, eighth)
    b_deep = pl.multiple_of(b_row + x * eighth, eighth)
    b_deep_other = pl.multiple_of(b_row + (1 - x) * eighth, eighth)
    a_own = pl.multiple_of(a_deep + z * piece, piece)
    b_own = pl.multiple_of(b_deep + z * piece, piece)

    def add_into(at, value):
        grads[at] = (grads[at].astype(F32) + value.astype(F32)).astype(LOW)

    def reduce_chunk(begin, count, homes):
        some = pl.ds(begin, count)

        def launch(copies):
            for copy in copies:
                copy.start()
            return copies

        def finish(copies):
            for copy in copies:
                copy.wait()

        def same_place(row, width, columns, peer):
            block = whole.at[some, pl.ds(row, width), columns]
            return sems.far(block, block, peer)

        everything = pl.ds(0, model)
        landed = pl.ds(begin % 6, count)
        flight = launch(
            [sems.far(grads.at[some, pl.ds(core_other, half)], take_core.at[landed], to_core)]
        )
        yield
        finish(flight)
        add_into((some, pl.ds(core_row, half), everything), take_core[landed])
        flight = launch(
            [
                sems.far(grads.at[some, pl.ds(a_other, quarter), left], take_x.at[some], to_x),
                sems.far(grads.at[some, pl.ds(b_other, quarter), right], take_y.at[some], to_y),
            ]
        )
        yield
        finish(flight)
        add_into((some, pl.ds(a_row, quarter), left), take_x[some])
        add_into((some, pl.ds(b_row, quarter), right), take_y[some])
        flight = launch(
            [
                sems.far(
                    grads.at[some, pl.ds(a_deep_other, eighth), left], take_ay.at[some], to_y
                ),
                sems.far(
                    grads.at[some, pl.ds(b_deep_other, eighth), right], take_bx.at[some], to_x
                ),
            ]
        )
        yield
        finish(flight)
        add_into((some, pl.ds(a_deep, eighth), left), take_ay[some])
        add_into((some, pl.ds(b_deep, eighth), right), take_bx[some])
        flight = []
        for step, level in enumerate(z_next):
            for side, (deep, columns) in enumerate(((a_deep, left), (b_deep, right))):
                row = pl.multiple_of(deep + level * piece, piece)
                flight.append(
                    sems.far(
                        grads.at[some, pl.ds(row, piece), columns],
                        take_z.at[step, side, some],
                        at_z(level),
                    )
                )
        launch(flight)
        yield
        finish(flight)
        for side, (own, columns) in enumerate(((a_own, left), (b_own, right))):
            at = (some, pl.ds(own, piece), columns)
            total = grads[at].astype(F32)
            for step in range(levels - 1):
                total = total + take_z[step, side, some].astype(F32)
            whole[at] = total.astype(LOW)
        flight = []
        for level in z_next:
            for own, columns in ((a_own, left), (b_own, right)):
                flight.append(same_place(own, piece, columns, at_z(level)))
        launch(flight)
        yield
        finish(flight)
        flight = launch(
            [same_place(a_deep, eighth, left, to_y), same_place(b_deep, eighth, right, to_x)]
        )
        yield
        finish(flight)
        flight = launch(
            [same_place(a_row, quarter, left, to_x), same_place(b_row, quarter, right, to_y)]
        )
        yield
        finish(flight)
        flight = launch([same_place(core_row, half, everything, to_core)])
        yield
        finish(flight)
        flight = launch([sems.local(whole.at[begin + k], homes[k]) for k in range(count)])
        yield
        finish(flight)

    def reduce_small():
        for step, peer in enumerate((to_core, to_x, to_y)):
            copy = sems.far(small.at[step], small_in.at[step], peer)
            copy.start()
            yield
            copy.wait()
            small[step + 1] = small[step] + small_in[step]
        copies = [sems.far(small.at[3], small_z.at[z], at_z(level)) for level in z_next]
        for copy in copies:
            copy.start()
        small_z[z] = small[3]
        yield
        for copy in copies:
            copy.wait()
        total = small_z[0]
        for level in range(1, levels):
            total = total + small_z[level]
        small_ref[...] = total

    active = []

    def pump(times=1):
        for _ in range(times):
            for chunk in list(active):
                if next(chunk, 0) == 0:
                    active.remove(chunk)

    def begin(chunk):
        next(chunk)
        active.append(chunk)

    def note(row, value):
        small[0, row : row + 1, :] = value

    reloads = []
    flow[...] = outer[...].astype(F32)
    for layer in reversed(range(LAYERS)):
        gain = [gains_ref[layer, k : k + 1, :] for k in range(2)]
        base = 6 * (LAYERS - 1 - layer)
        bias_row = 4 + 7 * layer
        grad = flow[...]
        normed = normed_two[layer].astype(F32)
        note(2 * layer + 1, column_sum(grad * normed))
        note(bias_row + 6, column_sum(grad))
        scaled = grad * gain[1]
        second = inverse_norm[:, 2 * layer + 1 : 2 * layer + 2] * (
            scaled
            - jnp.mean(scaled, axis=-1, keepdims=True)
            - normed * jnp.mean(scaled * normed, axis=-1, keepdims=True)
        )
        scores[0, 0:rows, :] = second
        down_low = second.astype(LOW)
        note(bias_row + 4, column_sum(down_low))
        grads[base] = tn(active_low[layer], down_low).astype(LOW)
        inner_low = (nt(down_low, wdn[layer]) * slope_low[layer].astype(F32)).astype(LOW)
        note(bias_row + 3, column_sum(inner_low))
        grads[base + 1] = tn(hidden_low[layer], inner_low).astype(LOW)
        begin(reduce_chunk(base, 2, [gdn_hbm.at[layer], gup_hbm.at[layer]]))
        grad = scores[0, 0:rows, :] + nt(inner_low, wup[layer])
        normed = normed_one[layer].astype(F32)
        note(2 * layer, column_sum(grad * normed))
        note(bias_row + 5, column_sum(grad))
        scaled = grad * gain[0]
        flow[...] = inverse_norm[:, 2 * layer : 2 * layer + 1] * (
            scaled
            - jnp.mean(scaled, axis=-1, keepdims=True)
            - normed * jnp.mean(scaled * normed, axis=-1, keepdims=True)
        )
        branch_low = flow[...].astype(LOW)
        note(bias_row + 2, column_sum(branch_low))
        pump()
        grads[base + 2] = tn(attended_low[layer], branch_low).astype(LOW)
        begin(reduce_chunk(base + 2, 1, [gout_hbm.at[layer]]))
        attended_grad_t = nt(branch_low, wout[layer]).astype(LOW).T
        turned[:, 0:rows] = keys[layer, 0:rows, :].T
        turned[:, rows:length] = keys[layer, rows:length, :].T
        gives = []
        for head in range(HEADS):
            pair = head // 2
            span = slice(64 * head, 64 * head + 64)
            lanes = slice(128 * pair, 128 * pair + 128)
            grad_low = (
                attended_grad_t[span, :].astype(F32) * inverse_total[layer, head : head + 1, :]
            ).astype(LOW)
            delta = column_sum(grad_low.astype(F32) * attended_t[layer, span, :])
            if layer + 1 < LAYERS:
                reloads[head].wait()
            weight_low = weights_t[head]
            prob_grad = nn(values[layer, :, lanes], pad_head(grad_low, head % 2))
            score_grad = (weight_low.astype(F32) * (prob_grad - delta)).astype(LOW)
            query_grad_t[span, :] = (
                nn(turned[span, :], score_grad) * (1.0 / math.sqrt(HEAD_DIM))
            ).astype(LOW)
            key_grad = nt(query_t[layer, span, :], score_grad)
            value_grad = nt(grad_low, weight_low)
            inside = slice(64 * (head % 2), 64 * (head % 2) + 64)
            mask[span, :] = key_grad[:, 0:rows]
            mask[64 * head + model : 64 * head + model + 64, :] = value_grad[:, 0:rows]
            give_t[pair, 0, inside, :] = key_grad[:, rows:length].astype(LOW)
            give_t[pair, 1, inside, :] = value_grad[:, rows:length].astype(LOW)
            if layer > 0:
                copy = sems.local(kept_hbm.at[layer - 1, head], weights_t.at[head])
                copy.start()
                reloads.append(copy)
            if head % 2 == 1:
                copy = sems.far(give_t.at[pair], take_t.at[layer, pair], to_core)
                copy.start()
                gives.append(copy)
            pump()
        stream_low = low[layer]
        grad_q = query_grad_t[...].T
        grads[base + 3] = tn(stream_low, grad_q).astype(LOW)
        homes = [gin_hbm.at[layer, :, pl.ds(model * k, model)] for k in range(3)]
        if layer == 0:
            begin(reduce_chunk(base + 3, 1, homes[:1]))
        note(bias_row, column_sum(grad_q))
        for copy in gives:
            copy.wait()
        pump()
        own_v = jnp.concatenate([take_t[layer, pair, 1] for pair in range(pairs)], axis=0)
        grad_v = (mask[model : 2 * model, :] + own_v.astype(F32)).astype(LOW).T
        grads[base + 5] = tn(stream_low, grad_v).astype(LOW)
        if layer == 0:
            begin(reduce_chunk(base + 5, 1, homes[2:]))
        note(bias_row + 1, column_sum(grad_v))
        own_k = jnp.concatenate([take_t[layer, pair, 0] for pair in range(pairs)], axis=0)
        grad_k = (mask[0:model, :] + own_k.astype(F32)).astype(LOW).T
        grads[base + 4] = tn(stream_low, grad_k).astype(LOW)
        if layer == 0:
            begin(reduce_chunk(base + 4, 1, homes[1:2]))
            begin(reduce_small())
        else:
            begin(reduce_chunk(base + 3, 3, homes))
        pump()
        grad = (
            flow[...]
            + nt(grad_q, win[layer, :, 0:model])
            + nt(grad_k, win[layer, :, model : 2 * model])
            + nt(grad_v, win[layer, :, 2 * model : 3 * model])
        )
        if layer > 0:
            flow[...] = grad

            @pl.when(moved)
            def _():
                away_result.wait()

            @pl.when(jnp.logical_not(moved))
            def _():
                stay_result.wait()

        else:
            outer[...] = grad.astype(LOW)
        pump()

    @pl.when(moved)
    def _():
        away_grad.start()

    @pl.when(jnp.logical_not(moved))
    def _():
        stay_grad.start()

    while active:
        pump()

    @pl.when(moved)
    def _():
        away_grad.wait()

    @pl.when(jnp.logical_not(moved))
    def _():
        stay_grad.wait()

    assert sems.far_used <= FAR_SEMS and sems.near_used <= NEAR_SEMS


def local_pair(
    tokens,
    cell_starts,
    generate_flags,
    valid_mask,
    in_weight,
    out_weight,
    up_weight,
    down_weight,
    norm_gains,
    biases,
    out_grad,
):
    rows, model = tokens.shape[1:]
    length = 2 * rows
    levels = lax.axis_size("dp") // 4
    half, quarter, eighth = model // 2, model // 4, model // 8
    square = (model, model)
    shape = jax.ShapeDtypeStruct
    vmem, anywhere = pl.BlockSpec(memory_space=pltpu.VMEM), pl.BlockSpec(memory_space=pl.ANY)
    matrices = 6 * LAYERS
    by_layer = (LAYERS, rows, model)
    scratch = [
        pltpu.VMEM(in_weight.shape, LOW),
        pltpu.VMEM(out_weight.shape, LOW),
        pltpu.VMEM(up_weight.shape, LOW),
        pltpu.VMEM(down_weight.shape, LOW),
        pltpu.VMEM(by_layer, LOW),
        pltpu.VMEM((rows, model), LOW),
        pltpu.VMEM((LAYERS, length, model), LOW),
        pltpu.VMEM((LAYERS, length, model), LOW),
        pltpu.VMEM((model, length), LOW),
        pltpu.VMEM((LAYERS, model, rows), LOW),
        pltpu.VMEM((HEADS, length, rows), LOW),
        pltpu.VMEM((LAYERS, model, rows), F32),
        pltpu.VMEM(by_layer, LOW),
        pltpu.VMEM((LAYERS, HEADS, rows), F32),
        pltpu.VMEM(by_layer, LOW),
        pltpu.VMEM(by_layer, LOW),
        pltpu.VMEM((rows, 2 * LAYERS), F32),
        pltpu.VMEM(by_layer, LOW),
        pltpu.VMEM(by_layer, LOW),
        pltpu.VMEM(by_layer, LOW),
        pltpu.VMEM((2, length, rows), F32),
        pltpu.VMEM((length, rows), F32),
        pltpu.VMEM((rows, model), F32),
        pltpu.VMEM((model, rows), LOW),
        pltpu.VMEM((HEADS // 2, 2, 128, rows), LOW),
        pltpu.VMEM((LAYERS, HEADS // 2, 2, 128, rows), LOW),
        pltpu.VMEM((8, length), F32),
        pltpu.VMEM((8, length), F32),
        pltpu.VMEM((4, SMALL_ROWS, model), F32),
        pltpu.VMEM((3, SMALL_ROWS, model), F32),
        pltpu.VMEM((levels, SMALL_ROWS, model), F32),
        pltpu.VMEM((matrices,) + square, LOW),
        pltpu.VMEM((matrices,) + square, LOW),
        pltpu.VMEM((matrices // LAYERS, half, model), LOW),
        pltpu.VMEM((matrices, quarter, half), LOW),
        pltpu.VMEM((matrices, quarter, half), LOW),
        pltpu.VMEM((matrices, eighth, half), LOW),
        pltpu.VMEM((matrices, eighth, half), LOW),
        pltpu.VMEM((max(levels - 1, 1), 2, matrices, eighth // levels, half), LOW),
        pltpu.SemaphoreType.DMA((FAR_SEMS,)),
        pltpu.SemaphoreType.DMA((FAR_SEMS,)),
        pltpu.SemaphoreType.DMA((NEAR_SEMS,)),
    ]
    lo, ig, gin, gout, gup, gdn, small, _ = pl.pallas_call(
        functools.partial(fused_kernel, levels),
        out_shape=[
            shape(tokens.shape, LOW),
            shape(tokens.shape, LOW),
            shape(in_weight.shape, LOW),
            shape(out_weight.shape, LOW),
            shape(up_weight.shape, LOW),
            shape(down_weight.shape, LOW),
            shape((SMALL_ROWS, model), F32),
            shape((LAYERS - 1, HEADS, length, rows), LOW),
        ],
        in_specs=[anywhere, vmem, vmem, vmem] + [anywhere] * 4 + [vmem, vmem, anywhere],
        out_specs=[anywhere] * 6 + [vmem, anywhere],
        scratch_shapes=scratch,
        compiler_params=pltpu.CompilerParams(
            collective_id=0, has_side_effects=True, vmem_limit_bytes=VMEM_BYTES
        ),
    )(
        tokens,
        cell_starts,
        generate_flags,
        valid_mask,
        in_weight,
        out_weight,
        up_weight,
        down_weight,
        norm_gains,
        biases,
        out_grad,
    )
    squares = jnp.sum(small[18 : 18 + 3 * LAYERS], axis=1).reshape(LAYERS, 3)
    count = jnp.sum(small[24])
    return (
        lo,
        ig.astype(F32),
        gin.astype(F32),
        gout.astype(F32),
        gup.astype(F32),
        gdn.astype(F32),
        small[0 : 2 * LAYERS].reshape(norm_gains.shape),
        small[4 : 4 + 7 * LAYERS].reshape(biases.shape),
        jnp.sqrt(squares / (count * model)),
    )


VMEM_BYTES = 63 * 1024 * 1024


def solution(mesh):
    placed = (
        P("dp", "seq", None),
        P("dp", None),
        P("dp", None),
        P("dp", None),
        P(),
        P(),
        P(),
        P(),
        P(),
        P(),
        P("dp", "seq", None),
    )
    paired = mesh.shape["seq"] == 2 and mesh.shape["dp"] % 4 == 0
    return jax.shard_map(
        local_pair if paired else local,
        mesh=mesh,
        in_specs=placed,
        out_specs=(P("dp", "seq", None), P("dp", "seq", None), P(), P(), P(), P(), P(), P(), P()),
        check_vma=False,
    )
```

```python
import functools
import math

import jax
import jax.numpy as jnp
from jax import lax
from jax.experimental import pallas as pl
from jax.experimental.pallas import tpu as pltpu
from jax.sharding import PartitionSpec as P

HEADS = 8
HEAD_DIM = 64
LAYERS = 2


EPS = 1e-05
NEG = -1e30


def block_width(count):
    for option in range(1024, 255, -1):
        if count % option == 0:
            return option
    return count


def segment_ids(starts_row, positions):
    return jnp.sum((positions[:, None] >= starts_row[None, :]).astype(jnp.int32), axis=1) - 1


def norm_rows(total, gain, shift):
    mean = jnp.mean(total, axis=-1, keepdims=True)
    centred = total - mean
    spread = jnp.mean(centred * centred, axis=-1, keepdims=True)
    inverse = lax.rsqrt(spread + EPS)
    normed = centred * inverse
    return (normed * gain + shift, normed, inverse)


def norm_back(grad, normed, inverse, gain):
    scaled = grad * gain
    return inverse * (
        scaled
        - jnp.mean(scaled, axis=-1, keepdims=True)
        - normed * jnp.mean(scaled * normed, axis=-1, keepdims=True)
    )


def gelu_slope(inner):
    return (
        0.5 * (1.0 + jax.scipy.special.erf(inner * 0.7071067811865476))
        + inner * jnp.exp(-0.5 * inner * inner) * 0.3989422804014327
    )


def make_mask(query_pos, query_seg, starts_row, key_ok_row):

    def mask_for(begin, width):
        key_pos = begin + jnp.arange(width, dtype=jnp.int32)
        key_seg = segment_ids(starts_row, key_pos)
        key_good = lax.dynamic_slice_in_dim(key_ok_row, begin, width, 0) > 0
        return (query_seg[:, None] == key_seg[None, :]) & (
            key_good[None, :] | (query_pos[:, None] == key_pos[None, :])
        )

    return mask_for


def make_attend(query_heads, mask_for, scale):

    def attend(carry, piece, start):
        count = piece.shape[0]
        width = block_width(count)
        model = piece.shape[1] // 2

        def attend_one_block(step, state):
            best, total, summed = state
            begin = step * width
            block = lax.dynamic_slice_in_dim(piece, begin, width, 0)
            key_heads = block[:, :model].reshape(width, HEADS, HEAD_DIM)
            value_heads = block[:, model:].reshape(width, HEADS, HEAD_DIM)
            allowed = mask_for(start + begin, width)[None]
            scores = (
                jnp.einsum(
                    "qhd,khd->hqk", query_heads, key_heads, preferred_element_type=jnp.float32
                )
                * scale
            )
            scores = jnp.where(allowed, scores, NEG)
            new_best = jnp.maximum(best, jnp.max(scores, axis=-1))
            factor = jnp.exp(best - new_best)
            weights = jnp.where(allowed, jnp.exp(scores - new_best[:, :, None]), 0.0)
            total = total * factor + jnp.sum(weights, axis=-1)
            update = jnp.einsum(
                "hqk,khd->qhd",
                weights.astype(jnp.bfloat16),
                value_heads,
                preferred_element_type=jnp.float32,
            )
            summed = summed * factor.T[:, :, None] + update
            return (new_best, total, summed)

        return lax.fori_loop(0, count // width, attend_one_block, carry)

    return attend


def make_back(query_heads, grad_heads, log_total, delta, mask_for, scale):

    def back(carry, piece, start):
        count = piece.shape[0]
        width = block_width(count)
        model = piece.shape[1] // 2

        def back_one_block(step, state):
            query_grad, full_grad = state
            begin = step * width
            block = lax.dynamic_slice_in_dim(piece, begin, width, 0)
            key_heads = block[:, :model].reshape(width, HEADS, HEAD_DIM)
            value_heads = block[:, model:].reshape(width, HEADS, HEAD_DIM)
            allowed = mask_for(start + begin, width)[None]
            scores = (
                jnp.einsum(
                    "qhd,khd->hqk", query_heads, key_heads, preferred_element_type=jnp.float32
                )
                * scale
            )
            probs = jnp.where(allowed, jnp.exp(scores - log_total[:, :, None]), 0.0)
            prob_grad = jnp.einsum(
                "qhd,khd->hqk", grad_heads, value_heads, preferred_element_type=jnp.float32
            )
            score_grad = (probs * (prob_grad - delta[:, :, None])).astype(jnp.bfloat16)
            query_grad = (
                query_grad
                + jnp.einsum(
                    "hqk,khd->qhd", score_grad, key_heads, preferred_element_type=jnp.float32
                )
                * scale
            )
            key_grad = (
                jnp.einsum(
                    "hqk,qhd->khd", score_grad, query_heads, preferred_element_type=jnp.float32
                )
                * scale
            )
            value_grad = jnp.einsum(
                "hqk,qhd->khd",
                probs.astype(jnp.bfloat16),
                grad_heads,
                preferred_element_type=jnp.float32,
            )
            update = jnp.concatenate(
                [key_grad.reshape(width, model), value_grad.reshape(width, model)], axis=1
            )
            place = start + begin
            current = lax.dynamic_slice_in_dim(full_grad, place, width, 0)
            full_grad = lax.dynamic_update_slice_in_dim(full_grad, current + update, place, 0)
            return (query_grad, full_grad)

        return lax.fori_loop(0, count // width, back_one_block, carry)

    return back


def local(
    tokens,
    cell_starts,
    generate_flags,
    valid_mask,
    in_weight,
    out_weight,
    up_weight,
    down_weight,
    norm_gains,
    biases,
    out_grad,
):
    rows = tokens.shape[1]
    model = tokens.shape[2]
    scale = 1.0 / math.sqrt(HEAD_DIM)
    first = lax.axis_index("seq") * rows
    query_pos = first + jnp.arange(rows, dtype=jnp.int32)
    starts_row = cell_starts[0]
    key_ok_row = valid_mask[0] * (1 - generate_flags[0])
    mask_for = make_mask(query_pos, segment_ids(starts_row, query_pos), starts_row, key_ok_row)
    valid_here = lax.dynamic_slice_in_dim(valid_mask[0], first, rows, 0).astype(jnp.float32)
    stream = tokens[0].astype(jnp.float32)
    stream_low = tokens[0]
    kept = []
    squares = []
    for layer in range(LAYERS):
        bias_rows = biases[layer]
        gains_pair = norm_gains[layer]
        mixed = jnp.dot(
            stream_low, in_weight[layer], preferred_element_type=jnp.float32
        ) + jnp.concatenate([bias_rows[0], jnp.zeros((model,), jnp.float32), bias_rows[1]])
        mixed_low = mixed.astype(jnp.bfloat16)
        query_heads = mixed_low[:, :model].reshape(rows, HEADS, HEAD_DIM)
        key_value = mixed_low[:, model:]
        attend = make_attend(query_heads, mask_for, scale)
        state = (
            jnp.full((HEADS, rows), NEG, jnp.float32),
            jnp.zeros((HEADS, rows), jnp.float32),
            jnp.zeros((rows, HEADS, HEAD_DIM), jnp.float32),
        )
        gathered = key_value
        best, total, summed = attend(
            state, lax.all_gather(key_value, "seq", axis=0, tiled=True), jnp.int32(0)
        )
        attended = (summed / total.T[:, :, None]).reshape(rows, model)
        log_total = best + jnp.log(total)
        attended_low = attended.astype(jnp.bfloat16)
        branch = (
            jnp.dot(attended_low, out_weight[layer], preferred_element_type=jnp.float32)
            + bias_rows[2]
        )
        hidden, normed_one, inverse_one = norm_rows(stream + branch, gains_pair[0], bias_rows[5])
        hidden_low = hidden.astype(jnp.bfloat16)
        inner = (
            jnp.dot(hidden_low, up_weight[layer], preferred_element_type=jnp.float32) + bias_rows[3]
        )
        active_low = jax.nn.gelu(inner, approximate=False).astype(jnp.bfloat16)
        ff_out = (
            jnp.dot(active_low, down_weight[layer], preferred_element_type=jnp.float32)
            + bias_rows[4]
        )
        result, normed_two, inverse_two = norm_rows(hidden + ff_out, gains_pair[1], bias_rows[6])
        squares.append(
            jnp.stack(
                [
                    jnp.sum(valid_here * jnp.sum(part * part, axis=-1))
                    for part in (stream, branch, ff_out)
                ]
            )
        )
        kept.append(
            (
                stream_low,
                query_heads,
                gathered,
                attended,
                attended_low,
                log_total,
                normed_one,
                inverse_one,
                hidden_low,
                inner,
                active_low,
                normed_two,
                inverse_two,
            )
        )
        stream = result
        stream_low = result.astype(jnp.bfloat16)
    layer_output = stream.astype(jnp.bfloat16)[None]
    square_local = jnp.stack(squares)
    count_local = jnp.sum(valid_here)
    square_total, count_total = lax.psum((square_local, count_local), ("dp", "seq"))
    grad = out_grad[0].astype(jnp.float32)
    length = rows * lax.axis_size("seq")
    collected = [None] * LAYERS
    for layer in reversed(range(LAYERS)):
        (
            stream_low,
            query_heads,
            gathered,
            attended,
            attended_low,
            log_total,
            normed_one,
            inverse_one,
            hidden_low,
            inner,
            active_low,
            normed_two,
            inverse_two,
        ) = kept[layer]
        gains_pair = norm_gains[layer]
        gain_two = jnp.sum(grad * normed_two, axis=0)
        shift_two = jnp.sum(grad, axis=0)
        second_grad = norm_back(grad, normed_two, inverse_two, gains_pair[1])
        down_grad_low = second_grad.astype(jnp.bfloat16)
        down_bias = jnp.sum(down_grad_low.astype(jnp.float32), axis=0)
        down_matrix_grad = jnp.einsum(
            "tf,td->fd", active_low, down_grad_low, preferred_element_type=jnp.float32
        )
        active_grad = jnp.einsum(
            "td,fd->tf", down_grad_low, down_weight[layer], preferred_element_type=jnp.float32
        )
        inner_grad_low = (active_grad * gelu_slope(inner)).astype(jnp.bfloat16)
        up_bias = jnp.sum(inner_grad_low.astype(jnp.float32), axis=0)
        up_matrix_grad = jnp.einsum(
            "td,tf->df", hidden_low, inner_grad_low, preferred_element_type=jnp.float32
        )
        hidden_grad = second_grad + jnp.einsum(
            "tf,df->td", inner_grad_low, up_weight[layer], preferred_element_type=jnp.float32
        )
        gain_one = jnp.sum(hidden_grad * normed_one, axis=0)
        shift_one = jnp.sum(hidden_grad, axis=0)
        first_grad = norm_back(hidden_grad, normed_one, inverse_one, gains_pair[0])
        branch_grad_low = first_grad.astype(jnp.bfloat16)
        out_bias = jnp.sum(branch_grad_low.astype(jnp.float32), axis=0)
        out_matrix_grad = jnp.einsum(
            "td,te->de", attended_low, branch_grad_low, preferred_element_type=jnp.float32
        )
        attended_grad_low = jnp.einsum(
            "te,de->td", branch_grad_low, out_weight[layer], preferred_element_type=jnp.float32
        ).astype(jnp.bfloat16)
        grad_heads = attended_grad_low.reshape(rows, HEADS, HEAD_DIM)
        delta = jnp.sum(
            (attended_grad_low.astype(jnp.float32) * attended).reshape(rows, HEADS, HEAD_DIM),
            axis=-1,
        ).T
        back = make_back(query_heads, grad_heads, log_total, delta, mask_for, scale)
        state = (
            jnp.zeros((rows, HEADS, HEAD_DIM), jnp.float32),
            jnp.zeros((length, 2 * model), jnp.float32),
        )
        query_grad, full_grad = back(
            state, lax.all_gather(gathered, "seq", axis=0, tiled=True), jnp.int32(0)
        )
        key_value_grad = lax.psum_scatter(
            full_grad.astype(jnp.bfloat16), "seq", scatter_dimension=0, tiled=True
        ).astype(jnp.float32)
        mixed_grad_low = jnp.concatenate(
            [query_grad.reshape(rows, model), key_value_grad], axis=1
        ).astype(jnp.bfloat16)
        query_bias = jnp.sum(mixed_grad_low[:, :model].astype(jnp.float32), axis=0)
        value_bias = jnp.sum(mixed_grad_low[:, 2 * model :].astype(jnp.float32), axis=0)
        in_matrix_grad = jnp.einsum(
            "td,tm->dm", stream_low, mixed_grad_low, preferred_element_type=jnp.float32
        )
        grad = first_grad + jnp.einsum(
            "tm,dm->td", mixed_grad_low, in_weight[layer], preferred_element_type=jnp.float32
        )
        collected[layer] = (
            in_matrix_grad,
            out_matrix_grad,
            up_matrix_grad,
            down_matrix_grad,
            jnp.stack([gain_one, gain_two]),
            jnp.stack([query_bias, value_bias, out_bias, up_bias, down_bias, shift_one, shift_two]),
        )
    in_stack = jnp.stack([collected[layer][0] for layer in range(LAYERS)])
    out_stack = jnp.stack([collected[layer][1] for layer in range(LAYERS)])
    up_stack = jnp.stack([collected[layer][2] for layer in range(LAYERS)])
    down_stack = jnp.stack([collected[layer][3] for layer in range(LAYERS)])
    gains_stack = jnp.stack([collected[layer][4] for layer in range(LAYERS)])
    biases_stack = jnp.stack([collected[layer][5] for layer in range(LAYERS)])
    in_total, out_total, up_total, down_total, gains_total, biases_total = lax.psum(
        (in_stack, out_stack, up_stack, down_stack, gains_stack, biases_stack), ("dp", "seq")
    )
    stream_rms = jnp.sqrt(square_total / (count_total * model))
    return (
        layer_output,
        grad[None],
        in_total,
        out_total,
        up_total,
        down_total,
        gains_total,
        biases_total,
        stream_rms,
    )


MESH = pl.DeviceIdType.MESH
LOW = jnp.bfloat16
F32 = jnp.float32
SMALL_ROWS = 32


def nn(left, right):
    return lax.dot_general(left, right, (((1,), (0,)), ((), ())), preferred_element_type=F32)


def nt(left, right):
    return lax.dot_general(left, right, (((1,), (1,)), ((), ())), preferred_element_type=F32)


def tn(left, right):
    return lax.dot_general(left, right, (((0,), (0,)), ((), ())), preferred_element_type=F32)


def column_sum(value):
    return jnp.sum(value.astype(F32), axis=0, keepdims=True)


def pad_head(rows, which):
    blank = jnp.zeros_like(rows)
    return jnp.concatenate([rows, blank] if which == 0 else [blank, rows], axis=0)


class Sems:
    def __init__(self, send, recv, near):
        self.send, self.recv, self.near = send, recv, near
        self.far_used = self.near_used = 0
        self.spare = []

    def take_set(self):
        if self.spare:
            return self.spare.pop(0)
        first = self.far_used
        self.far_used += SET
        return first

    def far(self, src, dst, device, index=None):
        if index is None:
            index = self.far_used
            self.far_used += 1
        return pltpu.make_async_remote_copy(
            src_ref=src,
            dst_ref=dst,
            send_sem=self.send.at[index],
            recv_sem=self.recv.at[index],
            device_id=device,
            device_id_type=MESH,
        )

    def local(self, src, dst):
        index = self.near_used
        self.near_used += 1
        return pltpu.make_async_copy(src, dst, self.near.at[index])


class Clock:
    def __init__(self):
        self.now = 0.0
        self.free = {"core": 0.0, "x": 0.0, "y": 0.0, "z": 0.0}

    def transfer(self, loads):
        end = 0.0
        for link, load in loads.items():
            begin = max(self.free[link], self.now)
            self.free[link] = begin + load
            end = max(end, self.free[link] + (0.9 if link == "core" else 2.2))
        return end


SET = 16
FAR_SEMS = 136
NEAR_SEMS = 46


def fused_kernel(
    levels,
    tok_ref,
    starts_ref,
    flags_ref,
    valid_ref,
    win_hbm,
    wout_hbm,
    wup_hbm,
    wdn_hbm,
    gains_ref,
    biases_ref,
    og_hbm,
    lo_hbm,
    ig_hbm,
    gin_hbm,
    gout_hbm,
    gup_hbm,
    gdn_hbm,
    small_ref,
    kept_hbm,
    win,
    wout,
    wup,
    wdn,
    low,
    outer,
    keys,
    values,
    turned,
    query_t,
    weights_t,
    attended_t,
    attended_low,
    inverse_total,
    normed_one,
    normed_two,
    inverse_norm,
    hidden_low,
    active_low,
    slope_low,
    scores,
    mask,
    flow,
    query_grad_t,
    give_t,
    take_t,
    meta,
    meta_sent,
    small,
    small_in,
    small_z,
    *rest,
):
    square_sum, wide_sum = rest[:8], rest[8:16]
    send_sems, recv_sems, near_sems = rest[16:]
    rows, model = low.shape[1], low.shape[2]
    length = 2 * rows
    pairs = HEADS // 2
    d = lax.axis_index("dp")
    x = lax.axis_index("seq")
    core = lax.rem(d, 2)
    y = lax.rem(lax.div(d, 2), 2)
    z = lax.div(d, 4)
    to_core = (d + 1 - 2 * core, x)
    to_x = (d, 1 - x)
    to_y = (d + 2 - 4 * y, x)
    to_diag = (d + 1 - 2 * core, 1 - x)

    def at_z(level):
        return (d + (level - z) * 4, x)

    z_next = [lax.rem(z + step, levels) for step in range(1, levels)]
    sems = Sems(send_sems, recv_sems, near_sems)
    barrier = pltpu.get_barrier_semaphore()
    peers = [to_core, to_x, to_y, to_diag] + [at_z(level) for level in z_next]
    for peer in peers:
        pl.semaphore_signal(barrier, inc=1, device_id=peer, device_id_type=MESH)

    def load(pairs_of):
        copies = [sems.local(src, dst) for src, dst in pairs_of]
        for copy in copies:
            copy.start()
        return copies

    moved = core != x
    away_low = sems.far(tok_ref.at[0], low.at[0], to_diag)
    away_outer = sems.far(og_hbm.at[0], outer, to_diag)
    away_meta = sems.far(meta_sent, meta, to_diag)
    stay_low = sems.local(tok_ref.at[0], low.at[0])
    stay_outer = sems.local(og_hbm.at[0], outer)

    position = lax.broadcasted_iota(jnp.int32, (1, length), 1)
    segment = jnp.zeros((1, length), jnp.int32) - 1
    for cell in range(starts_ref.shape[1]):
        segment = segment + (position >= starts_ref[0:1, cell : cell + 1]).astype(jnp.int32)
    good = valid_ref[...] * (1 - flags_ref[...]) > 0
    meta_sent[...] = jnp.zeros_like(meta_sent)
    meta_sent[0:1, :] = jnp.where(good, segment, -1).astype(F32)
    meta_sent[1:2, :] = segment.astype(F32)
    meta_sent[2:3, :] = valid_ref[...].astype(F32)

    pl.semaphore_wait(barrier, len(peers))

    @pl.when(moved)
    def _():
        away_meta.start()
        away_low.start()

    @pl.when(jnp.logical_not(moved))
    def _():
        stay_low.start()
        meta[...] = meta_sent[...]

    weight_loads = []
    for layer in range(LAYERS):
        weight_loads.append(
            [
                load([(win_hbm.at[layer], win.at[layer])])[0],
                load([(wout_hbm.at[layer], wout.at[layer])])[0],
                load([(wup_hbm.at[layer], wup.at[layer])])[0],
                load([(wdn_hbm.at[layer], wdn.at[layer])])[0],
            ]
        )

    small[...] = jnp.zeros_like(small)

    @pl.when(moved)
    def _():
        away_meta.wait()

    near = meta[:, pl.ds(pl.multiple_of(core * rows, 128), rows)]
    far = meta[:, pl.ds(pl.multiple_of((1 - core) * rows, 128), rows)]
    near_t, far_t = near.T, far.T
    same = lax.broadcasted_iota(jnp.int32, (rows, rows), 0) == lax.broadcasted_iota(
        jnp.int32, (rows, rows), 1
    )
    mask[0:rows, :] = jnp.where((near_t[:, 0:1] == near[1:2, :]) | same, 0.0, NEG)
    mask[rows:length, :] = jnp.where(far_t[:, 0:1] == near[1:2, :], 0.0, NEG)
    valid_column = near_t[:, 2:3]
    small[0, 24:25, :] = near[2:3, :]

    @pl.when(moved)
    def _():
        away_low.wait()
        away_outer.start()

    @pl.when(jnp.logical_not(moved))
    def _():
        stay_low.wait()
        stay_outer.start()

    def note_square(layer, which, value):
        row = 18 + 3 * layer + which
        small[0, row : row + 1, :] = column_sum(value * value * valid_column)

    staged = square_sum[0].at[3 * LAYERS - 1]
    spills = []
    flow[...] = low[0].astype(F32)
    for layer in range(LAYERS):
        bias = [biases_ref[k, layer : layer + 1, :] for k in range(7)]
        gain = [gains_ref[layer, k : k + 1, :] for k in range(2)]
        load_in, load_out, load_up, load_down = weight_loads[layer]
        load_in.wait()
        stream_low = low[layer]
        note_square(layer, 0, flow[...])
        keys[layer, 0:rows, :] = nn(stream_low, win[layer, :, model : 2 * model]).astype(LOW)
        send_keys = sems.far(
            keys.at[layer, pl.ds(0, rows)], keys.at[layer, pl.ds(rows, rows)], to_core
        )
        send_keys.start()
        values[layer, 0:rows, :] = (
            nn(stream_low, win[layer, :, 2 * model : 3 * model]) + bias[1]
        ).astype(LOW)
        send_values = sems.far(
            values.at[layer, pl.ds(0, rows)], values.at[layer, pl.ds(rows, rows)], to_core
        )
        send_values.start()
        query = (nn(stream_low, win[layer, :, 0:model]) + bias[0]).astype(LOW)
        query_t[layer] = (query.astype(F32) * (1.0 / math.sqrt(HEAD_DIM))).T.astype(LOW)
        turned[:, 0:rows] = values[layer, 0:rows, :].T
        send_keys.wait()
        send_values.wait()
        turned[:, rows:length] = values[layer, rows:length, :].T

        def score(head, layer=layer):
            pair = head // 2
            scores[head % 2] = (
                nn(
                    keys[layer, :, 128 * pair : 128 * pair + 128],
                    pad_head(query_t[layer, 64 * head : 64 * head + 64, :], head % 2),
                )
                + mask[...]
            )

        score(0)
        for head in range(HEADS):
            if head + 1 < HEADS:
                score(head + 1)
            if layer > 0:
                spills[layer - 1][head].wait()
            block = scores[head % 2]
            best = jnp.max(block, axis=0, keepdims=True)
            weight = jnp.exp(block - best)
            inverse = 1.0 / jnp.sum(weight, axis=0, keepdims=True)
            weight_low = weight.astype(LOW)
            weights_t[head] = weight_low
            span = slice(64 * head, 64 * head + 64)
            inverse_total[layer, head : head + 1, :] = inverse
            attended_t[layer, span, :] = nn(turned[span, :], weight_low) * inverse
            if layer + 1 < LAYERS:
                if head == 0:
                    spills.append([])
                copy = sems.local(weights_t.at[head], kept_hbm.at[layer, head])
                copy.start()
                spills[layer].append(copy)
        attended_low[layer] = attended_t[layer].T.astype(LOW)
        load_out.wait()
        branch = nn(attended_low[layer], wout[layer]) + bias[2]
        note_square(layer, 1, branch)
        total = flow[...] + branch
        centred = total - jnp.mean(total, axis=-1, keepdims=True)
        inverse = lax.rsqrt(jnp.mean(centred * centred, axis=-1, keepdims=True) + EPS)
        normed = centred * inverse
        normed_one[layer] = normed.astype(LOW)
        inverse_norm[:, 2 * layer : 2 * layer + 1] = inverse
        hidden = normed * gain[0] + bias[5]
        flow[...] = hidden
        hidden_low[layer] = hidden.astype(LOW)
        load_up.wait()
        inner = nn(hidden_low[layer], wup[layer]) + bias[3]
        share = 0.5 * (1.0 + lax.erf(inner * 0.7071067811865476))
        active_low[layer] = (inner * share).astype(LOW)
        slope_low[layer] = (
            share + inner * jnp.exp(-0.5 * inner * inner) * 0.3989422804014327
        ).astype(LOW)
        load_down.wait()
        ff_out = nn(active_low[layer], wdn[layer]) + bias[4]
        note_square(layer, 2, ff_out)
        total = flow[...] + ff_out
        centred = total - jnp.mean(total, axis=-1, keepdims=True)
        inverse = lax.rsqrt(jnp.mean(centred * centred, axis=-1, keepdims=True) + EPS)
        normed = centred * inverse
        normed_two[layer] = normed.astype(LOW)
        inverse_norm[:, 2 * layer + 1 : 2 * layer + 2] = inverse
        result = normed * gain[1] + bias[6]
        if layer + 1 < LAYERS:
            flow[...] = result
            low[layer + 1] = result.astype(LOW)
        else:
            staged[...] = result.astype(LOW).reshape(staged.shape)

    away_result = sems.far(staged, lo_hbm, to_diag)
    stay_result = sems.local(staged, lo_hbm)
    away_grad = sems.far(outer, ig_hbm.at[0], to_diag)
    stay_grad = sems.local(outer, ig_hbm.at[0])

    @pl.when(moved)
    def _():
        away_outer.wait()
        away_result.start()

    @pl.when(jnp.logical_not(moved))
    def _():
        stay_outer.wait()
        stay_result.start()

    piece = model // 8 // levels
    own_rows = pl.ds(pl.multiple_of(z * piece, piece), piece)
    clock = Clock()

    def reduce_chunk(buffers, begin, count, homes):
        mine, whole, take_core, take_x, take_y, take_ay, take_bx, take_z = buffers
        width = mine.shape[-1]
        size = count * width / model
        some = pl.ds(begin, count)
        landed = pl.ds(begin % take_core.shape[0], count)
        left, right = pl.ds(0, width // 2), pl.ds(width // 2, width // 2)
        every = slice(None)
        first = sems.take_set()
        used = [0]

        def send(src, dst, peer):
            copy = sems.far(src, dst, peer, first + used[0])
            used[0] += 1
            copy.start()
            return copy

        def send_same(at, peer):
            return send(whole.at[at], whole.at[at], peer)

        def add_into(at, value):
            mine[at] = (mine[at].astype(F32) + value.astype(F32)).astype(LOW)

        def finish(copies):
            for copy in copies:
                copy.wait()

        mine_core, mine_left, mine_right = (
            (some, core),
            (some, core, x, every, every, left),
            (some, core, every, y, every, right),
        )
        deep_left, deep_right = (some, core, x, y, every, left), (some, core, x, y, every, right)
        own = (some, core, x, y, own_rows)

        flight = [send(mine.at[some, 1 - core], take_core.at[landed], to_core)]
        yield {"core": 0.46 * size}
        finish(flight)
        add_into(mine_core, take_core[landed])
        flight = [
            send(mine.at[some, core, 1 - x, every, every, left], take_x.at[some], to_x),
            send(mine.at[some, core, every, 1 - y, every, right], take_y.at[some], to_y),
        ]
        yield {"x": 1.44 * size, "y": 1.44 * size}
        finish(flight)
        add_into(mine_left, take_x[some])
        add_into(mine_right, take_y[some])
        flight = [
            send(mine.at[some, core, x, 1 - y, every, left], take_ay.at[some], to_y),
            send(mine.at[some, core, 1 - x, y, every, right], take_bx.at[some], to_x),
        ]
        yield {"x": 0.72 * size, "y": 0.72 * size}
        finish(flight)
        add_into(deep_left, take_ay[some])
        add_into(deep_right, take_bx[some])
        flight = [
            send(
                mine.at[some, core, x, y, pl.ds(pl.multiple_of(level * piece, piece), piece)],
                take_z.at[step, some],
                at_z(level),
            )
            for step, level in enumerate(z_next)
        ]
        yield {"z": 1.35 * size}
        finish(flight)
        total = mine[own].astype(F32)
        for step in range(levels - 1):
            total = total + take_z[step, some].astype(F32)
        whole[own] = total.astype(LOW)
        flight = [send_same(own, at_z(level)) for level in z_next]
        yield {"z": 1.35 * size}
        finish(flight)
        flight = [send_same(deep_left, to_y), send_same(deep_right, to_x)]
        yield {"x": 0.72 * size, "y": 0.72 * size}
        finish(flight)
        flight = [send_same(mine_left, to_x), send_same(mine_right, to_y)]
        yield {"x": 1.44 * size, "y": 1.44 * size}
        finish(flight)
        flight = [send_same(mine_core, to_core)]
        yield {"core": 0.46 * size}
        finish(flight)
        sems.spare.append(first)
        for src, dst in homes:
            copy = sems.local(src, dst)
            copy.start()
            homing.append(copy)

    def reduce_small():
        for step, peer in enumerate((to_core, to_x, to_y)):
            copy = sems.far(small.at[step], small_in.at[step], peer)
            copy.start()
            yield {"core": 0.1} if step == 0 else {"xy"[step - 1]: 1.5}
            copy.wait()
            small[step + 1] = small[step] + small_in[step]
        copies = [sems.far(small.at[3], small_z.at[z], at_z(level)) for level in z_next]
        for copy in copies:
            copy.start()
        small_z[z] = small[3]
        yield {"z": 2.0}
        for copy in copies:
            copy.wait()
        total = small_z[0]
        for level in range(1, levels):
            total = total + small_z[level]
        small_ref[...] = total

    homing = []
    active = []

    def advance(entry):
        loads = next(entry[1], None)
        clock.now += 0.15
        if loads is None:
            active.remove(entry)
        else:
            entry[0] = clock.transfer(loads)

    def begin(chunk):
        entry = [0.0, chunk]
        active.append(entry)
        advance(entry)

    def pump(spent):
        clock.now += spent
        while True:
            ready = [entry for entry in active if entry[0] <= clock.now]
            if not ready:
                return
            advance(ready[0])

    def note(row, value):
        small[0, row : row + 1, :] = value

    reloads = []
    flow[...] = outer[...].astype(F32)
    for layer in reversed(range(LAYERS)):
        gain = [gains_ref[layer, k : k + 1, :] for k in range(2)]
        base = 3 * (LAYERS - 1 - layer)
        wide = 2 * (LAYERS - 1 - layer)
        mine, whole = square_sum[:2]
        folded = mine.shape[1:]
        bias_row = 4 + 7 * layer
        grad = flow[...]
        normed = normed_two[layer].astype(F32)
        note(2 * layer + 1, column_sum(grad * normed))
        note(bias_row + 6, column_sum(grad))
        scaled = grad * gain[1]
        second = inverse_norm[:, 2 * layer + 1 : 2 * layer + 2] * (
            scaled
            - jnp.mean(scaled, axis=-1, keepdims=True)
            - normed * jnp.mean(scaled * normed, axis=-1, keepdims=True)
        )
        scores[0, 0:rows, :] = second
        down_low = second.astype(LOW)
        note(bias_row + 4, column_sum(down_low))
        mine[base] = tn(active_low[layer], down_low).astype(LOW).reshape(folded)
        inner_low = (nt(down_low, wdn[layer]) * slope_low[layer].astype(F32)).astype(LOW)
        note(bias_row + 3, column_sum(inner_low))
        mine[base + 1] = tn(hidden_low[layer], inner_low).astype(LOW).reshape(folded)
        pump(4.0)
        begin(
            reduce_chunk(
                square_sum,
                base,
                2,
                [
                    (whole.at[base], gdn_hbm.at[layer]),
                    (whole.at[base + 1], gup_hbm.at[layer]),
                ],
            )
        )
        grad = scores[0, 0:rows, :] + nt(inner_low, wup[layer])
        normed = normed_one[layer].astype(F32)
        note(2 * layer, column_sum(grad * normed))
        note(bias_row + 5, column_sum(grad))
        scaled = grad * gain[0]
        flow[...] = inverse_norm[:, 2 * layer : 2 * layer + 1] * (
            scaled
            - jnp.mean(scaled, axis=-1, keepdims=True)
            - normed * jnp.mean(scaled * normed, axis=-1, keepdims=True)
        )
        branch_low = flow[...].astype(LOW)
        note(bias_row + 2, column_sum(branch_low))
        mine[base + 2] = tn(attended_low[layer], branch_low).astype(LOW).reshape(folded)
        pump(2.0)
        begin(
            reduce_chunk(square_sum, base + 2, 1, [(whole.at[base + 2], gout_hbm.at[layer])])
        )
        attended_grad_t = nt(branch_low, wout[layer]).astype(LOW).T
        turned[:, 0:rows] = keys[layer, 0:rows, :].T
        turned[:, rows:length] = keys[layer, rows:length, :].T
        pump(1.5)
        gives = []

        def close_half(half, layer=layer, wide=wide, bias_row=bias_row, gives=gives):
            side = slice(model // 2 * half, model // 2 * half + model // 2)
            for copy in gives[2 * half : 2 * half + 2]:
                copy.wait()
            taken = [
                jnp.concatenate([take_t[layer, 2 * half + k, which] for k in range(2)], axis=0)
                for which in range(2)
            ]
            values_side = slice(model + side.start, model + side.stop)
            parts = [
                query_grad_t[side, :].T,
                (mask[side, :] + taken[0].astype(F32)).astype(LOW).T,
                (mask[values_side, :] + taken[1].astype(F32)).astype(LOW).T,
            ]
            mine, whole = wide_sum[:2]
            homes = []
            for k, part in enumerate(parts):
                columns = slice(model // 2 * k, model // 2 * k + model // 2)
                mine[wide + half, :, :, :, :, columns] = (
                    tn(low[layer], part).astype(LOW).reshape(mine.shape[1:5] + (model // 2,))
                )
                homes.append(
                    (
                        whole.at[wide + half, :, :, :, :, columns],
                        gin_hbm.at[
                            layer, :, :, :, :, pl.ds(model * k + side.start, model // 2)
                        ],
                    )
                )
            small[0, bias_row : bias_row + 1, side] = column_sum(parts[0])
            small[0, bias_row + 1 : bias_row + 2, side] = column_sum(parts[2])
            pump(2.0)
            begin(reduce_chunk(wide_sum, wide + half, 1, homes))
            total = flow[...]
            for k, part in enumerate(parts):
                columns = slice(model * k + side.start, model * k + side.stop)
                total = total + nt(part, win[layer, :, columns])
            if layer > 0 or half == 0:
                flow[...] = total
            else:
                outer[...] = total.astype(LOW)

        for head in range(HEADS):
            pair = head // 2
            span = slice(64 * head, 64 * head + 64)
            lanes = slice(128 * pair, 128 * pair + 128)
            grad_low = (
                attended_grad_t[span, :].astype(F32) * inverse_total[layer, head : head + 1, :]
            ).astype(LOW)
            delta = column_sum(grad_low.astype(F32) * attended_t[layer, span, :])
            if layer + 1 < LAYERS:
                reloads[head].wait()
            weight_low = weights_t[head]
            prob_grad = nn(values[layer, :, lanes], pad_head(grad_low, head % 2))
            score_grad = (weight_low.astype(F32) * (prob_grad - delta)).astype(LOW)
            query_grad_t[span, :] = (
                nn(turned[span, :], score_grad) * (1.0 / math.sqrt(HEAD_DIM))
            ).astype(LOW)
            key_grad = nt(query_t[layer, span, :], score_grad)
            value_grad = nt(grad_low, weight_low)
            inside = slice(64 * (head % 2), 64 * (head % 2) + 64)
            mask[span, :] = key_grad[:, 0:rows]
            mask[64 * head + model : 64 * head + model + 64, :] = value_grad[:, 0:rows]
            give_t[pair, 0, inside, :] = key_grad[:, rows:length].astype(LOW)
            give_t[pair, 1, inside, :] = value_grad[:, rows:length].astype(LOW)
            if layer > 0:
                copy = sems.local(kept_hbm.at[layer - 1, head], weights_t.at[head])
                copy.start()
                reloads.append(copy)
            if head % 2 == 1:
                copy = sems.far(give_t.at[pair], take_t.at[layer, pair], to_core)
                copy.start()
                gives.append(copy)
            pump(1.15)
            if head == HEADS // 2:
                close_half(0)
        close_half(1)
        if layer == 0:
            begin(reduce_small())
        if layer > 0:

            @pl.when(moved)
            def _():
                away_result.wait()

            @pl.when(jnp.logical_not(moved))
            def _():
                stay_result.wait()

        pump(1.3)

    @pl.when(moved)
    def _():
        away_grad.start()

    @pl.when(jnp.logical_not(moved))
    def _():
        stay_grad.start()

    while active:
        clock.now = max(clock.now, min(entry[0] for entry in active))
        pump(0.0)
    for copy in homing:
        copy.wait()

    @pl.when(moved)
    def _():
        away_grad.wait()

    @pl.when(jnp.logical_not(moved))
    def _():
        stay_grad.wait()

    assert sems.far_used <= FAR_SEMS and sems.near_used <= NEAR_SEMS


def local_pair(
    tokens,
    cell_starts,
    generate_flags,
    valid_mask,
    in_weight,
    out_weight,
    up_weight,
    down_weight,
    norm_gains,
    biases,
    out_grad,
):
    rows, model = tokens.shape[1:]
    length = 2 * rows
    levels = lax.axis_size("dp") // 4
    eighth = model // 8
    folded = (2, 2, 2, eighth)

    def sum_buffers(count, shared, width):
        half = width // 2
        return [
            pltpu.VMEM((count,) + folded + (width,), LOW),
            pltpu.VMEM((count,) + folded + (width,), LOW),
            pltpu.VMEM((shared,) + folded[1:] + (width,), LOW),
            pltpu.VMEM((count, 2, eighth, half), LOW),
            pltpu.VMEM((count, 2, eighth, half), LOW),
            pltpu.VMEM((count, eighth, half), LOW),
            pltpu.VMEM((count, eighth, half), LOW),
            pltpu.VMEM((max(levels - 1, 1), count, eighth // levels, width), LOW),
        ]

    shape = jax.ShapeDtypeStruct
    vmem, anywhere = pl.BlockSpec(memory_space=pltpu.VMEM), pl.BlockSpec(memory_space=pl.ANY)
    by_layer = (LAYERS, rows, model)
    scratch = [
        pltpu.VMEM(in_weight.shape, LOW),
        pltpu.VMEM(out_weight.shape, LOW),
        pltpu.VMEM(up_weight.shape, LOW),
        pltpu.VMEM(down_weight.shape, LOW),
        pltpu.VMEM(by_layer, LOW),
        pltpu.VMEM((rows, model), LOW),
        pltpu.VMEM((LAYERS, length, model), LOW),
        pltpu.VMEM((LAYERS, length, model), LOW),
        pltpu.VMEM((model, length), LOW),
        pltpu.VMEM((LAYERS, model, rows), LOW),
        pltpu.VMEM((HEADS, length, rows), LOW),
        pltpu.VMEM((LAYERS, model, rows), F32),
        pltpu.VMEM(by_layer, LOW),
        pltpu.VMEM((LAYERS, HEADS, rows), F32),
        pltpu.VMEM(by_layer, LOW),
        pltpu.VMEM(by_layer, LOW),
        pltpu.VMEM((rows, 2 * LAYERS), F32),
        pltpu.VMEM(by_layer, LOW),
        pltpu.VMEM(by_layer, LOW),
        pltpu.VMEM(by_layer, LOW),
        pltpu.VMEM((2, length, rows), F32),
        pltpu.VMEM((length, rows), F32),
        pltpu.VMEM((rows, model), F32),
        pltpu.VMEM((model, rows), LOW),
        pltpu.VMEM((HEADS // 2, 2, 128, rows), LOW),
        pltpu.VMEM((LAYERS, HEADS // 2, 2, 128, rows), LOW),
        pltpu.VMEM((8, length), F32),
        pltpu.VMEM((8, length), F32),
        pltpu.VMEM((4, SMALL_ROWS, model), F32),
        pltpu.VMEM((3, SMALL_ROWS, model), F32),
        pltpu.VMEM((levels, SMALL_ROWS, model), F32),
        *sum_buffers(3 * LAYERS, 3, model),
        *sum_buffers(2 * LAYERS, 2, 3 * model // 2),
        pltpu.SemaphoreType.DMA((FAR_SEMS,)),
        pltpu.SemaphoreType.DMA((FAR_SEMS,)),
        pltpu.SemaphoreType.DMA((NEAR_SEMS,)),
    ]
    lo, ig, gin, gout, gup, gdn, small, _ = pl.pallas_call(
        functools.partial(fused_kernel, levels),
        out_shape=[
            shape(folded + (model,), LOW),
            shape(tokens.shape, LOW),
            shape((LAYERS,) + folded + (3 * model,), LOW),
            shape((LAYERS,) + folded + (model,), LOW),
            shape((LAYERS,) + folded + (model,), LOW),
            shape((LAYERS,) + folded + (model,), LOW),
            shape((SMALL_ROWS, model), F32),
            shape((LAYERS - 1, HEADS, length, rows), LOW),
        ],
        in_specs=[anywhere, vmem, vmem, vmem] + [anywhere] * 4 + [vmem, vmem, anywhere],
        out_specs=[anywhere] * 6 + [vmem, anywhere],
        scratch_shapes=scratch,
        compiler_params=pltpu.CompilerParams(
            collective_id=0, has_side_effects=True, vmem_limit_bytes=VMEM_BYTES
        ),
    )(
        tokens,
        cell_starts,
        generate_flags,
        valid_mask,
        in_weight,
        out_weight,
        up_weight,
        down_weight,
        norm_gains,
        biases.transpose(1, 0, 2),
        out_grad,
    )
    return finish(tokens, in_weight, lo, ig, gin, gout, gup, gdn, small)


VMEM_BYTES = 63 * 1024 * 1024


def finish_kernel(model, *refs):
    lo_in, ig_in, gin_in, gout_in, gup_in, gdn_in, small = refs[:7]
    lo, ig, gin, gout, gup, gdn, gains, shifts, rms = refs[7:16]
    low_wide, wide, low_square, square, in_sems, out_sems, straight_sem = refs[16:]
    straight = pltpu.make_async_copy(lo_in, lo, straight_sem)
    straight.start()
    pieces = []
    for index in range(low_wide.shape[0]):
        pieces.append((gin_in.at[index], low_wide.at[index], wide.at[index], gin.at[index]))
    count = 0
    for source, target in ((gout_in, gout), (gup_in, gup), (gdn_in, gdn), (ig_in, ig)):
        for index in range(source.shape[0]):
            pieces.append(
                (source.at[index], low_square.at[count], square.at[count], target.at[index])
            )
            count += 1
    reads = [
        pltpu.make_async_copy(piece[0], piece[1], in_sems.at[k]) for k, piece in enumerate(pieces)
    ]
    writes = [
        pltpu.make_async_copy(piece[2], piece[3], out_sems.at[k]) for k, piece in enumerate(pieces)
    ]
    for read in reads:
        read.start()
    for layer in range(LAYERS):
        for k in range(2):
            row = 2 * layer + k
            gains[layer, k : k + 1, :] = small[row : row + 1, :]
        for k in range(7):
            row = 2 * LAYERS + 7 * layer + k
            shifts[k, layer : layer + 1, :] = small[row : row + 1, :]
    first = 9 * LAYERS
    count = jnp.sum(small[first + 3 * LAYERS : first + 3 * LAYERS + 1, :], keepdims=True)
    line = lax.broadcasted_iota(jnp.int32, rms.shape, 0)
    place = lax.broadcasted_iota(jnp.int32, rms.shape, 1)
    squares = jnp.zeros(rms.shape, F32)
    for layer in range(LAYERS):
        for k in range(3):
            row = first + 3 * layer + k
            value = jnp.sum(small[row : row + 1, :], keepdims=True)
            squares = jnp.where((line == layer) & (place == k), value, squares)
    rms[...] = jnp.sqrt(squares / (count * model))
    for read, write, piece in zip(reads, writes, pieces):
        read.wait()
        piece[2][...] = piece[1][...].astype(F32)
        write.start()
    for write in writes:
        write.wait()
    straight.wait()


def finish(tokens, in_weight, lo, ig, gin, gout, gup, gdn, small):
    rows, model = tokens.shape[1:]
    shape = jax.ShapeDtypeStruct
    vmem, anywhere = pl.BlockSpec(memory_space=pltpu.VMEM), pl.BlockSpec(memory_space=pl.ANY)
    slabs = 4 * LAYERS
    wide = (slabs, model * LAYERS // slabs, 3 * model)
    square = (LAYERS, model, model)
    outs = pl.pallas_call(
        functools.partial(finish_kernel, model),
        out_shape=[
            shape(tokens.shape, LOW),
            shape(tokens.shape, F32),
            shape(wide, F32),
            shape(square, F32),
            shape(square, F32),
            shape(square, F32),
            shape((LAYERS, 2, model), F32),
            shape((7, LAYERS, model), F32),
            shape((LAYERS, 3), F32),
        ],
        in_specs=[anywhere] * 6 + [vmem],
        out_specs=[anywhere] * 6 + [vmem] * 3,
        scratch_shapes=[
            pltpu.VMEM(wide, LOW),
            pltpu.VMEM(wide, F32),
            pltpu.VMEM((3 * LAYERS + 1, model, model), LOW),
            pltpu.VMEM((3 * LAYERS + 1, model, model), F32),
            pltpu.SemaphoreType.DMA((slabs + 3 * LAYERS + 1,)),
            pltpu.SemaphoreType.DMA((slabs + 3 * LAYERS + 1,)),
            pltpu.SemaphoreType.DMA,
        ],
        compiler_params=pltpu.CompilerParams(vmem_limit_bytes=40 * 1024 * 1024),
    )(
        lo.reshape(tokens.shape),
        ig,
        gin.reshape(wide),
        gout.reshape(square),
        gup.reshape(square),
        gdn.reshape(square),
        small,
    )
    lo, ig, gin, gout, gup, gdn, gains, shifts, rms = outs
    return lo, ig, gin.reshape(in_weight.shape), gout, gup, gdn, gains, shifts.transpose(1, 0, 2), rms


def solution(mesh):
    placed = (
        P("dp", "seq", None),
        P("dp", None),
        P("dp", None),
        P("dp", None),
        P(),
        P(),
        P(),
        P(),
        P(),
        P(),
        P("dp", "seq", None),
    )
    paired = mesh.shape["seq"] == 2 and mesh.shape["dp"] % 4 == 0
    return jax.shard_map(
        local_pair if paired else local,
        mesh=mesh,
        in_specs=placed,
        out_specs=(P("dp", "seq", None), P("dp", "seq", None), P(), P(), P(), P(), P(), P(), P()),
        check_vma=False,
    )
```

```python
import functools
import math

import jax
import jax.numpy as jnp
from jax import lax
from jax.experimental import pallas as pl
from jax.experimental.pallas import tpu as pltpu
from jax.sharding import PartitionSpec as P

HEADS = 8
HEAD_DIM = 64
LAYERS = 2


EPS = 1e-05
NEG = -1e30


def block_width(count):
    for option in range(1024, 255, -1):
        if count % option == 0:
            return option
    return count


def segment_ids(starts_row, positions):
    return jnp.sum((positions[:, None] >= starts_row[None, :]).astype(jnp.int32), axis=1) - 1


def norm_rows(total, gain, shift):
    mean = jnp.mean(total, axis=-1, keepdims=True)
    centred = total - mean
    spread = jnp.mean(centred * centred, axis=-1, keepdims=True)
    inverse = lax.rsqrt(spread + EPS)
    normed = centred * inverse
    return (normed * gain + shift, normed, inverse)


def norm_back(grad, normed, inverse, gain):
    scaled = grad * gain
    return inverse * (
        scaled
        - jnp.mean(scaled, axis=-1, keepdims=True)
        - normed * jnp.mean(scaled * normed, axis=-1, keepdims=True)
    )


def gelu_slope(inner):
    return (
        0.5 * (1.0 + jax.scipy.special.erf(inner * 0.7071067811865476))
        + inner * jnp.exp(-0.5 * inner * inner) * 0.3989422804014327
    )


def make_mask(query_pos, query_seg, starts_row, key_ok_row):

    def mask_for(begin, width):
        key_pos = begin + jnp.arange(width, dtype=jnp.int32)
        key_seg = segment_ids(starts_row, key_pos)
        key_good = lax.dynamic_slice_in_dim(key_ok_row, begin, width, 0) > 0
        return (query_seg[:, None] == key_seg[None, :]) & (
            key_good[None, :] | (query_pos[:, None] == key_pos[None, :])
        )

    return mask_for


def make_attend(query_heads, mask_for, scale):

    def attend(carry, piece, start):
        count = piece.shape[0]
        width = block_width(count)
        model = piece.shape[1] // 2

        def attend_one_block(step, state):
            best, total, summed = state
            begin = step * width
            block = lax.dynamic_slice_in_dim(piece, begin, width, 0)
            key_heads = block[:, :model].reshape(width, HEADS, HEAD_DIM)
            value_heads = block[:, model:].reshape(width, HEADS, HEAD_DIM)
            allowed = mask_for(start + begin, width)[None]
            scores = (
                jnp.einsum(
                    "qhd,khd->hqk", query_heads, key_heads, preferred_element_type=jnp.float32
                )
                * scale
            )
            scores = jnp.where(allowed, scores, NEG)
            new_best = jnp.maximum(best, jnp.max(scores, axis=-1))
            factor = jnp.exp(best - new_best)
            weights = jnp.where(allowed, jnp.exp(scores - new_best[:, :, None]), 0.0)
            total = total * factor + jnp.sum(weights, axis=-1)
            update = jnp.einsum(
                "hqk,khd->qhd",
                weights.astype(jnp.bfloat16),
                value_heads,
                preferred_element_type=jnp.float32,
            )
            summed = summed * factor.T[:, :, None] + update
            return (new_best, total, summed)

        return lax.fori_loop(0, count // width, attend_one_block, carry)

    return attend


def make_back(query_heads, grad_heads, log_total, delta, mask_for, scale):

    def back(carry, piece, start):
        count = piece.shape[0]
        width = block_width(count)
        model = piece.shape[1] // 2

        def back_one_block(step, state):
            query_grad, full_grad = state
            begin = step * width
            block = lax.dynamic_slice_in_dim(piece, begin, width, 0)
            key_heads = block[:, :model].reshape(width, HEADS, HEAD_DIM)
            value_heads = block[:, model:].reshape(width, HEADS, HEAD_DIM)
            allowed = mask_for(start + begin, width)[None]
            scores = (
                jnp.einsum(
                    "qhd,khd->hqk", query_heads, key_heads, preferred_element_type=jnp.float32
                )
                * scale
            )
            probs = jnp.where(allowed, jnp.exp(scores - log_total[:, :, None]), 0.0)
            prob_grad = jnp.einsum(
                "qhd,khd->hqk", grad_heads, value_heads, preferred_element_type=jnp.float32
            )
            score_grad = (probs * (prob_grad - delta[:, :, None])).astype(jnp.bfloat16)
            query_grad = (
                query_grad
                + jnp.einsum(
                    "hqk,khd->qhd", score_grad, key_heads, preferred_element_type=jnp.float32
                )
                * scale
            )
            key_grad = (
                jnp.einsum(
                    "hqk,qhd->khd", score_grad, query_heads, preferred_element_type=jnp.float32
                )
                * scale
            )
            value_grad = jnp.einsum(
                "hqk,qhd->khd",
                probs.astype(jnp.bfloat16),
                grad_heads,
                preferred_element_type=jnp.float32,
            )
            update = jnp.concatenate(
                [key_grad.reshape(width, model), value_grad.reshape(width, model)], axis=1
            )
            place = start + begin
            current = lax.dynamic_slice_in_dim(full_grad, place, width, 0)
            full_grad = lax.dynamic_update_slice_in_dim(full_grad, current + update, place, 0)
            return (query_grad, full_grad)

        return lax.fori_loop(0, count // width, back_one_block, carry)

    return back


def local(
    tokens,
    cell_starts,
    generate_flags,
    valid_mask,
    in_weight,
    out_weight,
    up_weight,
    down_weight,
    norm_gains,
    biases,
    out_grad,
):
    rows = tokens.shape[1]
    model = tokens.shape[2]
    scale = 1.0 / math.sqrt(HEAD_DIM)
    first = lax.axis_index("seq") * rows
    query_pos = first + jnp.arange(rows, dtype=jnp.int32)
    starts_row = cell_starts[0]
    key_ok_row = valid_mask[0] * (1 - generate_flags[0])
    mask_for = make_mask(query_pos, segment_ids(starts_row, query_pos), starts_row, key_ok_row)
    valid_here = lax.dynamic_slice_in_dim(valid_mask[0], first, rows, 0).astype(jnp.float32)
    stream = tokens[0].astype(jnp.float32)
    stream_low = tokens[0]
    kept = []
    squares = []
    for layer in range(LAYERS):
        bias_rows = biases[layer]
        gains_pair = norm_gains[layer]
        mixed = jnp.dot(
            stream_low, in_weight[layer], preferred_element_type=jnp.float32
        ) + jnp.concatenate([bias_rows[0], jnp.zeros((model,), jnp.float32), bias_rows[1]])
        mixed_low = mixed.astype(jnp.bfloat16)
        query_heads = mixed_low[:, :model].reshape(rows, HEADS, HEAD_DIM)
        key_value = mixed_low[:, model:]
        attend = make_attend(query_heads, mask_for, scale)
        state = (
            jnp.full((HEADS, rows), NEG, jnp.float32),
            jnp.zeros((HEADS, rows), jnp.float32),
            jnp.zeros((rows, HEADS, HEAD_DIM), jnp.float32),
        )
        gathered = key_value
        best, total, summed = attend(
            state, lax.all_gather(key_value, "seq", axis=0, tiled=True), jnp.int32(0)
        )
        attended = (summed / total.T[:, :, None]).reshape(rows, model)
        log_total = best + jnp.log(total)
        attended_low = attended.astype(jnp.bfloat16)
        branch = (
            jnp.dot(attended_low, out_weight[layer], preferred_element_type=jnp.float32)
            + bias_rows[2]
        )
        hidden, normed_one, inverse_one = norm_rows(stream + branch, gains_pair[0], bias_rows[5])
        hidden_low = hidden.astype(jnp.bfloat16)
        inner = (
            jnp.dot(hidden_low, up_weight[layer], preferred_element_type=jnp.float32) + bias_rows[3]
        )
        active_low = jax.nn.gelu(inner, approximate=False).astype(jnp.bfloat16)
        ff_out = (
            jnp.dot(active_low, down_weight[layer], preferred_element_type=jnp.float32)
            + bias_rows[4]
        )
        result, normed_two, inverse_two = norm_rows(hidden + ff_out, gains_pair[1], bias_rows[6])
        squares.append(
            jnp.stack(
                [
                    jnp.sum(valid_here * jnp.sum(part * part, axis=-1))
                    for part in (stream, branch, ff_out)
                ]
            )
        )
        kept.append(
            (
                stream_low,
                query_heads,
                gathered,
                attended,
                attended_low,
                log_total,
                normed_one,
                inverse_one,
                hidden_low,
                inner,
                active_low,
                normed_two,
                inverse_two,
            )
        )
        stream = result
        stream_low = result.astype(jnp.bfloat16)
    layer_output = stream.astype(jnp.bfloat16)[None]
    square_local = jnp.stack(squares)
    count_local = jnp.sum(valid_here)
    square_total, count_total = lax.psum((square_local, count_local), ("dp", "seq"))
    grad = out_grad[0].astype(jnp.float32)
    length = rows * lax.axis_size("seq")
    collected = [None] * LAYERS
    for layer in reversed(range(LAYERS)):
        (
            stream_low,
            query_heads,
            gathered,
            attended,
            attended_low,
            log_total,
            normed_one,
            inverse_one,
            hidden_low,
            inner,
            active_low,
            normed_two,
            inverse_two,
        ) = kept[layer]
        gains_pair = norm_gains[layer]
        gain_two = jnp.sum(grad * normed_two, axis=0)
        shift_two = jnp.sum(grad, axis=0)
        second_grad = norm_back(grad, normed_two, inverse_two, gains_pair[1])
        down_grad_low = second_grad.astype(jnp.bfloat16)
        down_bias = jnp.sum(down_grad_low.astype(jnp.float32), axis=0)
        down_matrix_grad = jnp.einsum(
            "tf,td->fd", active_low, down_grad_low, preferred_element_type=jnp.float32
        )
        active_grad = jnp.einsum(
            "td,fd->tf", down_grad_low, down_weight[layer], preferred_element_type=jnp.float32
        )
        inner_grad_low = (active_grad * gelu_slope(inner)).astype(jnp.bfloat16)
        up_bias = jnp.sum(inner_grad_low.astype(jnp.float32), axis=0)
        up_matrix_grad = jnp.einsum(
            "td,tf->df", hidden_low, inner_grad_low, preferred_element_type=jnp.float32
        )
        hidden_grad = second_grad + jnp.einsum(
            "tf,df->td", inner_grad_low, up_weight[layer], preferred_element_type=jnp.float32
        )
        gain_one = jnp.sum(hidden_grad * normed_one, axis=0)
        shift_one = jnp.sum(hidden_grad, axis=0)
        first_grad = norm_back(hidden_grad, normed_one, inverse_one, gains_pair[0])
        branch_grad_low = first_grad.astype(jnp.bfloat16)
        out_bias = jnp.sum(branch_grad_low.astype(jnp.float32), axis=0)
        out_matrix_grad = jnp.einsum(
            "td,te->de", attended_low, branch_grad_low, preferred_element_type=jnp.float32
        )
        attended_grad_low = jnp.einsum(
            "te,de->td", branch_grad_low, out_weight[layer], preferred_element_type=jnp.float32
        ).astype(jnp.bfloat16)
        grad_heads = attended_grad_low.reshape(rows, HEADS, HEAD_DIM)
        delta = jnp.sum(
            (attended_grad_low.astype(jnp.float32) * attended).reshape(rows, HEADS, HEAD_DIM),
            axis=-1,
        ).T
        back = make_back(query_heads, grad_heads, log_total, delta, mask_for, scale)
        state = (
            jnp.zeros((rows, HEADS, HEAD_DIM), jnp.float32),
            jnp.zeros((length, 2 * model), jnp.float32),
        )
        query_grad, full_grad = back(
            state, lax.all_gather(gathered, "seq", axis=0, tiled=True), jnp.int32(0)
        )
        key_value_grad = lax.psum_scatter(
            full_grad.astype(jnp.bfloat16), "seq", scatter_dimension=0, tiled=True
        ).astype(jnp.float32)
        mixed_grad_low = jnp.concatenate(
            [query_grad.reshape(rows, model), key_value_grad], axis=1
        ).astype(jnp.bfloat16)
        query_bias = jnp.sum(mixed_grad_low[:, :model].astype(jnp.float32), axis=0)
        value_bias = jnp.sum(mixed_grad_low[:, 2 * model :].astype(jnp.float32), axis=0)
        in_matrix_grad = jnp.einsum(
            "td,tm->dm", stream_low, mixed_grad_low, preferred_element_type=jnp.float32
        )
        grad = first_grad + jnp.einsum(
            "tm,dm->td", mixed_grad_low, in_weight[layer], preferred_element_type=jnp.float32
        )
        collected[layer] = (
            in_matrix_grad,
            out_matrix_grad,
            up_matrix_grad,
            down_matrix_grad,
            jnp.stack([gain_one, gain_two]),
            jnp.stack([query_bias, value_bias, out_bias, up_bias, down_bias, shift_one, shift_two]),
        )
    in_stack = jnp.stack([collected[layer][0] for layer in range(LAYERS)])
    out_stack = jnp.stack([collected[layer][1] for layer in range(LAYERS)])
    up_stack = jnp.stack([collected[layer][2] for layer in range(LAYERS)])
    down_stack = jnp.stack([collected[layer][3] for layer in range(LAYERS)])
    gains_stack = jnp.stack([collected[layer][4] for layer in range(LAYERS)])
    biases_stack = jnp.stack([collected[layer][5] for layer in range(LAYERS)])
    in_total, out_total, up_total, down_total, gains_total, biases_total = lax.psum(
        (in_stack, out_stack, up_stack, down_stack, gains_stack, biases_stack), ("dp", "seq")
    )
    stream_rms = jnp.sqrt(square_total / (count_total * model))
    return (
        layer_output,
        grad[None],
        in_total,
        out_total,
        up_total,
        down_total,
        gains_total,
        biases_total,
        stream_rms,
    )


MESH = pl.DeviceIdType.MESH
LOW = jnp.bfloat16
F32 = jnp.float32
SMALL_ROWS = 32
SCALE = 1.0 / math.sqrt(HEAD_DIM)


def nn(left, right):
    return lax.dot_general(left, right, (((1,), (0,)), ((), ())), preferred_element_type=F32)


def nt(left, right):
    return lax.dot_general(left, right, (((1,), (1,)), ((), ())), preferred_element_type=F32)


def tn(left, right):
    return lax.dot_general(left, right, (((0,), (0,)), ((), ())), preferred_element_type=F32)


def column_sum(value):
    return jnp.sum(value.astype(F32), axis=0, keepdims=True)


def pad_head(rows, which):
    blank = jnp.zeros_like(rows)
    return jnp.concatenate([rows, blank] if which == 0 else [blank, rows], axis=0)


class Sems:
    def __init__(self, send, recv, near):
        self.send, self.recv, self.near = send, recv, near
        self.far_used = self.near_used = 0
        self.spare = []

    def take_set(self):
        if self.spare:
            return self.spare.pop(0)
        first = self.far_used
        self.far_used += SET
        return first

    def far(self, src, dst, device, index=None):
        if index is None:
            index = self.far_used
            self.far_used += 1
        return pltpu.make_async_remote_copy(
            src_ref=src,
            dst_ref=dst,
            send_sem=self.send.at[index],
            recv_sem=self.recv.at[index],
            device_id=device,
            device_id_type=MESH,
        )

    def local(self, src, dst):
        index = self.near_used
        self.near_used += 1
        return pltpu.make_async_copy(src, dst, self.near.at[index])


class Clock:
    QUEUE = 3.0

    def __init__(self):
        self.now = 0.0
        self.free = {"core": 0.0, "x": 0.0, "y": 0.0, "z": 0.0}

    def transfer(self, loads):
        end = 0.0
        for link, load in loads.items():
            begin = max(self.free[link], self.now)
            self.free[link] = begin + load
            end = max(end, self.free[link] + (0.9 if link == "core" else 2.3))
        return end

    def opens(self, loads):
        return max([self.free[link] - self.QUEUE for link in loads], default=0.0)


SET = 16
FAR_SEMS = 183
NEAR_SEMS = 40


def fused_kernel(
    levels,
    tok_ref,
    starts_ref,
    flags_ref,
    valid_ref,
    win_hbm,
    wout_hbm,
    wup_hbm,
    wdn_hbm,
    gains_ref,
    biases_ref,
    og_hbm,
    lo_hbm,
    ig_hbm,
    gin_hbm,
    gout_hbm,
    gup_hbm,
    gdn_hbm,
    small_ref,
    kept_hbm,
    win,
    wout,
    wup,
    wdn,
    low,
    outer,
    keys,
    values,
    turned,
    query_t,
    weights_t,
    attended_t,
    attended_low,
    inverse_total,
    normed_one,
    normed_two,
    inverse_norm,
    hidden_low,
    active_low,
    slope_low,
    scores,
    mask,
    flow,
    query_grad_t,
    give_t,
    take_t,
    meta,
    meta_sent,
    small,
    small_in,
    small_z,
    *rest,
):
    square_sum, wide_sum = rest[:8], rest[8:16]
    send_sems, recv_sems, near_sems = rest[16:]
    rows, model = low.shape[1], low.shape[2]
    length = 2 * rows
    pairs = HEADS // 2
    d = lax.axis_index("dp")
    x = lax.axis_index("seq")
    core = lax.rem(d, 2)
    y = lax.rem(lax.div(d, 2), 2)
    z = lax.div(d, 4)
    to_core = (d + 1 - 2 * core, x)
    to_x = (d, 1 - x)
    to_y = (d + 2 - 4 * y, x)
    to_diag = (d + 1 - 2 * core, 1 - x)

    def at_z(level):
        return (d + (level - z) * 4, x)

    z_next = [lax.rem(z + step, levels) for step in range(1, levels)]
    sems = Sems(send_sems, recv_sems, near_sems)
    barrier = pltpu.get_barrier_semaphore()
    peers = [to_core, to_x, to_y, to_diag] + [at_z(level) for level in z_next]
    for peer in peers:
        pl.semaphore_signal(barrier, inc=1, device_id=peer, device_id_type=MESH)

    def load(pairs_of):
        copies = [sems.local(src, dst) for src, dst in pairs_of]
        for copy in copies:
            copy.start()
        return copies

    moved = core != x
    away_low = sems.far(tok_ref.at[0], low.at[0], to_diag)
    away_outer = sems.far(og_hbm.at[0], outer, to_diag)
    away_meta = sems.far(meta_sent, meta, to_diag)
    stay_low = sems.local(tok_ref.at[0], low.at[0])
    stay_outer = sems.local(og_hbm.at[0], outer)

    position = lax.broadcasted_iota(jnp.int32, (1, length), 1)
    segment = jnp.zeros((1, length), jnp.int32) - 1
    for cell in range(starts_ref.shape[1]):
        segment = segment + (position >= starts_ref[0:1, cell : cell + 1]).astype(jnp.int32)
    good = valid_ref[...] * (1 - flags_ref[...]) > 0
    meta_sent[...] = jnp.zeros_like(meta_sent)
    meta_sent[0:1, :] = jnp.where(good, segment, -1).astype(F32)
    meta_sent[1:2, :] = segment.astype(F32)
    meta_sent[2:3, :] = valid_ref[...].astype(F32)

    pl.semaphore_wait(barrier, len(peers))

    @pl.when(moved)
    def _():
        away_meta.start()
        away_low.start()

    @pl.when(jnp.logical_not(moved))
    def _():
        stay_low.start()
        meta[...] = meta_sent[...]

    weight_loads = []
    for layer in range(LAYERS):
        weight_loads.append(
            [
                load([(win_hbm.at[layer], win.at[layer])])[0],
                load([(wout_hbm.at[layer], wout.at[layer])])[0],
                load([(wup_hbm.at[layer], wup.at[layer])])[0],
                load([(wdn_hbm.at[layer], wdn.at[layer])])[0],
            ]
        )

    small[...] = jnp.zeros_like(small)

    @pl.when(moved)
    def _():
        away_meta.wait()

    near = meta[:, pl.ds(pl.multiple_of(core * rows, 128), rows)]
    far = meta[:, pl.ds(pl.multiple_of((1 - core) * rows, 128), rows)]
    near_t, far_t = near.T, far.T
    same = lax.broadcasted_iota(jnp.int32, (rows, rows), 0) == lax.broadcasted_iota(
        jnp.int32, (rows, rows), 1
    )
    mask[0:rows, :] = jnp.where((near_t[:, 0:1] == near[1:2, :]) | same, 0.0, NEG)
    mask[rows:length, :] = jnp.where(far_t[:, 0:1] == near[1:2, :], 0.0, NEG)
    valid_column = near_t[:, 2:3]
    small[0, 24:25, :] = near[2:3, :]

    @pl.when(moved)
    def _():
        away_low.wait()
        away_outer.start()

    @pl.when(jnp.logical_not(moved))
    def _():
        stay_low.wait()
        stay_outer.start()

    def note_square(layer, which, value):
        row = 18 + 3 * layer + which
        small[0, row : row + 1, :] = column_sum(value * value * valid_column)

    staged = square_sum[0].at[3 * LAYERS - 1]
    spills = []
    flow[...] = low[0].astype(F32)
    for layer in range(LAYERS):
        bias = [biases_ref[k, layer : layer + 1, :] for k in range(7)]
        gain = [gains_ref[layer, k : k + 1, :] for k in range(2)]
        load_in, load_out, load_up, load_down = weight_loads[layer]
        load_in.wait()
        stream_low = low[layer]
        note_square(layer, 0, flow[...])
        keys[layer, 0:rows, :] = nn(stream_low, win[layer, :, model : 2 * model]).astype(LOW)
        send_keys = sems.far(
            keys.at[layer, pl.ds(0, rows)], keys.at[layer, pl.ds(rows, rows)], to_core
        )
        send_keys.start()
        values[layer, 0:rows, :] = (
            nn(stream_low, win[layer, :, 2 * model : 3 * model]) + bias[1]
        ).astype(LOW)
        send_values = sems.far(
            values.at[layer, pl.ds(0, rows)], values.at[layer, pl.ds(rows, rows)], to_core
        )
        send_values.start()
        query = nn(stream_low, win[layer, :, 0:model]) + bias[0]
        query_t[layer] = (query * (SCALE / math.log(2.0))).T.astype(LOW)
        turned[:, 0:rows] = values[layer, 0:rows, :].T
        send_keys.wait()

        def score(head, layer=layer):
            pair = head // 2
            scores[head % 2] = (
                nn(
                    keys[layer, :, 128 * pair : 128 * pair + 128],
                    pad_head(query_t[layer, 64 * head : 64 * head + 64, :], head % 2),
                )
                + mask[...]
            )

        score(0)
        for head in range(HEADS):
            if head + 1 < HEADS:
                score(head + 1)
            if head == 0:
                send_values.wait()
                turned[:, rows:length] = values[layer, rows:length, :].T
            if layer > 0:
                spills[layer - 1][head].wait()
            block = scores[head % 2]
            best = jnp.max(block, axis=0, keepdims=True)
            weight = jnp.exp2(block - best)
            inverse = 1.0 / jnp.sum(weight, axis=0, keepdims=True)
            weight_low = weight.astype(LOW)
            weights_t[head] = weight_low
            span = slice(64 * head, 64 * head + 64)
            inverse_total[layer, head : head + 1, :] = inverse
            attended_t[layer, span, :] = nn(turned[span, :], weight_low) * inverse
            if layer + 1 < LAYERS:
                if head == 0:
                    spills.append([])
                copy = sems.local(weights_t.at[head], kept_hbm.at[layer, head])
                copy.start()
                spills[layer].append(copy)
        attended_low[layer] = attended_t[layer].T.astype(LOW)
        load_out.wait()
        branch = nn(attended_low[layer], wout[layer]) + bias[2]
        note_square(layer, 1, branch)
        total = flow[...] + branch
        centred = total - jnp.mean(total, axis=-1, keepdims=True)
        inverse = lax.rsqrt(jnp.mean(centred * centred, axis=-1, keepdims=True) + EPS)
        normed = centred * inverse
        normed_one[layer] = normed.astype(LOW)
        inverse_norm[:, 2 * layer : 2 * layer + 1] = inverse
        hidden = normed * gain[0] + bias[5]
        flow[...] = hidden
        hidden_low[layer] = hidden.astype(LOW)
        load_up.wait()
        inner = nn(hidden_low[layer], wup[layer]) + bias[3]
        share = 0.5 * (1.0 + lax.erf(inner * 0.7071067811865476))
        active_low[layer] = (inner * share).astype(LOW)
        slope_low[layer] = (
            share + inner * jnp.exp(-0.5 * inner * inner) * 0.3989422804014327
        ).astype(LOW)
        load_down.wait()
        ff_out = nn(active_low[layer], wdn[layer]) + bias[4]
        note_square(layer, 2, ff_out)
        total = flow[...] + ff_out
        centred = total - jnp.mean(total, axis=-1, keepdims=True)
        inverse = lax.rsqrt(jnp.mean(centred * centred, axis=-1, keepdims=True) + EPS)
        normed = centred * inverse
        normed_two[layer] = normed.astype(LOW)
        inverse_norm[:, 2 * layer + 1 : 2 * layer + 2] = inverse
        result = normed * gain[1] + bias[6]
        if layer + 1 < LAYERS:
            flow[...] = result
            low[layer + 1] = result.astype(LOW)
        else:
            staged[...] = result.astype(LOW).reshape(staged.shape)

    away_result = sems.far(staged, lo_hbm, to_diag)
    stay_result = sems.local(staged, lo_hbm)
    away_grad = sems.far(outer, ig_hbm.at[0], to_diag)
    stay_grad = sems.local(outer, ig_hbm.at[0])

    @pl.when(moved)
    def _():
        away_outer.wait()
        away_result.start()

    @pl.when(jnp.logical_not(moved))
    def _():
        stay_outer.wait()
        stay_result.start()

    piece = model // 8 // levels
    own_rows = pl.ds(pl.multiple_of(z * piece, piece), piece)
    clock = Clock()
    clock.free["x"] = 5.8

    def reduce_chunk(buffers, begin, count, homes):
        return loads_of(buffers, count), steps_of(buffers, begin, count, homes)

    def share_of(width):
        return width // 256 * 128

    def loads_of(buffers, count):
        width = buffers[0].shape[-1]
        size = count * width / model
        part = share_of(width) / width
        first = {"x": 2.88 * part * size, "y": 2.88 * (1 - part) * size}
        second = {"x": 1.44 * (1 - part) * size, "y": 1.44 * part * size}
        core_load, z_load = {"core": 0.46 * size}, {"z": 1.35 * size}
        return [core_load, first, second, z_load, z_load, second, first, core_load]

    def steps_of(buffers, begin, count, homes):
        mine, whole, take_core, take_x, take_y, take_ay, take_bx, take_z = buffers
        width = mine.shape[-1]
        some = pl.ds(begin, count)
        landed = pl.ds(begin % take_core.shape[0], count)
        split = share_of(width)
        left, right = pl.ds(0, split), pl.ds(split, width - split)
        every = slice(None)
        first = sems.take_set()
        used = [0]

        def send(src, dst, peer):
            copy = sems.far(src, dst, peer, first + used[0])
            used[0] += 1
            copy.start()
            return copy

        def send_same(at, peer):
            return send(whole.at[at], whole.at[at], peer)

        def add_into(at, value):
            mine[at] = mine[at] + value

        def finish(copies):
            for copy in copies:
                copy.wait()

        mine_core, mine_left, mine_right = (
            (some, core),
            (some, core, x, every, every, left),
            (some, core, every, y, every, right),
        )
        deep_left, deep_right = (some, core, x, y, every, left), (some, core, x, y, every, right)
        own = (some, core, x, y, own_rows)

        flight = [send(mine.at[some, 1 - core], take_core.at[landed], to_core)]
        yield
        finish(flight)
        add_into(mine_core, take_core[landed])
        flight = [
            send(mine.at[some, core, 1 - x, every, every, left], take_x.at[some], to_x),
            send(mine.at[some, core, every, 1 - y, every, right], take_y.at[some], to_y),
        ]
        yield
        finish(flight)
        add_into(mine_left, take_x[some])
        add_into(mine_right, take_y[some])
        flight = [
            send(mine.at[some, core, x, 1 - y, every, left], take_ay.at[some], to_y),
            send(mine.at[some, core, 1 - x, y, every, right], take_bx.at[some], to_x),
        ]
        yield
        finish(flight)
        add_into(deep_left, take_ay[some])
        add_into(deep_right, take_bx[some])
        flight = [
            send(
                mine.at[some, core, x, y, pl.ds(pl.multiple_of(level * piece, piece), piece)],
                take_z.at[step, some],
                at_z(level),
            )
            for step, level in enumerate(z_next)
        ]
        yield
        finish(flight)
        total = mine[own].astype(F32)
        for step in range(levels - 1):
            total = total + take_z[step, some].astype(F32)
        whole[own] = total.astype(LOW)
        flight = [send_same(own, at_z(level)) for level in z_next]
        yield
        finish(flight)
        flight = [send_same(deep_left, to_y), send_same(deep_right, to_x)]
        yield
        finish(flight)
        flight = [send_same(mine_left, to_x), send_same(mine_right, to_y)]
        yield
        finish(flight)
        flight = [send_same(mine_core, to_core)]
        yield
        finish(flight)
        sems.spare.append(first)
        for src, dst in homes:
            copy = sems.local(src, dst)
            copy.start()
            homing.append(copy)

    def reduce_small():
        for step, peer in enumerate((to_core, to_x, to_y)):
            copy = sems.far(small.at[step], small_in.at[step], peer)
            copy.start()
            yield
            copy.wait()
            small[step + 1] = small[step] + small_in[step]
        copies = [sems.far(small.at[3], small_z.at[z], at_z(level)) for level in z_next]
        for copy in copies:
            copy.start()
        small_z[z] = small[3]
        yield
        for copy in copies:
            copy.wait()
        total = small_z[0]
        for level in range(1, levels):
            total = total + small_z[level]
        small_ref[...] = total

    homing = []
    active = []

    def advance(entry):
        loads = entry[2]
        if next(entry[1], True):
            active.remove(entry)
            clock.now += 0.1
        else:
            clock.now += 0.25
            entry[0] = clock.transfer(loads.pop(0))

    def begin(chunk):
        loads, steps = chunk
        entry = [0.0, steps, loads]
        active.append(entry)
        advance(entry)

    def when(entry):
        return max(entry[0], clock.opens(entry[2][0] if entry[2] else {}))

    def pump(spent):
        clock.now += spent
        while True:
            ready = [entry for entry in active if when(entry) <= clock.now]
            if not ready:
                return
            advance(max(ready, key=lambda entry: len(entry[2])))

    def note(row, value):
        small[0, row : row + 1, :] = value

    reloads = []
    flow[...] = outer[...].astype(F32)
    for layer in reversed(range(LAYERS)):
        gain = [gains_ref[layer, k : k + 1, :] for k in range(2)]
        base = 3 * (LAYERS - 1 - layer)
        wide = pairs * (LAYERS - 1 - layer)
        mine, whole = square_sum[:2]
        folded = mine.shape[1:]
        bias_row = 4 + 7 * layer
        grad = flow[...]
        normed = normed_two[layer].astype(F32)
        note(2 * layer + 1, column_sum(grad * normed))
        note(bias_row + 6, column_sum(grad))
        scaled = grad * gain[1]
        second = inverse_norm[:, 2 * layer + 1 : 2 * layer + 2] * (
            scaled
            - jnp.mean(scaled, axis=-1, keepdims=True)
            - normed * jnp.mean(scaled * normed, axis=-1, keepdims=True)
        )
        scores[0, 0:rows, :] = second
        down_low = second.astype(LOW)
        note(bias_row + 4, column_sum(down_low))
        mine[base] = tn(active_low[layer], down_low).astype(LOW).reshape(folded)
        inner_low = (nt(down_low, wdn[layer]) * slope_low[layer].astype(F32)).astype(LOW)
        note(bias_row + 3, column_sum(inner_low))
        mine[base + 1] = tn(hidden_low[layer], inner_low).astype(LOW).reshape(folded)
        pump(2.6)
        begin(
            reduce_chunk(
                square_sum,
                base,
                2,
                [
                    (whole.at[base], gdn_hbm.at[layer]),
                    (whole.at[base + 1], gup_hbm.at[layer]),
                ],
            )
        )
        grad = scores[0, 0:rows, :] + nt(inner_low, wup[layer])
        normed = normed_one[layer].astype(F32)
        note(2 * layer, column_sum(grad * normed))
        note(bias_row + 5, column_sum(grad))
        scaled = grad * gain[0]
        flow[...] = inverse_norm[:, 2 * layer : 2 * layer + 1] * (
            scaled
            - jnp.mean(scaled, axis=-1, keepdims=True)
            - normed * jnp.mean(scaled * normed, axis=-1, keepdims=True)
        )
        branch_low = flow[...].astype(LOW)
        note(bias_row + 2, column_sum(branch_low))
        mine[base + 2] = tn(attended_low[layer], branch_low).astype(LOW).reshape(folded)
        pump(1.2)
        begin(
            reduce_chunk(square_sum, base + 2, 1, [(whole.at[base + 2], gout_hbm.at[layer])])
        )
        attended_grad_t = nt(branch_low, wout[layer]).astype(LOW).T
        turned[:, 0:rows] = keys[layer, 0:rows, :].T
        turned[:, rows:length] = keys[layer, rows:length, :].T
        pump(1.0)
        gives = []

        def close_pairs(chosen, layer=layer, wide=wide, bias_row=bias_row, gives=gives):
            mine, whole = wide_sum[:2]
            parts = []
            for pair in chosen:
                side = slice(128 * pair, 128 * pair + 128)
                gives[pair].wait()
                taken = [take_t[layer, pair, which].astype(F32) for which in range(2)]
                values_side = slice(model + side.start, model + side.stop)
                three = [
                    query_grad_t[side, :].T,
                    (mask[side, :] + taken[0]).astype(LOW).T,
                    (mask[values_side, :] + taken[1]).astype(LOW).T,
                ]
                small[0, bias_row : bias_row + 1, side] = column_sum(three[0])
                small[0, bias_row + 1 : bias_row + 2, side] = column_sum(three[2])
                parts += three
            part = jnp.concatenate(parts, axis=1)
            product = tn(low[layer], part).astype(LOW)
            homes = []
            for k, pair in enumerate(chosen):
                slot = wide + pair
                mine[slot] = product[:, 384 * k : 384 * k + 384].reshape(mine.shape[1:])
            first, count = wide + chosen[0], len(chosen)
            homes = [
                (whole.at[pl.ds(first, count)], gin_hbm.at[layer, pl.ds(chosen[0], count)])
            ]
            pump(0.4 * count)
            begin(reduce_chunk(wide_sum, first, count, homes))
            weight = jnp.concatenate(
                [
                    win[layer, :, model * k + 128 * pair : model * k + 128 * pair + 128]
                    for pair in chosen
                    for k in range(3)
                ],
                axis=1,
            )
            total = flow[...] + nt(part, weight)
            if layer > 0 or chosen[-1] < pairs - 1:
                flow[...] = total
            else:
                outer[...] = total.astype(LOW)

        for head in range(HEADS):
            pair = head // 2
            span = slice(64 * head, 64 * head + 64)
            lanes = slice(128 * pair, 128 * pair + 128)
            grad_low = (
                attended_grad_t[span, :].astype(F32) * inverse_total[layer, head : head + 1, :]
            ).astype(LOW)
            delta = column_sum(grad_low.astype(F32) * attended_t[layer, span, :])
            if layer + 1 < LAYERS:
                reloads[head].wait()
            weight_low = weights_t[head]
            prob_grad = nn(values[layer, :, lanes], pad_head(grad_low, head % 2))
            score_grad = (weight_low.astype(F32) * (prob_grad - delta)).astype(LOW)
            query_grad_t[span, :] = (
                nn(turned[span, :], score_grad) * SCALE
            ).astype(LOW)
            key_grad = nt(query_t[layer, span, :], score_grad) * math.log(2.0)
            value_grad = nt(grad_low, weight_low)
            inside = slice(64 * (head % 2), 64 * (head % 2) + 64)
            mask[span, :] = key_grad[:, 0:rows]
            mask[64 * head + model : 64 * head + model + 64, :] = value_grad[:, 0:rows]
            give_t[pair, 0, inside, :] = key_grad[:, rows:length].astype(LOW)
            give_t[pair, 1, inside, :] = value_grad[:, rows:length].astype(LOW)
            if layer > 0:
                copy = sems.local(kept_hbm.at[layer - 1, head], weights_t.at[head])
                copy.start()
                reloads.append(copy)
            if head % 2 == 1:
                copy = sems.far(give_t.at[pair], take_t.at[layer, pair], to_core)
                copy.start()
                gives.append(copy)
            pump(1.15)
            if layer > 0 and head == HEADS // 2:
                close_pairs([0, 1])
            if layer == 0 and head % 2 == 0 and head > 0:
                close_pairs([pair - 1])
        close_pairs([2, 3] if layer > 0 else [3])
        if layer == 0:
            begin(([{"core": 0.1}, {"x": 1.5}, {"y": 1.5}, {"z": 2.0}], reduce_small()))
        if layer > 0:

            @pl.when(moved)
            def _():
                away_result.wait()

            @pl.when(jnp.logical_not(moved))
            def _():
                stay_result.wait()

        pump(0.4)

    @pl.when(moved)
    def _():
        away_grad.start()

    @pl.when(jnp.logical_not(moved))
    def _():
        stay_grad.start()

    clock.free["x"] = max(clock.free["x"], clock.now) + 5.8
    while active:
        clock.now = max(clock.now, min(when(entry) for entry in active))
        pump(0.0)
    for copy in homing:
        copy.wait()

    @pl.when(moved)
    def _():
        away_grad.wait()

    @pl.when(jnp.logical_not(moved))
    def _():
        stay_grad.wait()

    assert sems.far_used <= FAR_SEMS and sems.near_used <= NEAR_SEMS


def local_pair(
    tokens,
    cell_starts,
    generate_flags,
    valid_mask,
    in_weight,
    out_weight,
    up_weight,
    down_weight,
    norm_gains,
    biases,
    out_grad,
):
    rows, model = tokens.shape[1:]
    length = 2 * rows
    levels = lax.axis_size("dp") // 4
    eighth = model // 8
    folded = (2, 2, 2, eighth)

    def sum_buffers(count, shared, width):
        split = width // 256 * 128
        return [
            pltpu.VMEM((count,) + folded + (width,), LOW),
            pltpu.VMEM((count,) + folded + (width,), LOW),
            pltpu.VMEM((shared,) + folded[1:] + (width,), LOW),
            pltpu.VMEM((count, 2, eighth, split), LOW),
            pltpu.VMEM((count, 2, eighth, width - split), LOW),
            pltpu.VMEM((count, eighth, split), LOW),
            pltpu.VMEM((count, eighth, width - split), LOW),
            pltpu.VMEM((max(levels - 1, 1), count, eighth // levels, width), LOW),
        ]

    shape = jax.ShapeDtypeStruct
    vmem, anywhere = pl.BlockSpec(memory_space=pltpu.VMEM), pl.BlockSpec(memory_space=pl.ANY)
    by_layer = (LAYERS, rows, model)
    scratch = [
        pltpu.VMEM(in_weight.shape, LOW),
        pltpu.VMEM(out_weight.shape, LOW),
        pltpu.VMEM(up_weight.shape, LOW),
        pltpu.VMEM(down_weight.shape, LOW),
        pltpu.VMEM(by_layer, LOW),
        pltpu.VMEM((rows, model), LOW),
        pltpu.VMEM((LAYERS, length, model), LOW),
        pltpu.VMEM((LAYERS, length, model), LOW),
        pltpu.VMEM((model, length), LOW),
        pltpu.VMEM((LAYERS, model, rows), LOW),
        pltpu.VMEM((HEADS, length, rows), LOW),
        pltpu.VMEM((LAYERS, model, rows), F32),
        pltpu.VMEM(by_layer, LOW),
        pltpu.VMEM((LAYERS, HEADS, rows), F32),
        pltpu.VMEM(by_layer, LOW),
        pltpu.VMEM(by_layer, LOW),
        pltpu.VMEM((rows, 2 * LAYERS), F32),
        pltpu.VMEM(by_layer, LOW),
        pltpu.VMEM(by_layer, LOW),
        pltpu.VMEM(by_layer, LOW),
        pltpu.VMEM((2, length, rows), F32),
        pltpu.VMEM((length, rows), F32),
        pltpu.VMEM((rows, model), F32),
        pltpu.VMEM((model, rows), LOW),
        pltpu.VMEM((HEADS // 2, 2, 128, rows), LOW),
        pltpu.VMEM((LAYERS, HEADS // 2, 2, 128, rows), LOW),
        pltpu.VMEM((8, length), F32),
        pltpu.VMEM((8, length), F32),
        pltpu.VMEM((4, SMALL_ROWS, model), F32),
        pltpu.VMEM((3, SMALL_ROWS, model), F32),
        pltpu.VMEM((levels, SMALL_ROWS, model), F32),
        *sum_buffers(3 * LAYERS, 3, model),
        *sum_buffers(HEADS // 2 * LAYERS, HEADS // 2, 384),
        pltpu.SemaphoreType.DMA((FAR_SEMS,)),
        pltpu.SemaphoreType.DMA((FAR_SEMS,)),
        pltpu.SemaphoreType.DMA((NEAR_SEMS,)),
    ]
    lo, ig, gin, gout, gup, gdn, small, _ = pl.pallas_call(
        functools.partial(fused_kernel, levels),
        out_shape=[
            shape(folded + (model,), LOW),
            shape(tokens.shape, LOW),
            shape((LAYERS, HEADS // 2) + folded + (384,), LOW),
            shape((LAYERS,) + folded + (model,), LOW),
            shape((LAYERS,) + folded + (model,), LOW),
            shape((LAYERS,) + folded + (model,), LOW),
            shape((SMALL_ROWS, model), F32),
            shape((LAYERS - 1, HEADS, length, rows), LOW),
        ],
        in_specs=[anywhere, vmem, vmem, vmem] + [anywhere] * 4 + [vmem, vmem, anywhere],
        out_specs=[anywhere] * 6 + [vmem, anywhere],
        scratch_shapes=scratch,
        compiler_params=pltpu.CompilerParams(
            collective_id=0, has_side_effects=True, vmem_limit_bytes=VMEM_BYTES
        ),
    )(
        tokens,
        cell_starts,
        generate_flags,
        valid_mask,
        in_weight,
        out_weight,
        up_weight,
        down_weight,
        norm_gains,
        biases.transpose(1, 0, 2),
        out_grad,
    )
    return finish(tokens, in_weight, lo, ig, gin, gout, gup, gdn, small)


VMEM_BYTES = 63 * 1024 * 1024


def finish_kernel(model, *refs):
    lo_in, ig_in, gin_in, gout_in, gup_in, gdn_in, small = refs[:7]
    lo, ig, gin, gout, gup, gdn, gains, shifts, rms = refs[7:16]
    low_wide, wide, low_square, square, passing, wide_sems, in_sems, out_sems = refs[16:]
    pieces = [(lo_in, passing, passing, lo)]
    pairs = gin_in.shape[1]
    spread = []
    for layer in reversed(range(LAYERS)):
        for pair in range(pairs):
            slot = pairs * layer + pair
            spread.append(
                pltpu.make_async_copy(gin_in.at[layer, pair], low_wide.at[slot], wide_sems.at[slot])
            )
            spread[-1].start()
    count = 0
    for source, target in ((gout_in, gout), (gup_in, gup), (gdn_in, gdn), (ig_in, ig)):
        for index in range(source.shape[0]):
            pieces.append(
                (source.at[index], low_square.at[count], square.at[count], target.at[index])
            )
            count += 1
    reads = [
        pltpu.make_async_copy(piece[0], piece[1], in_sems.at[k]) for k, piece in enumerate(pieces)
    ]
    writes = [
        pltpu.make_async_copy(piece[2], piece[3], out_sems.at[k]) for k, piece in enumerate(pieces)
    ]
    for read in reads:
        read.start()
    for layer in range(LAYERS):
        for k in range(2):
            row = 2 * layer + k
            gains[layer, k : k + 1, :] = small[row : row + 1, :]
        for k in range(7):
            row = 2 * LAYERS + 7 * layer + k
            shifts[k, layer : layer + 1, :] = small[row : row + 1, :]
    first = 9 * LAYERS
    count = jnp.sum(small[first + 3 * LAYERS : first + 3 * LAYERS + 1, :], keepdims=True)
    line = lax.broadcasted_iota(jnp.int32, rms.shape, 0)
    place = lax.broadcasted_iota(jnp.int32, rms.shape, 1)
    squares = jnp.zeros(rms.shape, F32)
    for layer in range(LAYERS):
        for k in range(3):
            row = first + 3 * layer + k
            value = jnp.sum(small[row : row + 1, :], keepdims=True)
            squares = jnp.where((line == layer) & (place == k), value, squares)
    rms[...] = jnp.sqrt(squares / (count * model))
    for layer in reversed(range(LAYERS)):
        for pair in range(pairs):
            spread.pop(0).wait()
            for k in range(3):
                begin = model * k + 128 * pair
                wide[layer, :, begin : begin + 128] = low_wide[
                    pairs * layer + pair, :, 128 * k : 128 * k + 128
                ].astype(F32)
        write = pltpu.make_async_copy(
            wide.at[layer], gin.at[layer], out_sems.at[len(pieces) + layer]
        )
        write.start()
        writes.append(write)
    for read, write, piece in zip(reads, writes, pieces):
        read.wait()
        if piece[1] is not piece[2]:
            piece[2][...] = piece[1][...].astype(F32)
        write.start()
    for write in writes:
        write.wait()


def finish(tokens, in_weight, lo, ig, gin, gout, gup, gdn, small):
    rows, model = tokens.shape[1:]
    shape = jax.ShapeDtypeStruct
    vmem, far = pl.BlockSpec(memory_space=pltpu.VMEM), pl.BlockSpec(memory_space=pltpu.HBM)
    square = (LAYERS, model, model)
    slots = LAYERS * HEADS // 2
    outs = pl.pallas_call(
        functools.partial(finish_kernel, model),
        out_shape=[
            shape(tokens.shape, LOW),
            shape(tokens.shape, F32),
            shape(in_weight.shape, F32),
            shape(square, F32),
            shape(square, F32),
            shape(square, F32),
            shape((LAYERS, 2, model), F32),
            shape((7, LAYERS, model), F32),
            shape((LAYERS, 3), F32),
        ],
        in_specs=[far] * 6 + [vmem],
        out_specs=[far] * 6 + [vmem] * 3,
        scratch_shapes=[
            pltpu.VMEM((slots, model, 384), LOW),
            pltpu.VMEM(in_weight.shape, F32),
            pltpu.VMEM((3 * LAYERS + 1, model, model), LOW),
            pltpu.VMEM((3 * LAYERS + 1, model, model), F32),
            pltpu.VMEM(tokens.shape, LOW),
            pltpu.SemaphoreType.DMA((slots,)),
            pltpu.SemaphoreType.DMA((3 * LAYERS + 2,)),
            pltpu.SemaphoreType.DMA((4 * LAYERS + 2,)),
        ],
        compiler_params=pltpu.CompilerParams(vmem_limit_bytes=VMEM_BYTES),
    )(
        lo.reshape(tokens.shape),
        ig,
        gin.reshape(LAYERS, HEADS // 2, model, 384),
        gout.reshape(square),
        gup.reshape(square),
        gdn.reshape(square),
        small,
    )
    lo, ig, gin, gout, gup, gdn, gains, shifts, rms = outs
    return lo, ig, gin, gout, gup, gdn, gains, shifts.transpose(1, 0, 2), rms


def solution(mesh):
    placed = (
        P("dp", "seq", None),
        P("dp", None),
        P("dp", None),
        P("dp", None),
        P(),
        P(),
        P(),
        P(),
        P(),
        P(),
        P("dp", "seq", None),
    )
    paired = mesh.shape["seq"] == 2 and mesh.shape["dp"] % 4 == 0
    return jax.shard_map(
        local_pair if paired else local,
        mesh=mesh,
        in_specs=placed,
        out_specs=(P("dp", "seq", None), P("dp", "seq", None), P(), P(), P(), P(), P(), P(), P()),
        check_vma=False,
    )
```

```python
import functools
import math

import jax
import jax.numpy as jnp
from jax import lax
from jax.experimental import pallas as pl
from jax.experimental.pallas import tpu as pltpu
from jax.sharding import PartitionSpec as P

HEADS = 8
HEAD_DIM = 64
LAYERS = 2


EPS = 1e-05
NEG = -1e30


def block_width(count):
    for option in range(1024, 255, -1):
        if count % option == 0:
            return option
    return count


def segment_ids(starts_row, positions):
    return jnp.sum((positions[:, None] >= starts_row[None, :]).astype(jnp.int32), axis=1) - 1


def norm_rows(total, gain, shift):
    mean = jnp.mean(total, axis=-1, keepdims=True)
    centred = total - mean
    spread = jnp.mean(centred * centred, axis=-1, keepdims=True)
    inverse = lax.rsqrt(spread + EPS)
    normed = centred * inverse
    return (normed * gain + shift, normed, inverse)


def norm_back(grad, normed, inverse, gain):
    scaled = grad * gain
    return inverse * (
        scaled
        - jnp.mean(scaled, axis=-1, keepdims=True)
        - normed * jnp.mean(scaled * normed, axis=-1, keepdims=True)
    )


def gelu_slope(inner):
    return (
        0.5 * (1.0 + jax.scipy.special.erf(inner * 0.7071067811865476))
        + inner * jnp.exp(-0.5 * inner * inner) * 0.3989422804014327
    )


def make_mask(query_pos, query_seg, starts_row, key_ok_row):

    def mask_for(begin, width):
        key_pos = begin + jnp.arange(width, dtype=jnp.int32)
        key_seg = segment_ids(starts_row, key_pos)
        key_good = lax.dynamic_slice_in_dim(key_ok_row, begin, width, 0) > 0
        return (query_seg[:, None] == key_seg[None, :]) & (
            key_good[None, :] | (query_pos[:, None] == key_pos[None, :])
        )

    return mask_for


def make_attend(query_heads, mask_for, scale):

    def attend(carry, piece, start):
        count = piece.shape[0]
        width = block_width(count)
        model = piece.shape[1] // 2

        def attend_one_block(step, state):
            best, total, summed = state
            begin = step * width
            block = lax.dynamic_slice_in_dim(piece, begin, width, 0)
            key_heads = block[:, :model].reshape(width, HEADS, HEAD_DIM)
            value_heads = block[:, model:].reshape(width, HEADS, HEAD_DIM)
            allowed = mask_for(start + begin, width)[None]
            scores = (
                jnp.einsum(
                    "qhd,khd->hqk", query_heads, key_heads, preferred_element_type=jnp.float32
                )
                * scale
            )
            scores = jnp.where(allowed, scores, NEG)
            new_best = jnp.maximum(best, jnp.max(scores, axis=-1))
            factor = jnp.exp(best - new_best)
            weights = jnp.where(allowed, jnp.exp(scores - new_best[:, :, None]), 0.0)
            total = total * factor + jnp.sum(weights, axis=-1)
            update = jnp.einsum(
                "hqk,khd->qhd",
                weights.astype(jnp.bfloat16),
                value_heads,
                preferred_element_type=jnp.float32,
            )
            summed = summed * factor.T[:, :, None] + update
            return (new_best, total, summed)

        return lax.fori_loop(0, count // width, attend_one_block, carry)

    return attend


def make_back(query_heads, grad_heads, log_total, delta, mask_for, scale):

    def back(carry, piece, start):
        count = piece.shape[0]
        width = block_width(count)
        model = piece.shape[1] // 2

        def back_one_block(step, state):
            query_grad, full_grad = state
            begin = step * width
            block = lax.dynamic_slice_in_dim(piece, begin, width, 0)
            key_heads = block[:, :model].reshape(width, HEADS, HEAD_DIM)
            value_heads = block[:, model:].reshape(width, HEADS, HEAD_DIM)
            allowed = mask_for(start + begin, width)[None]
            scores = (
                jnp.einsum(
                    "qhd,khd->hqk", query_heads, key_heads, preferred_element_type=jnp.float32
                )
                * scale
            )
            probs = jnp.where(allowed, jnp.exp(scores - log_total[:, :, None]), 0.0)
            prob_grad = jnp.einsum(
                "qhd,khd->hqk", grad_heads, value_heads, preferred_element_type=jnp.float32
            )
            score_grad = (probs * (prob_grad - delta[:, :, None])).astype(jnp.bfloat16)
            query_grad = (
                query_grad
                + jnp.einsum(
                    "hqk,khd->qhd", score_grad, key_heads, preferred_element_type=jnp.float32
                )
                * scale
            )
            key_grad = (
                jnp.einsum(
                    "hqk,qhd->khd", score_grad, query_heads, preferred_element_type=jnp.float32
                )
                * scale
            )
            value_grad = jnp.einsum(
                "hqk,qhd->khd",
                probs.astype(jnp.bfloat16),
                grad_heads,
                preferred_element_type=jnp.float32,
            )
            update = jnp.concatenate(
                [key_grad.reshape(width, model), value_grad.reshape(width, model)], axis=1
            )
            place = start + begin
            current = lax.dynamic_slice_in_dim(full_grad, place, width, 0)
            full_grad = lax.dynamic_update_slice_in_dim(full_grad, current + update, place, 0)
            return (query_grad, full_grad)

        return lax.fori_loop(0, count // width, back_one_block, carry)

    return back


def local(
    tokens,
    cell_starts,
    generate_flags,
    valid_mask,
    in_weight,
    out_weight,
    up_weight,
    down_weight,
    norm_gains,
    biases,
    out_grad,
):
    rows = tokens.shape[1]
    model = tokens.shape[2]
    scale = 1.0 / math.sqrt(HEAD_DIM)
    first = lax.axis_index("seq") * rows
    query_pos = first + jnp.arange(rows, dtype=jnp.int32)
    starts_row = cell_starts[0]
    key_ok_row = valid_mask[0] * (1 - generate_flags[0])
    mask_for = make_mask(query_pos, segment_ids(starts_row, query_pos), starts_row, key_ok_row)
    valid_here = lax.dynamic_slice_in_dim(valid_mask[0], first, rows, 0).astype(jnp.float32)
    stream = tokens[0].astype(jnp.float32)
    stream_low = tokens[0]
    kept = []
    squares = []
    for layer in range(LAYERS):
        bias_rows = biases[layer]
        gains_pair = norm_gains[layer]
        mixed = jnp.dot(
            stream_low, in_weight[layer], preferred_element_type=jnp.float32
        ) + jnp.concatenate([bias_rows[0], jnp.zeros((model,), jnp.float32), bias_rows[1]])
        mixed_low = mixed.astype(jnp.bfloat16)
        query_heads = mixed_low[:, :model].reshape(rows, HEADS, HEAD_DIM)
        key_value = mixed_low[:, model:]
        attend = make_attend(query_heads, mask_for, scale)
        state = (
            jnp.full((HEADS, rows), NEG, jnp.float32),
            jnp.zeros((HEADS, rows), jnp.float32),
            jnp.zeros((rows, HEADS, HEAD_DIM), jnp.float32),
        )
        gathered = key_value
        best, total, summed = attend(
            state, lax.all_gather(key_value, "seq", axis=0, tiled=True), jnp.int32(0)
        )
        attended = (summed / total.T[:, :, None]).reshape(rows, model)
        log_total = best + jnp.log(total)
        attended_low = attended.astype(jnp.bfloat16)
        branch = (
            jnp.dot(attended_low, out_weight[layer], preferred_element_type=jnp.float32)
            + bias_rows[2]
        )
        hidden, normed_one, inverse_one = norm_rows(stream + branch, gains_pair[0], bias_rows[5])
        hidden_low = hidden.astype(jnp.bfloat16)
        inner = (
            jnp.dot(hidden_low, up_weight[layer], preferred_element_type=jnp.float32) + bias_rows[3]
        )
        active_low = jax.nn.gelu(inner, approximate=False).astype(jnp.bfloat16)
        ff_out = (
            jnp.dot(active_low, down_weight[layer], preferred_element_type=jnp.float32)
            + bias_rows[4]
        )
        result, normed_two, inverse_two = norm_rows(hidden + ff_out, gains_pair[1], bias_rows[6])
        squares.append(
            jnp.stack(
                [
                    jnp.sum(valid_here * jnp.sum(part * part, axis=-1))
                    for part in (stream, branch, ff_out)
                ]
            )
        )
        kept.append(
            (
                stream_low,
                query_heads,
                gathered,
                attended,
                attended_low,
                log_total,
                normed_one,
                inverse_one,
                hidden_low,
                inner,
                active_low,
                normed_two,
                inverse_two,
            )
        )
        stream = result
        stream_low = result.astype(jnp.bfloat16)
    layer_output = stream.astype(jnp.bfloat16)[None]
    square_local = jnp.stack(squares)
    count_local = jnp.sum(valid_here)
    square_total, count_total = lax.psum((square_local, count_local), ("dp", "seq"))
    grad = out_grad[0].astype(jnp.float32)
    length = rows * lax.axis_size("seq")
    collected = [None] * LAYERS
    for layer in reversed(range(LAYERS)):
        (
            stream_low,
            query_heads,
            gathered,
            attended,
            attended_low,
            log_total,
            normed_one,
            inverse_one,
            hidden_low,
            inner,
            active_low,
            normed_two,
            inverse_two,
        ) = kept[layer]
        gains_pair = norm_gains[layer]
        gain_two = jnp.sum(grad * normed_two, axis=0)
        shift_two = jnp.sum(grad, axis=0)
        second_grad = norm_back(grad, normed_two, inverse_two, gains_pair[1])
        down_grad_low = second_grad.astype(jnp.bfloat16)
        down_bias = jnp.sum(down_grad_low.astype(jnp.float32), axis=0)
        down_matrix_grad = jnp.einsum(
            "tf,td->fd", active_low, down_grad_low, preferred_element_type=jnp.float32
        )
        active_grad = jnp.einsum(
            "td,fd->tf", down_grad_low, down_weight[layer], preferred_element_type=jnp.float32
        )
        inner_grad_low = (active_grad * gelu_slope(inner)).astype(jnp.bfloat16)
        up_bias = jnp.sum(inner_grad_low.astype(jnp.float32), axis=0)
        up_matrix_grad = jnp.einsum(
            "td,tf->df", hidden_low, inner_grad_low, preferred_element_type=jnp.float32
        )
        hidden_grad = second_grad + jnp.einsum(
            "tf,df->td", inner_grad_low, up_weight[layer], preferred_element_type=jnp.float32
        )
        gain_one = jnp.sum(hidden_grad * normed_one, axis=0)
        shift_one = jnp.sum(hidden_grad, axis=0)
        first_grad = norm_back(hidden_grad, normed_one, inverse_one, gains_pair[0])
        branch_grad_low = first_grad.astype(jnp.bfloat16)
        out_bias = jnp.sum(branch_grad_low.astype(jnp.float32), axis=0)
        out_matrix_grad = jnp.einsum(
            "td,te->de", attended_low, branch_grad_low, preferred_element_type=jnp.float32
        )
        attended_grad_low = jnp.einsum(
            "te,de->td", branch_grad_low, out_weight[layer], preferred_element_type=jnp.float32
        ).astype(jnp.bfloat16)
        grad_heads = attended_grad_low.reshape(rows, HEADS, HEAD_DIM)
        delta = jnp.sum(
            (attended_grad_low.astype(jnp.float32) * attended).reshape(rows, HEADS, HEAD_DIM),
            axis=-1,
        ).T
        back = make_back(query_heads, grad_heads, log_total, delta, mask_for, scale)
        state = (
            jnp.zeros((rows, HEADS, HEAD_DIM), jnp.float32),
            jnp.zeros((length, 2 * model), jnp.float32),
        )
        query_grad, full_grad = back(
            state, lax.all_gather(gathered, "seq", axis=0, tiled=True), jnp.int32(0)
        )
        key_value_grad = lax.psum_scatter(
            full_grad.astype(jnp.bfloat16), "seq", scatter_dimension=0, tiled=True
        ).astype(jnp.float32)
        mixed_grad_low = jnp.concatenate(
            [query_grad.reshape(rows, model), key_value_grad], axis=1
        ).astype(jnp.bfloat16)
        query_bias = jnp.sum(mixed_grad_low[:, :model].astype(jnp.float32), axis=0)
        value_bias = jnp.sum(mixed_grad_low[:, 2 * model :].astype(jnp.float32), axis=0)
        in_matrix_grad = jnp.einsum(
            "td,tm->dm", stream_low, mixed_grad_low, preferred_element_type=jnp.float32
        )
        grad = first_grad + jnp.einsum(
            "tm,dm->td", mixed_grad_low, in_weight[layer], preferred_element_type=jnp.float32
        )
        collected[layer] = (
            in_matrix_grad,
            out_matrix_grad,
            up_matrix_grad,
            down_matrix_grad,
            jnp.stack([gain_one, gain_two]),
            jnp.stack([query_bias, value_bias, out_bias, up_bias, down_bias, shift_one, shift_two]),
        )
    in_stack = jnp.stack([collected[layer][0] for layer in range(LAYERS)])
    out_stack = jnp.stack([collected[layer][1] for layer in range(LAYERS)])
    up_stack = jnp.stack([collected[layer][2] for layer in range(LAYERS)])
    down_stack = jnp.stack([collected[layer][3] for layer in range(LAYERS)])
    gains_stack = jnp.stack([collected[layer][4] for layer in range(LAYERS)])
    biases_stack = jnp.stack([collected[layer][5] for layer in range(LAYERS)])
    in_total, out_total, up_total, down_total, gains_total, biases_total = lax.psum(
        (in_stack, out_stack, up_stack, down_stack, gains_stack, biases_stack), ("dp", "seq")
    )
    stream_rms = jnp.sqrt(square_total / (count_total * model))
    return (
        layer_output,
        grad[None],
        in_total,
        out_total,
        up_total,
        down_total,
        gains_total,
        biases_total,
        stream_rms,
    )


MESH = pl.DeviceIdType.MESH
LOW = jnp.bfloat16
F32 = jnp.float32
SMALL_ROWS = 32
HOME_QUEUE = 0.5
SCALE = 1.0 / math.sqrt(HEAD_DIM)


def nn(left, right):
    return lax.dot_general(left, right, (((1,), (0,)), ((), ())), preferred_element_type=F32)


def nt(left, right):
    return lax.dot_general(left, right, (((1,), (1,)), ((), ())), preferred_element_type=F32)


def tn(left, right):
    return lax.dot_general(left, right, (((0,), (0,)), ((), ())), preferred_element_type=F32)


def column_sum(value):
    return jnp.sum(value.astype(F32), axis=0, keepdims=True)


def pad_head(rows, which):
    blank = jnp.zeros_like(rows)
    return jnp.concatenate([rows, blank] if which == 0 else [blank, rows], axis=0)


class Sems:
    def __init__(self, send, recv, near, set_size):
        self.set_size = set_size
        self.send, self.recv, self.near = send, recv, near
        self.far_used = self.near_used = 0
        self.spare = []

    def take_set(self):
        if self.spare:
            return self.spare.pop(0)
        first = self.far_used
        self.far_used += self.set_size
        return first

    def far(self, src, dst, device, index=None):
        if index is None:
            index = self.far_used
            self.far_used += 1
        return pltpu.make_async_remote_copy(
            src_ref=src,
            dst_ref=dst,
            send_sem=self.send.at[index],
            recv_sem=self.recv.at[index],
            device_id=device,
            device_id_type=MESH,
        )

    def local(self, src, dst):
        index = self.near_used
        self.near_used += 1
        return pltpu.make_async_copy(src, dst, self.near.at[index])


class Clock:
    QUEUE = 3.0

    def __init__(self):
        self.now = 0.0
        self.free = {"core": 0.0, "x": 0.0, "y": 0.0, "z": 0.0}

    def transfer(self, loads):
        end = 0.0
        for link, load in loads.items():
            begin = max(self.free[link], self.now)
            self.free[link] = begin + load
            end = max(end, self.free[link] + (0.9 if link == "core" else 2.8))
        return end

    def opens(self, loads):
        return max([self.free[link] - self.QUEUE for link in loads], default=0.0)


FAR_SEMS = 149
NEAR_SEMS = 38


def fused_kernel(
    levels,
    tok_ref,
    starts_ref,
    flags_ref,
    valid_ref,
    win_hbm,
    wout_hbm,
    wup_hbm,
    wdn_hbm,
    gains_ref,
    biases_ref,
    og_hbm,
    lo_hbm,
    ig_hbm,
    gin_hbm,
    gsq_hbm,
    small_ref,
    kept_hbm,
    win,
    wout,
    wup,
    wdn,
    low,
    outer,
    keys,
    values,
    turned,
    query_low,
    query_t,
    weights_t,
    attended_t,
    attended_low,
    inverse_total,
    normed_one,
    normed_two,
    inverse_norm,
    hidden_low,
    active_low,
    slope_low,
    scores,
    mask,
    flow,
    grad_low_t,
    grad_low,
    query_grad_t,
    give,
    take,
    meta,
    meta_sent,
    small,
    small_in,
    small_z,
    *rest,
):
    square_sum, wide_sum = rest[:8], rest[8:16]
    send_sems, recv_sems, near_sems = rest[16:]
    rows, model = low.shape[1], low.shape[2]
    length = 2 * rows
    pairs = HEADS // 2
    d = lax.axis_index("dp")
    x = lax.axis_index("seq")
    core = lax.rem(d, 2)
    y = lax.rem(lax.div(d, 2), 2)
    z = lax.div(d, 4)
    to_core = (d + 1 - 2 * core, x)
    to_x = (d, 1 - x)
    to_y = (d + 2 - 4 * y, x)
    to_diag = (d + 1 - 2 * core, 1 - x)

    def at_z(level):
        return (d + (level - z) * 4, x)

    z_next = [lax.rem(z + step, levels) for step in range(1, levels)]
    sems = Sems(send_sems, recv_sems, near_sems, 6 + 2 * (levels - 1))
    barrier = pltpu.get_barrier_semaphore()
    peers = [to_core, to_x, to_y, to_diag] + [at_z(level) for level in z_next]
    for peer in peers:
        pl.semaphore_signal(barrier, inc=1, device_id=peer, device_id_type=MESH)

    def load(pairs_of):
        copies = [sems.local(src, dst) for src, dst in pairs_of]
        for copy in copies:
            copy.start()
        return copies

    moved = core != x
    away_low = sems.far(tok_ref.at[0], low.at[0], to_diag)
    away_outer = sems.far(og_hbm.at[0], outer, to_diag)
    away_meta = sems.far(meta_sent, meta, to_diag)
    stay_low = sems.local(tok_ref.at[0], low.at[0])
    stay_outer = sems.local(og_hbm.at[0], outer)

    position = lax.broadcasted_iota(jnp.int32, (1, length), 1)
    segment = jnp.zeros((1, length), jnp.int32) - 1
    for cell in range(starts_ref.shape[1]):
        segment = segment + (position >= starts_ref[0:1, cell : cell + 1]).astype(jnp.int32)
    good = valid_ref[...] * (1 - flags_ref[...]) > 0
    meta_sent[...] = jnp.zeros_like(meta_sent)
    meta_sent[0:1, :] = jnp.where(good, segment, -1).astype(F32)
    meta_sent[1:2, :] = segment.astype(F32)
    meta_sent[2:3, :] = valid_ref[...].astype(F32)

    pl.semaphore_wait(barrier, len(peers))

    @pl.when(moved)
    def _():
        away_meta.start()
        away_low.start()

    @pl.when(jnp.logical_not(moved))
    def _():
        stay_low.start()
        meta[...] = meta_sent[...]

    weight_loads = []
    for layer in range(LAYERS):
        weight_loads.append(
            [
                load([(win_hbm.at[layer], win.at[layer])])[0],
                load([(wout_hbm.at[layer], wout.at[layer])])[0],
                load([(wup_hbm.at[layer], wup.at[layer])])[0],
                load([(wdn_hbm.at[layer], wdn.at[layer])])[0],
            ]
        )

    small[...] = jnp.zeros_like(small)

    @pl.when(moved)
    def _():
        away_meta.wait()

    near = meta[:, pl.ds(pl.multiple_of(core * rows, 128), rows)]
    far = meta[:, pl.ds(pl.multiple_of((1 - core) * rows, 128), rows)]
    near_t, far_t = near.T, far.T
    same = lax.broadcasted_iota(jnp.int32, (rows, rows), 0) == lax.broadcasted_iota(
        jnp.int32, (rows, rows), 1
    )
    mask[0:rows, :] = jnp.where((near_t[:, 0:1] == near[1:2, :]) | same, 0.0, NEG)
    mask[rows:length, :] = jnp.where(far_t[:, 0:1] == near[1:2, :], 0.0, NEG)
    valid_column = near_t[:, 2:3]
    small[0, 24:25, :] = near[2:3, :]

    @pl.when(moved)
    def _():
        away_low.wait()
        away_outer.start()

    @pl.when(jnp.logical_not(moved))
    def _():
        stay_low.wait()
        stay_outer.start()

    def note_square(layer, which, value):
        row = 18 + 3 * layer + which
        small[0, row : row + 1, :] = column_sum(value * value * valid_column)

    staged = square_sum[0].at[3 * LAYERS - 1]
    spills = []
    flow[...] = low[0].astype(F32)
    for layer in range(LAYERS):
        bias = [biases_ref[k, layer : layer + 1, :] for k in range(7)]
        gain = [gains_ref[layer, k : k + 1, :] for k in range(2)]
        load_in, load_out, load_up, load_down = weight_loads[layer]
        load_in.wait()
        stream_low = low[layer]
        note_square(layer, 0, flow[...])
        keys[layer, 0:rows, :] = nn(stream_low, win[layer, :, model : 2 * model]).astype(LOW)
        send_keys = sems.far(
            keys.at[layer, pl.ds(0, rows)], keys.at[layer, pl.ds(rows, rows)], to_core
        )
        send_keys.start()
        values[layer, 0:rows, :] = (
            nn(stream_low, win[layer, :, 2 * model : 3 * model]) + bias[1]
        ).astype(LOW)
        send_values = sems.far(
            values.at[layer, pl.ds(0, rows)], values.at[layer, pl.ds(rows, rows)], to_core
        )
        send_values.start()
        query = nn(stream_low, win[layer, :, 0:model]) + bias[0]
        query_low[layer] = (query * (SCALE / math.log(2.0))).astype(LOW)
        query_t[layer] = query_low[layer].T
        turned[:, 0:rows] = values[layer, 0:rows, :].T
        def score(head, begin=0, end=length, layer=layer):
            pair = head // 2
            scores[head % 2, begin:end] = (
                nn(
                    keys[layer, begin:end, 128 * pair : 128 * pair + 128],
                    pad_head(query_t[layer, 64 * head : 64 * head + 64, :], head % 2),
                )
                + mask[begin:end]
            )

        score(0, 0, rows)
        send_keys.wait()
        score(0, rows, length)
        for head in range(HEADS):
            if head + 1 < HEADS:
                score(head + 1)
            if head == 0:
                send_values.wait()
                turned[:, rows:length] = values[layer, rows:length, :].T
            if layer > 0:
                spills[layer - 1][head].wait()
            block = scores[head % 2]
            best = jnp.max(block, axis=0, keepdims=True)
            weight = jnp.exp2(block - best)
            inverse = 1.0 / jnp.sum(weight, axis=0, keepdims=True)
            weight_low = weight.astype(LOW)
            weights_t[head] = weight_low
            span = slice(64 * head, 64 * head + 64)
            inverse_total[layer, head : head + 1, :] = inverse
            attended_t[layer, span, :] = nn(turned[span, :], weight_low) * inverse
            if layer + 1 < LAYERS:
                if head == 0:
                    spills.append([])
                copy = sems.local(weights_t.at[head], kept_hbm.at[layer, head])
                copy.start()
                spills[layer].append(copy)
        attended_low[layer] = attended_t[layer].T.astype(LOW)
        load_out.wait()
        branch = nn(attended_low[layer], wout[layer]) + bias[2]
        note_square(layer, 1, branch)
        total = flow[...] + branch
        centred = total - jnp.mean(total, axis=-1, keepdims=True)
        inverse = lax.rsqrt(jnp.mean(centred * centred, axis=-1, keepdims=True) + EPS)
        normed = centred * inverse
        normed_one[layer] = normed.astype(LOW)
        inverse_norm[:, 2 * layer : 2 * layer + 1] = inverse
        hidden = normed * gain[0] + bias[5]
        flow[...] = hidden
        hidden_low[layer] = hidden.astype(LOW)
        load_up.wait()
        inner = nn(hidden_low[layer], wup[layer]) + bias[3]
        share = 0.5 * (1.0 + lax.erf(inner * 0.7071067811865476))
        active_low[layer] = (inner * share).astype(LOW)
        slope_low[layer] = (
            share + inner * jnp.exp(-0.5 * inner * inner) * 0.3989422804014327
        ).astype(LOW)
        load_down.wait()
        ff_out = nn(active_low[layer], wdn[layer]) + bias[4]
        note_square(layer, 2, ff_out)
        total = flow[...] + ff_out
        centred = total - jnp.mean(total, axis=-1, keepdims=True)
        inverse = lax.rsqrt(jnp.mean(centred * centred, axis=-1, keepdims=True) + EPS)
        normed = centred * inverse
        normed_two[layer] = normed.astype(LOW)
        inverse_norm[:, 2 * layer + 1 : 2 * layer + 2] = inverse
        result = normed * gain[1] + bias[6]
        if layer + 1 < LAYERS:
            flow[...] = result
            low[layer + 1] = result.astype(LOW)
        else:
            staged[...] = result.astype(LOW).reshape(staged.shape)

    away_result = [
        sems.far(staged.at[i, j], lo_hbm.at[i, j], to_diag) for i in range(2) for j in range(2)
    ]
    stay_result = sems.local(staged, lo_hbm)
    strips = [pl.ds(rows // 4 * k, rows // 4) for k in range(4)]
    away_grad = [sems.far(outer.at[strip], ig_hbm.at[0, strip], to_diag) for strip in strips]
    stay_grad = sems.local(outer, ig_hbm.at[0])

    @pl.when(moved)
    def _():
        away_outer.wait()

    @pl.when(jnp.logical_not(moved))
    def _():
        stay_outer.wait()
        stay_result.start()

    piece = model // 8 // levels
    own_rows = pl.ds(pl.multiple_of(z * piece, piece), piece)
    clock = Clock()

    def reduce_chunk(buffers, begin, count, home):
        return loads_of(buffers, count), steps_of(buffers, begin, count, home)

    def share_of(width):
        return width // 256 * 128

    def loads_of(buffers, count):
        width = buffers[0].shape[-1]
        size = count * width / model
        part = share_of(width) / width
        first = {"x": 2.88 * part * size, "y": 2.88 * (1 - part) * size}
        second = {"x": 1.44 * (1 - part) * size, "y": 1.44 * part * size}
        core_load, z_load = {"core": 0.46 * size}, {"z": 1.35 * size}
        return [core_load, first, second, z_load, z_load, second, first, core_load]

    def steps_of(buffers, begin, count, home):
        mine, whole, take_core, take_x, take_y, take_ay, take_bx, take_z = buffers
        width = mine.shape[-1]
        some = pl.ds(begin, count)
        landed = pl.ds(begin % take_core.shape[0], count)
        split = share_of(width)
        left, right = pl.ds(0, split), pl.ds(split, width - split)
        every = slice(None)
        first = sems.take_set()

        def send(src, dst, peer, index):
            copy = sems.far(src, dst, peer, first + index)
            copy.start()
            return copy

        def send_same(at, peer, index):
            return send(whole.at[at], whole.at[at], peer, index)

        def add_into(at, value):
            mine[at] = mine[at] + value

        def finish(copies):
            for copy in copies:
                copy.wait()

        mine_core, mine_left, mine_right = (
            (some, core),
            (some, core, x, every, every, left),
            (some, core, every, y, every, right),
        )
        deep_left, deep_right = (some, core, x, y, every, left), (some, core, x, y, every, right)
        own = (some, core, x, y, own_rows)
        by_core, by_x, by_y, by_y_deep, by_x_deep, back_core, by_z = 0, 1, 2, 3, 4, 5, 6
        back_z = by_z + levels - 1

        flight = [send(mine.at[some, 1 - core], take_core.at[landed], to_core, by_core)]
        yield
        finish(flight)
        add_into(mine_core, take_core[landed])
        flight = [
            send(mine.at[some, core, 1 - x, every, every, left], take_x.at[some], to_x, by_x),
            send(mine.at[some, core, every, 1 - y, every, right], take_y.at[some], to_y, by_y),
        ]
        yield
        finish(flight)
        add_into(mine_left, take_x[some])
        add_into(mine_right, take_y[some])
        flight = [
            send(mine.at[some, core, x, 1 - y, every, left], take_ay.at[some], to_y, by_y_deep),
            send(mine.at[some, core, 1 - x, y, every, right], take_bx.at[some], to_x, by_x_deep),
        ]
        yield
        finish(flight)
        add_into(deep_left, take_ay[some])
        add_into(deep_right, take_bx[some])
        flight = [
            send(
                mine.at[some, core, x, y, pl.ds(pl.multiple_of(level * piece, piece), piece)],
                take_z.at[step, some],
                at_z(level),
                by_z + step,
            )
            for step, level in enumerate(z_next)
        ]
        yield
        finish(flight)
        total = mine[own].astype(F32)
        for step in range(levels - 1):
            total = total + take_z[step, some].astype(F32)
        whole[own[:1] + own[2:]] = total.astype(LOW)
        flight = [
            send_same(own[:1] + own[2:], at_z(level), back_z + step)
            for step, level in enumerate(z_next)
        ]
        yield
        finish(flight)
        flight = [
            send_same((some, x, y, every, left), to_y, by_y),
            send_same((some, x, y, every, right), to_x, by_x),
        ]
        yield
        finish(flight)
        flight = [
            send_same((some, x, every, every, left), to_x, by_x_deep),
            send_same((some, every, y, every, right), to_y, by_y_deep),
        ]
        yield
        finish(flight)
        flight = [send(whole.at[some], home, to_core, back_core)]
        copy = sems.local(whole.at[some], home)
        copy.start()
        homing.append(copy)
        yield
        finish(flight)
        sems.spare.append(first)

    def send_home(copies):
        for copy in copies:
            pl.when(moved)(copy.start)
            yield
        for copy in copies:
            pl.when(moved)(copy.wait)

    def reduce_small():
        for step, peer in enumerate((to_core, to_x, to_y)):
            copy = sems.far(small.at[step], small_in.at[step], peer)
            copy.start()
            yield
            copy.wait()
            small[step + 1] = small[step] + small_in[step]
        copies = [sems.far(small.at[3], small_z.at[z], at_z(level)) for level in z_next]
        for copy in copies:
            copy.start()
        small_z[z] = small[3]
        yield
        for copy in copies:
            copy.wait()
        total = small_z[0]
        for level in range(1, levels):
            total = total + small_z[level]
        small_ref[...] = total

    homing = []
    active = []

    def advance(entry):
        loads = entry[2]
        if next(entry[1], True):
            active.remove(entry)
            clock.now += 0.1
        else:
            clock.now += 0.25
            entry[0] = clock.transfer(loads.pop(0))

    def begin(chunk):
        loads, steps = chunk
        entry = [0.0, steps, loads, True]
        active.append(entry)
        advance(entry)

    def begin_home(copies):
        entry = [clock.now, send_home(copies), [{"x": 1.45} for _ in copies], False]
        active.append(entry)
        return entry

    def when(entry):
        if not entry[2]:
            return entry[0]
        if not entry[3]:
            return max(clock.now, clock.free["x"] - HOME_QUEUE)
        return max(entry[0], clock.opens(entry[2][0]))

    def pump(spent):
        clock.now += spent
        while True:
            ready = [entry for entry in active if when(entry) <= clock.now]
            if not ready:
                return
            advance(max(ready, key=lambda entry: (entry[3], len(entry[2]))))

    def note(row, value):
        small[0, row : row + 1, :] = value

    reloads = []
    result_home = begin_home(away_result)
    flow[...] = outer[...].astype(F32)
    for layer in reversed(range(LAYERS)):
        gain = [gains_ref[layer, k : k + 1, :] for k in range(2)]
        base = 3 * (LAYERS - 1 - layer)
        wide = pairs * (LAYERS - 1 - layer)
        mine = square_sum[0]
        folded = mine.shape[1:]
        bias_row = 4 + 7 * layer
        turned[...] = keys[layer].T
        grad = flow[...]
        normed = normed_two[layer].astype(F32)
        note(2 * layer + 1, column_sum(grad * normed))
        note(bias_row + 6, column_sum(grad))
        scaled = grad * gain[1]
        second = inverse_norm[:, 2 * layer + 1 : 2 * layer + 2] * (
            scaled
            - jnp.mean(scaled, axis=-1, keepdims=True)
            - normed * jnp.mean(scaled * normed, axis=-1, keepdims=True)
        )
        scores[0, 0:rows, :] = second
        down_low = second.astype(LOW)
        note(bias_row + 4, column_sum(down_low))
        mine[base] = tn(active_low[layer], down_low).astype(LOW).reshape(folded)
        inner_low = (nt(down_low, wdn[layer]) * slope_low[layer].astype(F32)).astype(LOW)
        note(bias_row + 3, column_sum(inner_low))
        mine[base + 1] = tn(hidden_low[layer], inner_low).astype(LOW).reshape(folded)
        pump(2.6)
        begin(
            reduce_chunk(
                square_sum,
                base,
                2,
                gsq_hbm.at[layer, pl.ds(0, 2), core],
            )
        )
        grad = scores[0, 0:rows, :] + nt(inner_low, wup[layer])
        normed = normed_one[layer].astype(F32)
        note(2 * layer, column_sum(grad * normed))
        note(bias_row + 5, column_sum(grad))
        scaled = grad * gain[0]
        flow[...] = inverse_norm[:, 2 * layer : 2 * layer + 1] * (
            scaled
            - jnp.mean(scaled, axis=-1, keepdims=True)
            - normed * jnp.mean(scaled * normed, axis=-1, keepdims=True)
        )
        branch_low = flow[...].astype(LOW)
        note(bias_row + 2, column_sum(branch_low))
        mine[base + 2] = tn(attended_low[layer], branch_low).astype(LOW).reshape(folded)
        pump(1.2)
        begin(
            reduce_chunk(square_sum, base + 2, 1, gsq_hbm.at[layer, pl.ds(2, 1), core])
        )
        attended_grad_t = nt(branch_low, wout[layer]).astype(LOW).T
        for head in range(HEADS):
            span = slice(64 * head, 64 * head + 64)
            grad_low_t[span, :] = (
                attended_grad_t[span, :].astype(F32) * inverse_total[layer, head : head + 1, :]
            ).astype(LOW)
        grad_low[...] = grad_low_t[...].T
        pump(1.0)
        gives = []

        def close_pairs(chosen, layer=layer, wide=wide, bias_row=bias_row, gives=gives):
            mine = wide_sum[0]
            parts = []
            for pair in chosen:
                side = slice(128 * pair, 128 * pair + 128)
                gives[pair].wait()
                taken = [take[layer, pair, which].astype(F32) for which in range(2)]
                three = [
                    query_grad_t[side, :].T,
                    (mask[0:rows, side] + taken[0]).astype(LOW),
                    (mask[rows:length, side] + taken[1]).astype(LOW),
                ]
                small[0, bias_row : bias_row + 1, side] = column_sum(three[0])
                small[0, bias_row + 1 : bias_row + 2, side] = column_sum(three[2])
                parts += three
            part = jnp.concatenate(parts, axis=1)
            product = tn(low[layer], part).astype(LOW)
            for k, pair in enumerate(chosen):
                slot = wide + pair
                mine[slot] = product[:, 384 * k : 384 * k + 384].reshape(mine.shape[1:])
            first, count = wide + chosen[0], len(chosen)
            home = gin_hbm.at[layer, pl.ds(chosen[0], count), core]
            pump(0.4 * count)
            begin(reduce_chunk(wide_sum, first, count, home))
            weight = jnp.concatenate(
                [
                    win[layer, :, model * k + 128 * pair : model * k + 128 * pair + 128]
                    for pair in chosen
                    for k in range(3)
                ],
                axis=1,
            )
            total = flow[...] + nt(part, weight)
            if layer > 0 or chosen[-1] < pairs - 1:
                flow[...] = total
            else:
                outer[...] = total.astype(LOW)

        first_half = lax.broadcasted_iota(jnp.int32, (1, 128), 1) < HEAD_DIM
        for head in range(HEADS):
            pair = head // 2
            span = slice(64 * head, 64 * head + 64)
            lanes = slice(128 * pair, 128 * pair + 128)
            grad_part = grad_low_t[span, :]
            delta = column_sum(grad_part.astype(F32) * attended_t[layer, span, :])
            if layer + 1 < LAYERS:
                reloads[head].wait()
            prob_grad = nn(values[layer, :, lanes], pad_head(grad_part, head % 2))
            score_grad = (weights_t[head].astype(F32) * (prob_grad - delta)).astype(LOW)
            query_grad_t[span, :] = (nn(turned[span, :], score_grad) * SCALE).astype(LOW)
            key_part = nn(score_grad, query_low[layer, :, lanes])
            value_part = nn(weights_t[head], grad_low[:, lanes])
            if head % 2 == 0:
                key_even, value_even = key_part, value_part
            else:
                key_grad = jnp.where(first_half, key_even, key_part) * math.log(2.0)
                value_grad = jnp.where(first_half, value_even, value_part)
                mask[0:rows, lanes] = key_grad[0:rows]
                mask[rows:length, lanes] = value_grad[0:rows]
                give[pair, 0] = key_grad[rows:length].astype(LOW)
                give[pair, 1] = value_grad[rows:length].astype(LOW)
                copy = sems.far(give.at[pair], take.at[layer, pair], to_core)
                copy.start()
                gives.append(copy)
            if layer > 0:
                copy = sems.local(kept_hbm.at[layer - 1, head], weights_t.at[head])
                copy.start()
                reloads.append(copy)
            pump(1.15)
            if layer > 0 and head == HEADS // 2:
                close_pairs([0, 1])
            if layer == 0 and head % 2 == 0 and head > 0:
                close_pairs([pair - 1])
        close_pairs([2, 3] if layer > 0 else [3])
        if layer == 0:
            begin(([{"core": 0.1}, {"x": 1.5}, {"y": 1.5}, {"z": 2.0}], reduce_small()))
        if layer > 0:

            while result_home in active:
                advance(result_home)

            @pl.when(jnp.logical_not(moved))
            def _():
                stay_result.wait()

        pump(0.4)

    begin_home(away_grad)

    @pl.when(jnp.logical_not(moved))
    def _():
        stay_grad.start()

    while active:
        clock.now = max(clock.now, min(when(entry) for entry in active))
        pump(0.0)
    for copy in homing:
        copy.wait()

    @pl.when(jnp.logical_not(moved))
    def _():
        stay_grad.wait()

    assert sems.far_used <= FAR_SEMS and sems.near_used <= NEAR_SEMS


def local_pair(
    tokens,
    cell_starts,
    generate_flags,
    valid_mask,
    in_weight,
    out_weight,
    up_weight,
    down_weight,
    norm_gains,
    biases,
    out_grad,
):
    rows, model = tokens.shape[1:]
    length = 2 * rows
    levels = lax.axis_size("dp") // 4
    eighth = model // 8
    folded = (2, 2, 2, eighth)

    def sum_buffers(count, shared, width):
        split = width // 256 * 128
        return [
            pltpu.VMEM((count,) + folded + (width,), LOW),
            pltpu.VMEM((count,) + folded[1:] + (width,), LOW),
            pltpu.VMEM((shared,) + folded[1:] + (width,), LOW),
            pltpu.VMEM((count, 2, eighth, split), LOW),
            pltpu.VMEM((count, 2, eighth, width - split), LOW),
            pltpu.VMEM((count, eighth, split), LOW),
            pltpu.VMEM((count, eighth, width - split), LOW),
            pltpu.VMEM((max(levels - 1, 1), count, eighth // levels, width), LOW),
        ]

    shape = jax.ShapeDtypeStruct
    vmem, anywhere = pl.BlockSpec(memory_space=pltpu.VMEM), pl.BlockSpec(memory_space=pl.ANY)
    by_layer = (LAYERS, rows, model)
    scratch = [
        pltpu.VMEM(in_weight.shape, LOW),
        pltpu.VMEM(out_weight.shape, LOW),
        pltpu.VMEM(up_weight.shape, LOW),
        pltpu.VMEM(down_weight.shape, LOW),
        pltpu.VMEM(by_layer, LOW),
        pltpu.VMEM((rows, model), LOW),
        pltpu.VMEM((LAYERS, length, model), LOW),
        pltpu.VMEM((LAYERS, length, model), LOW),
        pltpu.VMEM((model, length), LOW),
        pltpu.VMEM(by_layer, LOW),
        pltpu.VMEM((LAYERS, model, rows), LOW),
        pltpu.VMEM((HEADS, length, rows), LOW),
        pltpu.VMEM((LAYERS, model, rows), F32),
        pltpu.VMEM(by_layer, LOW),
        pltpu.VMEM((LAYERS, HEADS, rows), F32),
        pltpu.VMEM(by_layer, LOW),
        pltpu.VMEM(by_layer, LOW),
        pltpu.VMEM((rows, 2 * LAYERS), F32),
        pltpu.VMEM(by_layer, LOW),
        pltpu.VMEM(by_layer, LOW),
        pltpu.VMEM(by_layer, LOW),
        pltpu.VMEM((2, length, rows), F32),
        pltpu.VMEM((length, rows), F32),
        pltpu.VMEM((rows, model), F32),
        pltpu.VMEM((model, rows), LOW),
        pltpu.VMEM((rows, model), LOW),
        pltpu.VMEM((model, rows), LOW),
        pltpu.VMEM((HEADS // 2, 2, rows, 128), LOW),
        pltpu.VMEM((LAYERS, HEADS // 2, 2, rows, 128), LOW),
        pltpu.VMEM((8, length), F32),
        pltpu.VMEM((8, length), F32),
        pltpu.VMEM((4, SMALL_ROWS, model), F32),
        pltpu.VMEM((3, SMALL_ROWS, model), F32),
        pltpu.VMEM((levels, SMALL_ROWS, model), F32),
        *sum_buffers(3 * LAYERS, 3, model),
        *sum_buffers(HEADS // 2 * LAYERS, HEADS // 2, 384),
        pltpu.SemaphoreType.DMA((FAR_SEMS,)),
        pltpu.SemaphoreType.DMA((FAR_SEMS,)),
        pltpu.SemaphoreType.DMA((NEAR_SEMS,)),
    ]
    lo, ig, gin, gsq, small, _ = pl.pallas_call(
        functools.partial(fused_kernel, levels),
        out_shape=[
            shape(folded + (model,), LOW),
            shape(tokens.shape, LOW),
            shape((LAYERS, HEADS // 2) + folded + (384,), LOW),
            shape((LAYERS, 3) + folded + (model,), LOW),
            shape((SMALL_ROWS, model), F32),
            shape((LAYERS - 1, HEADS, length, rows), LOW),
        ],
        in_specs=[anywhere, vmem, vmem, vmem] + [anywhere] * 4 + [vmem, vmem, anywhere],
        out_specs=[anywhere] * 4 + [vmem, anywhere],
        scratch_shapes=scratch,
        compiler_params=pltpu.CompilerParams(
            collective_id=0, has_side_effects=True, vmem_limit_bytes=VMEM_BYTES
        ),
    )(
        tokens,
        cell_starts,
        generate_flags,
        valid_mask,
        in_weight,
        out_weight,
        up_weight,
        down_weight,
        norm_gains,
        biases.transpose(1, 0, 2),
        out_grad,
    )
    return finish(tokens, in_weight, lo, ig, gin, gsq, small)


VMEM_BYTES = 63 * 1024 * 1024


def finish_kernel(model, *refs):
    lo_in, ig_in, gin_in, gsq_in, small = refs[:5]
    lo, ig, gin, gout, gup, gdn, gains, shifts, rms = refs[5:14]
    low_wide, wide, low_square, square, passing, in_sems, out_sems = refs[14:]
    pairs = gin_in.shape[1]
    reads, writes = [], []

    def read(src, dst):
        copy = pltpu.make_async_copy(src, dst, in_sems.at[len(reads)])
        copy.start()
        reads.append(copy)
        return copy

    def write(src, dst):
        copy = pltpu.make_async_copy(src, dst, out_sems.at[len(writes)])
        copy.start()
        writes.append(copy)

    def widen_square(slot, copy, target):
        copy.wait()
        square[slot] = low_square[slot].astype(F32)
        write(square.at[slot], target)

    reads_lo = read(lo_in, passing)
    reads_square, reads_wide = [], []
    for layer in range(LAYERS):
        for k in range(3):
            reads_square.append(read(gsq_in.at[layer, k], low_square.at[3 * layer + k]))
            if k == 0:
                for pair in range(pairs):
                    reads_wide.append(
                        read(gin_in.at[layer, pair], low_wide.at[pairs * layer + pair])
                    )
    reads_ig = read(ig_in.at[0], low_square.at[3 * LAYERS])
    for layer in range(LAYERS):
        for k in range(2):
            row = 2 * layer + k
            gains[layer, k : k + 1, :] = small[row : row + 1, :]
        for k in range(7):
            row = 2 * LAYERS + 7 * layer + k
            shifts[k, layer : layer + 1, :] = small[row : row + 1, :]
    first = 9 * LAYERS
    count = jnp.sum(small[first + 3 * LAYERS : first + 3 * LAYERS + 1, :], keepdims=True)
    line = lax.broadcasted_iota(jnp.int32, rms.shape, 0)
    place = lax.broadcasted_iota(jnp.int32, rms.shape, 1)
    squares = jnp.zeros(rms.shape, F32)
    for layer in range(LAYERS):
        for k in range(3):
            row = first + 3 * layer + k
            value = jnp.sum(small[row : row + 1, :], keepdims=True)
            squares = jnp.where((line == layer) & (place == k), value, squares)
    rms[...] = jnp.sqrt(squares / (count * model))
    reads_lo.wait()
    write(passing, lo)
    for layer in range(LAYERS):
        for k, target in enumerate((gdn, gup, gout)):
            slot = 3 * layer + k
            widen_square(slot, reads_square[slot], target.at[layer])
            if k == 0:
                for pair in range(pairs):
                    slot = pairs * layer + pair
                    reads_wide[slot].wait()
                    for part in range(3):
                        begin = model * part + 128 * pair
                        wide[layer, :, begin : begin + 128] = low_wide[
                            slot, :, 128 * part : 128 * part + 128
                        ].astype(F32)
                write(wide.at[layer], gin.at[layer])
    widen_square(3 * LAYERS, reads_ig, ig.at[0])
    for copy in writes:
        copy.wait()


def finish(tokens, in_weight, lo, ig, gin, gsq, small):
    rows, model = tokens.shape[1:]
    shape = jax.ShapeDtypeStruct
    vmem, far = pl.BlockSpec(memory_space=pltpu.VMEM), pl.BlockSpec(memory_space=pltpu.HBM)
    square = (LAYERS, model, model)
    slots = LAYERS * HEADS // 2
    outs = pl.pallas_call(
        functools.partial(finish_kernel, model),
        out_shape=[
            shape(tokens.shape, LOW),
            shape(tokens.shape, F32),
            shape(in_weight.shape, F32),
            shape(square, F32),
            shape(square, F32),
            shape(square, F32),
            shape((LAYERS, 2, model), F32),
            shape((7, LAYERS, model), F32),
            shape((LAYERS, 3), F32),
        ],
        in_specs=[far] * 4 + [vmem],
        out_specs=[far] * 6 + [vmem] * 3,
        scratch_shapes=[
            pltpu.VMEM((slots, model, 384), LOW),
            pltpu.VMEM(in_weight.shape, F32),
            pltpu.VMEM((3 * LAYERS + 1, model, model), LOW),
            pltpu.VMEM((3 * LAYERS + 1, model, model), F32),
            pltpu.VMEM(tokens.shape, LOW),
            pltpu.SemaphoreType.DMA((slots + 3 * LAYERS + 2,)),
            pltpu.SemaphoreType.DMA((4 * LAYERS + 2,)),
        ],
        compiler_params=pltpu.CompilerParams(vmem_limit_bytes=VMEM_BYTES),
    )(
        lo.reshape(tokens.shape),
        ig,
        gin.reshape(LAYERS, HEADS // 2, model, 384),
        gsq.reshape(LAYERS, 3, model, model),
        small,
    )
    lo, ig, gin, gout, gup, gdn, gains, shifts, rms = outs
    return lo, ig, gin, gout, gup, gdn, gains, shifts.transpose(1, 0, 2), rms


def solution(mesh):
    placed = (
        P("dp", "seq", None),
        P("dp", None),
        P("dp", None),
        P("dp", None),
        P(),
        P(),
        P(),
        P(),
        P(),
        P(),
        P("dp", "seq", None),
    )
    paired = mesh.shape["seq"] == 2 and mesh.shape["dp"] % 4 == 0
    return jax.shard_map(
        local_pair if paired else local,
        mesh=mesh,
        in_specs=placed,
        out_specs=(P("dp", "seq", None), P("dp", "seq", None), P(), P(), P(), P(), P(), P(), P()),
        check_vma=False,
    )
```

```python
import functools
import math

import jax
import jax.numpy as jnp
from jax import lax
from jax.experimental import pallas as pl
from jax.experimental.pallas import tpu as pltpu
from jax.sharding import PartitionSpec as P

HEADS = 8
HEAD_DIM = 64
LAYERS = 2


EPS = 1e-05
NEG = -1e30


def block_width(count):
    for option in range(1024, 255, -1):
        if count % option == 0:
            return option
    return count


def segment_ids(starts_row, positions):
    return jnp.sum((positions[:, None] >= starts_row[None, :]).astype(jnp.int32), axis=1) - 1


def norm_rows(total, gain, shift):
    mean = jnp.mean(total, axis=-1, keepdims=True)
    centred = total - mean
    spread = jnp.mean(centred * centred, axis=-1, keepdims=True)
    inverse = lax.rsqrt(spread + EPS)
    normed = centred * inverse
    return (normed * gain + shift, normed, inverse)


def norm_back(grad, normed, inverse, gain):
    scaled = grad * gain
    return inverse * (
        scaled
        - jnp.mean(scaled, axis=-1, keepdims=True)
        - normed * jnp.mean(scaled * normed, axis=-1, keepdims=True)
    )


def gelu_slope(inner):
    return (
        0.5 * (1.0 + jax.scipy.special.erf(inner * 0.7071067811865476))
        + inner * jnp.exp(-0.5 * inner * inner) * 0.3989422804014327
    )


def make_mask(query_pos, query_seg, starts_row, key_ok_row):

    def mask_for(begin, width):
        key_pos = begin + jnp.arange(width, dtype=jnp.int32)
        key_seg = segment_ids(starts_row, key_pos)
        key_good = lax.dynamic_slice_in_dim(key_ok_row, begin, width, 0) > 0
        return (query_seg[:, None] == key_seg[None, :]) & (
            key_good[None, :] | (query_pos[:, None] == key_pos[None, :])
        )

    return mask_for


def make_attend(query_heads, mask_for, scale):

    def attend(carry, piece, start):
        count = piece.shape[0]
        width = block_width(count)
        model = piece.shape[1] // 2

        def attend_one_block(step, state):
            best, total, summed = state
            begin = step * width
            block = lax.dynamic_slice_in_dim(piece, begin, width, 0)
            key_heads = block[:, :model].reshape(width, HEADS, HEAD_DIM)
            value_heads = block[:, model:].reshape(width, HEADS, HEAD_DIM)
            allowed = mask_for(start + begin, width)[None]
            scores = (
                jnp.einsum(
                    "qhd,khd->hqk", query_heads, key_heads, preferred_element_type=jnp.float32
                )
                * scale
            )
            scores = jnp.where(allowed, scores, NEG)
            new_best = jnp.maximum(best, jnp.max(scores, axis=-1))
            factor = jnp.exp(best - new_best)
            weights = jnp.where(allowed, jnp.exp(scores - new_best[:, :, None]), 0.0)
            total = total * factor + jnp.sum(weights, axis=-1)
            update = jnp.einsum(
                "hqk,khd->qhd",
                weights.astype(jnp.bfloat16),
                value_heads,
                preferred_element_type=jnp.float32,
            )
            summed = summed * factor.T[:, :, None] + update
            return (new_best, total, summed)

        return lax.fori_loop(0, count // width, attend_one_block, carry)

    return attend


def make_back(query_heads, grad_heads, log_total, delta, mask_for, scale):

    def back(carry, piece, start):
        count = piece.shape[0]
        width = block_width(count)
        model = piece.shape[1] // 2

        def back_one_block(step, state):
            query_grad, full_grad = state
            begin = step * width
            block = lax.dynamic_slice_in_dim(piece, begin, width, 0)
            key_heads = block[:, :model].reshape(width, HEADS, HEAD_DIM)
            value_heads = block[:, model:].reshape(width, HEADS, HEAD_DIM)
            allowed = mask_for(start + begin, width)[None]
            scores = (
                jnp.einsum(
                    "qhd,khd->hqk", query_heads, key_heads, preferred_element_type=jnp.float32
                )
                * scale
            )
            probs = jnp.where(allowed, jnp.exp(scores - log_total[:, :, None]), 0.0)
            prob_grad = jnp.einsum(
                "qhd,khd->hqk", grad_heads, value_heads, preferred_element_type=jnp.float32
            )
            score_grad = (probs * (prob_grad - delta[:, :, None])).astype(jnp.bfloat16)
            query_grad = (
                query_grad
                + jnp.einsum(
                    "hqk,khd->qhd", score_grad, key_heads, preferred_element_type=jnp.float32
                )
                * scale
            )
            key_grad = (
                jnp.einsum(
                    "hqk,qhd->khd", score_grad, query_heads, preferred_element_type=jnp.float32
                )
                * scale
            )
            value_grad = jnp.einsum(
                "hqk,qhd->khd",
                probs.astype(jnp.bfloat16),
                grad_heads,
                preferred_element_type=jnp.float32,
            )
            update = jnp.concatenate(
                [key_grad.reshape(width, model), value_grad.reshape(width, model)], axis=1
            )
            place = start + begin
            current = lax.dynamic_slice_in_dim(full_grad, place, width, 0)
            full_grad = lax.dynamic_update_slice_in_dim(full_grad, current + update, place, 0)
            return (query_grad, full_grad)

        return lax.fori_loop(0, count // width, back_one_block, carry)

    return back


def local(
    tokens,
    cell_starts,
    generate_flags,
    valid_mask,
    in_weight,
    out_weight,
    up_weight,
    down_weight,
    norm_gains,
    biases,
    out_grad,
):
    rows = tokens.shape[1]
    model = tokens.shape[2]
    scale = 1.0 / math.sqrt(HEAD_DIM)
    first = lax.axis_index("seq") * rows
    query_pos = first + jnp.arange(rows, dtype=jnp.int32)
    starts_row = cell_starts[0]
    key_ok_row = valid_mask[0] * (1 - generate_flags[0])
    mask_for = make_mask(query_pos, segment_ids(starts_row, query_pos), starts_row, key_ok_row)
    valid_here = lax.dynamic_slice_in_dim(valid_mask[0], first, rows, 0).astype(jnp.float32)
    stream = tokens[0].astype(jnp.float32)
    stream_low = tokens[0]
    kept = []
    squares = []
    for layer in range(LAYERS):
        bias_rows = biases[layer]
        gains_pair = norm_gains[layer]
        mixed = jnp.dot(
            stream_low, in_weight[layer], preferred_element_type=jnp.float32
        ) + jnp.concatenate([bias_rows[0], jnp.zeros((model,), jnp.float32), bias_rows[1]])
        mixed_low = mixed.astype(jnp.bfloat16)
        query_heads = mixed_low[:, :model].reshape(rows, HEADS, HEAD_DIM)
        key_value = mixed_low[:, model:]
        attend = make_attend(query_heads, mask_for, scale)
        state = (
            jnp.full((HEADS, rows), NEG, jnp.float32),
            jnp.zeros((HEADS, rows), jnp.float32),
            jnp.zeros((rows, HEADS, HEAD_DIM), jnp.float32),
        )
        gathered = key_value
        best, total, summed = attend(
            state, lax.all_gather(key_value, "seq", axis=0, tiled=True), jnp.int32(0)
        )
        attended = (summed / total.T[:, :, None]).reshape(rows, model)
        log_total = best + jnp.log(total)
        attended_low = attended.astype(jnp.bfloat16)
        branch = (
            jnp.dot(attended_low, out_weight[layer], preferred_element_type=jnp.float32)
            + bias_rows[2]
        )
        hidden, normed_one, inverse_one = norm_rows(stream + branch, gains_pair[0], bias_rows[5])
        hidden_low = hidden.astype(jnp.bfloat16)
        inner = (
            jnp.dot(hidden_low, up_weight[layer], preferred_element_type=jnp.float32) + bias_rows[3]
        )
        active_low = jax.nn.gelu(inner, approximate=False).astype(jnp.bfloat16)
        ff_out = (
            jnp.dot(active_low, down_weight[layer], preferred_element_type=jnp.float32)
            + bias_rows[4]
        )
        result, normed_two, inverse_two = norm_rows(hidden + ff_out, gains_pair[1], bias_rows[6])
        squares.append(
            jnp.stack(
                [
                    jnp.sum(valid_here * jnp.sum(part * part, axis=-1))
                    for part in (stream, branch, ff_out)
                ]
            )
        )
        kept.append(
            (
                stream_low,
                query_heads,
                gathered,
                attended,
                attended_low,
                log_total,
                normed_one,
                inverse_one,
                hidden_low,
                inner,
                active_low,
                normed_two,
                inverse_two,
            )
        )
        stream = result
        stream_low = result.astype(jnp.bfloat16)
    layer_output = stream.astype(jnp.bfloat16)[None]
    square_local = jnp.stack(squares)
    count_local = jnp.sum(valid_here)
    square_total, count_total = lax.psum((square_local, count_local), ("dp", "seq"))
    grad = out_grad[0].astype(jnp.float32)
    length = rows * lax.axis_size("seq")
    collected = [None] * LAYERS
    for layer in reversed(range(LAYERS)):
        (
            stream_low,
            query_heads,
            gathered,
            attended,
            attended_low,
            log_total,
            normed_one,
            inverse_one,
            hidden_low,
            inner,
            active_low,
            normed_two,
            inverse_two,
        ) = kept[layer]
        gains_pair = norm_gains[layer]
        gain_two = jnp.sum(grad * normed_two, axis=0)
        shift_two = jnp.sum(grad, axis=0)
        second_grad = norm_back(grad, normed_two, inverse_two, gains_pair[1])
        down_grad_low = second_grad.astype(jnp.bfloat16)
        down_bias = jnp.sum(down_grad_low.astype(jnp.float32), axis=0)
        down_matrix_grad = jnp.einsum(
            "tf,td->fd", active_low, down_grad_low, preferred_element_type=jnp.float32
        )
        active_grad = jnp.einsum(
            "td,fd->tf", down_grad_low, down_weight[layer], preferred_element_type=jnp.float32
        )
        inner_grad_low = (active_grad * gelu_slope(inner)).astype(jnp.bfloat16)
        up_bias = jnp.sum(inner_grad_low.astype(jnp.float32), axis=0)
        up_matrix_grad = jnp.einsum(
            "td,tf->df", hidden_low, inner_grad_low, preferred_element_type=jnp.float32
        )
        hidden_grad = second_grad + jnp.einsum(
            "tf,df->td", inner_grad_low, up_weight[layer], preferred_element_type=jnp.float32
        )
        gain_one = jnp.sum(hidden_grad * normed_one, axis=0)
        shift_one = jnp.sum(hidden_grad, axis=0)
        first_grad = norm_back(hidden_grad, normed_one, inverse_one, gains_pair[0])
        branch_grad_low = first_grad.astype(jnp.bfloat16)
        out_bias = jnp.sum(branch_grad_low.astype(jnp.float32), axis=0)
        out_matrix_grad = jnp.einsum(
            "td,te->de", attended_low, branch_grad_low, preferred_element_type=jnp.float32
        )
        attended_grad_low = jnp.einsum(
            "te,de->td", branch_grad_low, out_weight[layer], preferred_element_type=jnp.float32
        ).astype(jnp.bfloat16)
        grad_heads = attended_grad_low.reshape(rows, HEADS, HEAD_DIM)
        delta = jnp.sum(
            (attended_grad_low.astype(jnp.float32) * attended).reshape(rows, HEADS, HEAD_DIM),
            axis=-1,
        ).T
        back = make_back(query_heads, grad_heads, log_total, delta, mask_for, scale)
        state = (
            jnp.zeros((rows, HEADS, HEAD_DIM), jnp.float32),
            jnp.zeros((length, 2 * model), jnp.float32),
        )
        query_grad, full_grad = back(
            state, lax.all_gather(gathered, "seq", axis=0, tiled=True), jnp.int32(0)
        )
        key_value_grad = lax.psum_scatter(
            full_grad.astype(jnp.bfloat16), "seq", scatter_dimension=0, tiled=True
        ).astype(jnp.float32)
        mixed_grad_low = jnp.concatenate(
            [query_grad.reshape(rows, model), key_value_grad], axis=1
        ).astype(jnp.bfloat16)
        query_bias = jnp.sum(mixed_grad_low[:, :model].astype(jnp.float32), axis=0)
        value_bias = jnp.sum(mixed_grad_low[:, 2 * model :].astype(jnp.float32), axis=0)
        in_matrix_grad = jnp.einsum(
            "td,tm->dm", stream_low, mixed_grad_low, preferred_element_type=jnp.float32
        )
        grad = first_grad + jnp.einsum(
            "tm,dm->td", mixed_grad_low, in_weight[layer], preferred_element_type=jnp.float32
        )
        collected[layer] = (
            in_matrix_grad,
            out_matrix_grad,
            up_matrix_grad,
            down_matrix_grad,
            jnp.stack([gain_one, gain_two]),
            jnp.stack([query_bias, value_bias, out_bias, up_bias, down_bias, shift_one, shift_two]),
        )
    in_stack = jnp.stack([collected[layer][0] for layer in range(LAYERS)])
    out_stack = jnp.stack([collected[layer][1] for layer in range(LAYERS)])
    up_stack = jnp.stack([collected[layer][2] for layer in range(LAYERS)])
    down_stack = jnp.stack([collected[layer][3] for layer in range(LAYERS)])
    gains_stack = jnp.stack([collected[layer][4] for layer in range(LAYERS)])
    biases_stack = jnp.stack([collected[layer][5] for layer in range(LAYERS)])
    in_total, out_total, up_total, down_total, gains_total, biases_total = lax.psum(
        (in_stack, out_stack, up_stack, down_stack, gains_stack, biases_stack), ("dp", "seq")
    )
    stream_rms = jnp.sqrt(square_total / (count_total * model))
    return (
        layer_output,
        grad[None],
        in_total,
        out_total,
        up_total,
        down_total,
        gains_total,
        biases_total,
        stream_rms,
    )


MESH = pl.DeviceIdType.MESH
LOW = jnp.bfloat16
F32 = jnp.float32
SMALL_ROWS = 32
HOME_QUEUE = 0.5
SCALE = 1.0 / math.sqrt(HEAD_DIM)


def nn(left, right):
    return lax.dot_general(left, right, (((1,), (0,)), ((), ())), preferred_element_type=F32)


def nt(left, right):
    return lax.dot_general(left, right, (((1,), (1,)), ((), ())), preferred_element_type=F32)


def tn(left, right):
    return lax.dot_general(left, right, (((0,), (0,)), ((), ())), preferred_element_type=F32)


def column_sum(value):
    return jnp.sum(value.astype(F32), axis=0, keepdims=True)


def pad_head(rows, which):
    blank = jnp.zeros_like(rows)
    return jnp.concatenate([rows, blank] if which == 0 else [blank, rows], axis=0)


class Sems:
    def __init__(self, send, recv, near, set_size):
        self.set_size = set_size
        self.send, self.recv, self.near = send, recv, near
        self.far_used = self.near_used = 0
        self.spare = []

    def take_set(self):
        if self.spare:
            return self.spare.pop(0)
        first = self.far_used
        self.far_used += self.set_size
        return first

    def far(self, src, dst, device, index=None):
        if index is None:
            index = self.far_used
            self.far_used += 1
        return pltpu.make_async_remote_copy(
            src_ref=src,
            dst_ref=dst,
            send_sem=self.send.at[index],
            recv_sem=self.recv.at[index],
            device_id=device,
            device_id_type=MESH,
        )

    def local(self, src, dst):
        index = self.near_used
        self.near_used += 1
        return pltpu.make_async_copy(src, dst, self.near.at[index])


class Clock:
    QUEUE = 3.0

    def __init__(self):
        self.now = 0.0
        self.free = {"core": 0.0, "x": 0.0, "y": 0.0, "z": 0.0}

    def transfer(self, loads):
        end = 0.0
        for link, load in loads.items():
            begin = max(self.free[link], self.now)
            self.free[link] = begin + load
            end = max(end, self.free[link] + (0.9 if link == "core" else 2.6))
        return end

    def opens(self, loads):
        return max([self.free[link] - self.QUEUE for link in loads], default=0.0)


FAR_SEMS = 149
NEAR_SEMS = 44


def fused_kernel(
    levels,
    tok_ref,
    starts_hbm,
    flags_hbm,
    valid_hbm,
    win_hbm,
    wout_hbm,
    wup_hbm,
    wdn_hbm,
    gains_hbm,
    biases_hbm,
    og_hbm,
    lo_hbm,
    ig_hbm,
    gin_hbm,
    gsq_hbm,
    small_ref,
    kept_hbm,
    starts_ref,
    flags_ref,
    valid_ref,
    gains_ref,
    biases_ref,
    win,
    wout,
    wup,
    wdn,
    low,
    outer,
    keys,
    values,
    turned,
    query_low,
    query_t,
    weights_t,
    attended_t,
    attended_low,
    inverse_total,
    normed_one,
    normed_two,
    inverse_norm,
    hidden_low,
    active_low,
    slope_low,
    scores,
    mask,
    flow,
    grad_low_t,
    grad_low,
    query_grad_t,
    give,
    take,
    meta,
    meta_sent,
    small,
    small_in,
    small_z,
    *rest,
):
    square_sum, wide_sum = rest[:8], rest[8:16]
    send_sems, recv_sems, near_sems = rest[16:]
    rows, model = low.shape[1], low.shape[2]
    length = 2 * rows
    pairs = HEADS // 2
    d = lax.axis_index("dp")
    x = lax.axis_index("seq")
    core = lax.rem(d, 2)
    y = lax.rem(lax.div(d, 2), 2)
    z = lax.div(d, 4)
    to_core = (d + 1 - 2 * core, x)
    to_x = (d, 1 - x)
    to_y = (d + 2 - 4 * y, x)
    to_diag = (d + 1 - 2 * core, 1 - x)

    def at_z(level):
        return (d + (level - z) * 4, x)

    z_next = [lax.rem(z + step, levels) for step in range(1, levels)]
    sems = Sems(send_sems, recv_sems, near_sems, 6 + 2 * (levels - 1))
    barrier = pltpu.get_barrier_semaphore()
    peers = [to_core, to_x, to_y, to_diag] + [at_z(level) for level in z_next]
    for peer in peers:
        pl.semaphore_signal(barrier, inc=1, device_id=peer, device_id_type=MESH)

    def load(pairs_of):
        copies = [sems.local(src, dst) for src, dst in pairs_of]
        for copy in copies:
            copy.start()
        return copies

    row_loads = load(
        [(starts_hbm, starts_ref), (flags_hbm, flags_ref), (valid_hbm, valid_ref)]
    )
    shift_loads = load([(gains_hbm, gains_ref), (biases_hbm, biases_ref)])
    moved = core != x
    away_low = sems.far(tok_ref.at[0], low.at[0], to_diag)
    away_outer = sems.far(og_hbm.at[0], outer, to_diag)
    away_meta = sems.far(meta_sent, meta, to_diag)
    stay_low = sems.local(tok_ref.at[0], low.at[0])
    stay_outer = sems.local(og_hbm.at[0], outer)

    for copy in row_loads:
        copy.wait()
    position = lax.broadcasted_iota(jnp.int32, (1, length), 1)
    segment = jnp.zeros((1, length), jnp.int32) - 1
    for cell in range(starts_ref.shape[1]):
        segment = segment + (position >= starts_ref[0:1, cell : cell + 1]).astype(jnp.int32)
    good = valid_ref[...] * (1 - flags_ref[...]) > 0
    meta_sent[...] = jnp.zeros_like(meta_sent)
    meta_sent[0:1, :] = jnp.where(good, segment, -1).astype(F32)
    meta_sent[1:2, :] = segment.astype(F32)
    meta_sent[2:3, :] = valid_ref[...].astype(F32)

    pl.semaphore_wait(barrier, len(peers))

    @pl.when(moved)
    def _():
        away_meta.start()
        away_low.start()

    @pl.when(jnp.logical_not(moved))
    def _():
        stay_low.start()
        meta[...] = meta_sent[...]

    weight_loads = []
    for layer in range(LAYERS):
        weight_loads.append(
            [
                load([(win_hbm.at[layer], win.at[layer])])[0],
                load([(wout_hbm.at[layer], wout.at[layer])])[0],
                load([(wup_hbm.at[layer], wup.at[layer])])[0],
                load([(wdn_hbm.at[layer], wdn.at[layer])])[0],
            ]
        )

    small[...] = jnp.zeros_like(small)
    for copy in shift_loads:
        copy.wait()

    @pl.when(moved)
    def _():
        away_meta.wait()

    near = meta[:, pl.ds(pl.multiple_of(core * rows, 128), rows)]
    far = meta[:, pl.ds(pl.multiple_of((1 - core) * rows, 128), rows)]
    near_t, far_t = near.T, far.T
    same = lax.broadcasted_iota(jnp.int32, (rows, rows), 0) == lax.broadcasted_iota(
        jnp.int32, (rows, rows), 1
    )
    mask[0:rows, :] = jnp.where((near_t[:, 0:1] == near[1:2, :]) | same, 0.0, NEG)
    mask[rows:length, :] = jnp.where(far_t[:, 0:1] == near[1:2, :], 0.0, NEG)
    valid_column = near_t[:, 2:3]
    small[0, 24:25, :] = near[2:3, :]

    @pl.when(moved)
    def _():
        away_low.wait()
        away_outer.start()

    @pl.when(jnp.logical_not(moved))
    def _():
        stay_low.wait()
        stay_outer.start()

    def note_square(layer, which, value):
        row = 18 + 3 * layer + which
        small[0, row : row + 1, :] = column_sum(value * value * valid_column)

    staged = square_sum[0].at[3 * LAYERS - 1]
    spills = []
    flow[...] = low[0].astype(F32)
    for layer in range(LAYERS):
        bias = [biases_ref[k, layer : layer + 1, :] for k in range(7)]
        gain = [gains_ref[layer, k : k + 1, :] for k in range(2)]
        load_in, load_out, load_up, load_down = weight_loads[layer]
        load_in.wait()
        stream_low = low[layer]
        note_square(layer, 0, flow[...])
        keys[layer, 0:rows, :] = nn(stream_low, win[layer, :, model : 2 * model]).astype(LOW)
        send_keys = sems.far(
            keys.at[layer, pl.ds(0, rows)], keys.at[layer, pl.ds(rows, rows)], to_core
        )
        send_keys.start()
        values[layer, 0:rows, :] = (
            nn(stream_low, win[layer, :, 2 * model : 3 * model]) + bias[1]
        ).astype(LOW)
        send_values = sems.far(
            values.at[layer, pl.ds(0, rows)], values.at[layer, pl.ds(rows, rows)], to_core
        )
        send_values.start()
        query = nn(stream_low, win[layer, :, 0:model]) + bias[0]
        query_low[layer] = (query * (SCALE / math.log(2.0))).astype(LOW)
        query_t[layer] = query_low[layer].T
        turned[:, 0:rows] = values[layer, 0:rows, :].T
        def score(head, begin=0, end=length, layer=layer):
            pair = head // 2
            scores[head % 2, begin:end] = (
                nn(
                    keys[layer, begin:end, 128 * pair : 128 * pair + 128],
                    pad_head(query_t[layer, 64 * head : 64 * head + 64, :], head % 2),
                )
                + mask[begin:end]
            )

        score(0, 0, rows)
        send_keys.wait()
        score(0, rows, length)
        for head in range(HEADS):
            if head + 1 < HEADS:
                score(head + 1)
            if head == 0:
                send_values.wait()
                turned[:, rows:length] = values[layer, rows:length, :].T
            if layer > 0:
                spills[layer - 1][head].wait()
            block = scores[head % 2]
            best = jnp.max(block, axis=0, keepdims=True)
            weight = jnp.exp2(block - best)
            inverse = 1.0 / jnp.sum(weight, axis=0, keepdims=True)
            weight_low = weight.astype(LOW)
            weights_t[head] = weight_low
            span = slice(64 * head, 64 * head + 64)
            inverse_total[layer, head : head + 1, :] = inverse
            attended_t[layer, span, :] = nn(turned[span, :], weight_low) * inverse
            if layer + 1 < LAYERS:
                if head == 0:
                    spills.append([])
                copy = sems.local(weights_t.at[head], kept_hbm.at[layer, head])
                copy.start()
                spills[layer].append(copy)
        attended_low[layer] = attended_t[layer].T.astype(LOW)
        load_out.wait()
        branch = nn(attended_low[layer], wout[layer]) + bias[2]
        note_square(layer, 1, branch)
        total = flow[...] + branch
        centred = total - jnp.mean(total, axis=-1, keepdims=True)
        inverse = lax.rsqrt(jnp.mean(centred * centred, axis=-1, keepdims=True) + EPS)
        normed = centred * inverse
        normed_one[layer] = normed.astype(LOW)
        inverse_norm[:, 2 * layer : 2 * layer + 1] = inverse
        hidden = normed * gain[0] + bias[5]
        flow[...] = hidden
        hidden_low[layer] = hidden.astype(LOW)
        load_up.wait()
        inner = nn(hidden_low[layer], wup[layer]) + bias[3]
        share = 0.5 * (1.0 + lax.erf(inner * 0.7071067811865476))
        active_low[layer] = (inner * share).astype(LOW)
        slope_low[layer] = (
            share + inner * jnp.exp(-0.5 * inner * inner) * 0.3989422804014327
        ).astype(LOW)
        load_down.wait()
        ff_out = nn(active_low[layer], wdn[layer]) + bias[4]
        note_square(layer, 2, ff_out)
        total = flow[...] + ff_out
        centred = total - jnp.mean(total, axis=-1, keepdims=True)
        inverse = lax.rsqrt(jnp.mean(centred * centred, axis=-1, keepdims=True) + EPS)
        normed = centred * inverse
        normed_two[layer] = normed.astype(LOW)
        inverse_norm[:, 2 * layer + 1 : 2 * layer + 2] = inverse
        result = normed * gain[1] + bias[6]
        if layer + 1 < LAYERS:
            flow[...] = result
            low[layer + 1] = result.astype(LOW)
        else:
            staged[...] = result.astype(LOW).reshape(staged.shape)

    away_result = [
        sems.far(staged.at[i, j], lo_hbm.at[i, j], to_diag) for i in range(2) for j in range(2)
    ]
    stay_result = sems.local(staged, lo_hbm)
    strips = [pl.ds(rows // 4 * k, rows // 4) for k in range(4)]
    away_grad = [sems.far(outer.at[strip], ig_hbm.at[0, strip], to_diag) for strip in strips]
    stay_grad = sems.local(outer, ig_hbm.at[0])

    @pl.when(moved)
    def _():
        away_outer.wait()

    @pl.when(jnp.logical_not(moved))
    def _():
        stay_outer.wait()
        stay_result.start()

    piece = model // 8 // levels
    own_rows = pl.ds(pl.multiple_of(z * piece, piece), piece)
    clock = Clock()

    def reduce_chunk(buffers, begin, count, home):
        return loads_of(buffers, count), steps_of(buffers, begin, count, home)

    def share_of(width):
        return width // 256 * 128

    def loads_of(buffers, count):
        width = buffers[0].shape[-1]
        size = count * width / model
        part = share_of(width) / width
        first = {"x": 2.88 * part * size, "y": 2.88 * (1 - part) * size}
        second = {"x": 1.44 * (1 - part) * size, "y": 1.44 * part * size}
        core_load, z_load = {"core": 0.46 * size}, {"z": 1.35 * size}
        return [core_load, first, second, z_load, z_load, second, first, core_load]

    def steps_of(buffers, begin, count, home):
        mine, whole, take_core, take_x, take_y, take_ay, take_bx, take_z = buffers
        width = mine.shape[-1]
        some = pl.ds(begin, count)
        landed = pl.ds(begin % take_core.shape[0], count)
        split = share_of(width)
        left, right = pl.ds(0, split), pl.ds(split, width - split)
        every = slice(None)
        first = sems.take_set()

        def send(src, dst, peer, index):
            copy = sems.far(src, dst, peer, first + index)
            copy.start()
            return copy

        def send_same(at, peer, index):
            return send(whole.at[at], whole.at[at], peer, index)

        def add_into(at, value):
            mine[at] = mine[at] + value

        def finish(copies):
            for copy in copies:
                copy.wait()

        mine_core, mine_left, mine_right = (
            (some, core),
            (some, core, x, every, every, left),
            (some, core, every, y, every, right),
        )
        deep_left, deep_right = (some, core, x, y, every, left), (some, core, x, y, every, right)
        own = (some, core, x, y, own_rows)
        by_core, by_x, by_y, by_y_deep, by_x_deep, back_core, by_z = 0, 1, 2, 3, 4, 5, 6
        back_z = by_z + levels - 1

        flight = [send(mine.at[some, 1 - core], take_core.at[landed], to_core, by_core)]
        yield
        finish(flight)
        add_into(mine_core, take_core[landed])
        flight = [
            send(mine.at[some, core, 1 - x, every, every, left], take_x.at[some], to_x, by_x),
            send(mine.at[some, core, every, 1 - y, every, right], take_y.at[some], to_y, by_y),
        ]
        yield
        finish(flight)
        add_into(mine_left, take_x[some])
        add_into(mine_right, take_y[some])
        flight = [
            send(mine.at[some, core, x, 1 - y, every, left], take_ay.at[some], to_y, by_y_deep),
            send(mine.at[some, core, 1 - x, y, every, right], take_bx.at[some], to_x, by_x_deep),
        ]
        yield
        finish(flight)
        add_into(deep_left, take_ay[some])
        add_into(deep_right, take_bx[some])
        flight = [
            send(
                mine.at[some, core, x, y, pl.ds(pl.multiple_of(level * piece, piece), piece)],
                take_z.at[step, some],
                at_z(level),
                by_z + step,
            )
            for step, level in enumerate(z_next)
        ]
        yield
        finish(flight)
        total = mine[own].astype(F32)
        for step in range(levels - 1):
            total = total + take_z[step, some].astype(F32)
        whole[own[:1] + own[2:]] = total.astype(LOW)
        flight = [
            send_same(own[:1] + own[2:], at_z(level), back_z + step)
            for step, level in enumerate(z_next)
        ]
        yield
        finish(flight)
        flight = [
            send_same((some, x, y, every, left), to_y, by_y),
            send_same((some, x, y, every, right), to_x, by_x),
        ]
        yield
        finish(flight)
        flight = [
            send_same((some, x, every, every, left), to_x, by_x_deep),
            send_same((some, every, y, every, right), to_y, by_y_deep),
        ]
        yield
        finish(flight)
        flight = [send(whole.at[some], home, to_core, back_core)]
        copy = sems.local(whole.at[some], home)
        copy.start()
        homing.append(copy)
        yield
        finish(flight)
        sems.spare.append(first)

    def send_home(copies):
        for copy in copies:
            pl.when(moved)(copy.start)
            yield
        for copy in copies:
            pl.when(moved)(copy.wait)

    def reduce_small():
        for step, peer in enumerate((to_core, to_x, to_y)):
            copy = sems.far(small.at[step], small_in.at[step], peer)
            copy.start()
            yield
            copy.wait()
            small[step + 1] = small[step] + small_in[step]
        copies = [sems.far(small.at[3], small_z.at[z], at_z(level)) for level in z_next]
        for copy in copies:
            copy.start()
        small_z[z] = small[3]
        yield
        for copy in copies:
            copy.wait()
        total = small_z[0]
        for level in range(1, levels):
            total = total + small_z[level]
        small_in[0] = total
        copy = sems.local(small_in.at[0], small_ref)
        copy.start()
        homing.append(copy)

    homing = []
    active = []

    def advance(entry):
        loads = entry[2]
        if next(entry[1], True):
            active.remove(entry)
            clock.now += 0.1
        else:
            clock.now += 0.25
            entry[0] = clock.transfer(loads.pop(0))

    def begin(chunk):
        loads, steps = chunk
        entry = [0.0, steps, loads, True]
        active.append(entry)
        advance(entry)

    def begin_home(copies):
        entry = [clock.now, send_home(copies), [{"x": 1.45} for _ in copies], False]
        active.append(entry)
        return entry

    def when(entry):
        if not entry[2]:
            return entry[0]
        if not entry[3]:
            return max(clock.now, clock.free["x"] - HOME_QUEUE)
        return max(entry[0], clock.opens(entry[2][0]))

    def pump(spent):
        clock.now += spent
        while True:
            ready = [entry for entry in active if when(entry) <= clock.now]
            if not ready:
                return
            advance(max(ready, key=lambda entry: (entry[3], len(entry[2]))))

    def note(row, value):
        small[0, row : row + 1, :] = value

    reloads = []
    result_home = begin_home(away_result)
    flow[...] = outer[...].astype(F32)
    for layer in reversed(range(LAYERS)):
        gain = [gains_ref[layer, k : k + 1, :] for k in range(2)]
        base = 3 * (LAYERS - 1 - layer)
        wide = pairs * (LAYERS - 1 - layer)
        mine = square_sum[0]
        folded = mine.shape[1:]
        bias_row = 4 + 7 * layer
        turned[...] = keys[layer].T
        grad = flow[...]
        normed = normed_two[layer].astype(F32)
        note(2 * layer + 1, column_sum(grad * normed))
        note(bias_row + 6, column_sum(grad))
        scaled = grad * gain[1]
        second = inverse_norm[:, 2 * layer + 1 : 2 * layer + 2] * (
            scaled
            - jnp.mean(scaled, axis=-1, keepdims=True)
            - normed * jnp.mean(scaled * normed, axis=-1, keepdims=True)
        )
        scores[0, 0:rows, :] = second
        down_low = second.astype(LOW)
        note(bias_row + 4, column_sum(down_low))
        mine[base] = tn(active_low[layer], down_low).astype(LOW).reshape(folded)
        inner_low = (nt(down_low, wdn[layer]) * slope_low[layer].astype(F32)).astype(LOW)
        note(bias_row + 3, column_sum(inner_low))
        mine[base + 1] = tn(hidden_low[layer], inner_low).astype(LOW).reshape(folded)
        pump(2.6)
        begin(
            reduce_chunk(
                square_sum,
                base,
                2,
                gsq_hbm.at[layer, pl.ds(0, 2), core],
            )
        )
        grad = scores[0, 0:rows, :] + nt(inner_low, wup[layer])
        normed = normed_one[layer].astype(F32)
        note(2 * layer, column_sum(grad * normed))
        note(bias_row + 5, column_sum(grad))
        scaled = grad * gain[0]
        flow[...] = inverse_norm[:, 2 * layer : 2 * layer + 1] * (
            scaled
            - jnp.mean(scaled, axis=-1, keepdims=True)
            - normed * jnp.mean(scaled * normed, axis=-1, keepdims=True)
        )
        branch_low = flow[...].astype(LOW)
        note(bias_row + 2, column_sum(branch_low))
        mine[base + 2] = tn(attended_low[layer], branch_low).astype(LOW).reshape(folded)
        pump(1.2)
        begin(
            reduce_chunk(square_sum, base + 2, 1, gsq_hbm.at[layer, pl.ds(2, 1), core])
        )
        attended_grad_t = nt(branch_low, wout[layer]).astype(LOW).T
        for head in range(HEADS):
            span = slice(64 * head, 64 * head + 64)
            grad_low_t[span, :] = (
                attended_grad_t[span, :].astype(F32) * inverse_total[layer, head : head + 1, :]
            ).astype(LOW)
        grad_low[...] = grad_low_t[...].T
        pump(1.0)
        gives = []

        def close_pairs(chosen, layer=layer, wide=wide, bias_row=bias_row, gives=gives):
            mine = wide_sum[0]
            parts = []
            for pair in chosen:
                side = slice(128 * pair, 128 * pair + 128)
                gives[pair].wait()
                taken = [take[layer, pair, which].astype(F32) for which in range(2)]
                three = [
                    query_grad_t[side, :].T,
                    (mask[0:rows, side] + taken[0]).astype(LOW),
                    (mask[rows:length, side] + taken[1]).astype(LOW),
                ]
                small[0, bias_row : bias_row + 1, side] = column_sum(three[0])
                small[0, bias_row + 1 : bias_row + 2, side] = column_sum(three[2])
                parts += three
            part = jnp.concatenate(parts, axis=1)
            product = tn(low[layer], part).astype(LOW)
            for k, pair in enumerate(chosen):
                slot = wide + pair
                mine[slot] = product[:, 384 * k : 384 * k + 384].reshape(mine.shape[1:])
            first, count = wide + chosen[0], len(chosen)
            home = gin_hbm.at[layer, pl.ds(chosen[0], count), core]
            pump(0.4 * count)
            begin(reduce_chunk(wide_sum, first, count, home))
            weight = jnp.concatenate(
                [
                    win[layer, :, model * k + 128 * pair : model * k + 128 * pair + 128]
                    for pair in chosen
                    for k in range(3)
                ],
                axis=1,
            )
            total = flow[...] + nt(part, weight)
            if layer > 0 or chosen[-1] < pairs - 1:
                flow[...] = total
            else:
                outer[...] = total.astype(LOW)

        first_half = lax.broadcasted_iota(jnp.int32, (1, 128), 1) < HEAD_DIM
        for head in range(HEADS):
            pair = head // 2
            span = slice(64 * head, 64 * head + 64)
            lanes = slice(128 * pair, 128 * pair + 128)
            grad_part = grad_low_t[span, :]
            delta = column_sum(grad_part.astype(F32) * attended_t[layer, span, :])
            if layer + 1 < LAYERS:
                reloads[head].wait()
            prob_grad = nn(values[layer, :, lanes], pad_head(grad_part, head % 2))
            score_grad = (weights_t[head].astype(F32) * (prob_grad - delta)).astype(LOW)
            query_grad_t[span, :] = (nn(turned[span, :], score_grad) * SCALE).astype(LOW)
            key_part = nn(score_grad, query_low[layer, :, lanes])
            value_part = nn(weights_t[head], grad_low[:, lanes])
            if head % 2 == 0:
                key_even, value_even = key_part, value_part
            else:
                key_grad = jnp.where(first_half, key_even, key_part) * math.log(2.0)
                value_grad = jnp.where(first_half, value_even, value_part)
                mask[0:rows, lanes] = key_grad[0:rows]
                mask[rows:length, lanes] = value_grad[0:rows]
                give[pair, 0] = key_grad[rows:length].astype(LOW)
                give[pair, 1] = value_grad[rows:length].astype(LOW)
                copy = sems.far(give.at[pair], take.at[layer, pair], to_core)
                copy.start()
                gives.append(copy)
            if layer > 0:
                copy = sems.local(kept_hbm.at[layer - 1, head], weights_t.at[head])
                copy.start()
                reloads.append(copy)
            pump(1.15)
            if layer > 0 and head == HEADS // 2:
                close_pairs([0, 1])
            if layer == 0 and head % 2 == 0 and head > 0:
                close_pairs([pair - 1])
        close_pairs([2, 3] if layer > 0 else [3])
        if layer == 0:
            begin(([{"core": 0.1}, {"x": 1.5}, {"y": 1.5}, {"z": 2.0}], reduce_small()))
        if layer > 0:

            while result_home in active:
                advance(result_home)

            @pl.when(jnp.logical_not(moved))
            def _():
                stay_result.wait()

        pump(0.4)

    begin_home(away_grad)

    @pl.when(jnp.logical_not(moved))
    def _():
        stay_grad.start()

    while active:
        clock.now = max(clock.now, min(when(entry) for entry in active))
        pump(0.0)
    for copy in homing:
        copy.wait()

    @pl.when(jnp.logical_not(moved))
    def _():
        stay_grad.wait()

    assert sems.far_used <= FAR_SEMS and sems.near_used <= NEAR_SEMS


def local_pair(
    tokens,
    cell_starts,
    generate_flags,
    valid_mask,
    in_weight,
    out_weight,
    up_weight,
    down_weight,
    norm_gains,
    biases,
    out_grad,
):
    rows, model = tokens.shape[1:]
    length = 2 * rows
    levels = lax.axis_size("dp") // 4
    eighth = model // 8
    folded = (2, 2, 2, eighth)

    def sum_buffers(count, shared, width):
        split = width // 256 * 128
        return [
            pltpu.VMEM((count,) + folded + (width,), LOW),
            pltpu.VMEM((count,) + folded[1:] + (width,), LOW),
            pltpu.VMEM((shared,) + folded[1:] + (width,), LOW),
            pltpu.VMEM((count, 2, eighth, split), LOW),
            pltpu.VMEM((count, 2, eighth, width - split), LOW),
            pltpu.VMEM((count, eighth, split), LOW),
            pltpu.VMEM((count, eighth, width - split), LOW),
            pltpu.VMEM((max(levels - 1, 1), count, eighth // levels, width), LOW),
        ]

    shape = jax.ShapeDtypeStruct
    anywhere = pl.BlockSpec(memory_space=pl.ANY)
    by_layer = (LAYERS, rows, model)
    scratch = [
        pltpu.VMEM(cell_starts.shape, jnp.int32),
        pltpu.VMEM(generate_flags.shape, jnp.int32),
        pltpu.VMEM(valid_mask.shape, jnp.int32),
        pltpu.VMEM(norm_gains.shape, F32),
        pltpu.VMEM((7, LAYERS, model), F32),
        pltpu.VMEM(in_weight.shape, LOW),
        pltpu.VMEM(out_weight.shape, LOW),
        pltpu.VMEM(up_weight.shape, LOW),
        pltpu.VMEM(down_weight.shape, LOW),
        pltpu.VMEM(by_layer, LOW),
        pltpu.VMEM((rows, model), LOW),
        pltpu.VMEM((LAYERS, length, model), LOW),
        pltpu.VMEM((LAYERS, length, model), LOW),
        pltpu.VMEM((model, length), LOW),
        pltpu.VMEM(by_layer, LOW),
        pltpu.VMEM((LAYERS, model, rows), LOW),
        pltpu.VMEM((HEADS, length, rows), LOW),
        pltpu.VMEM((LAYERS, model, rows), F32),
        pltpu.VMEM(by_layer, LOW),
        pltpu.VMEM((LAYERS, HEADS, rows), F32),
        pltpu.VMEM(by_layer, LOW),
        pltpu.VMEM(by_layer, LOW),
        pltpu.VMEM((rows, 2 * LAYERS), F32),
        pltpu.VMEM(by_layer, LOW),
        pltpu.VMEM(by_layer, LOW),
        pltpu.VMEM(by_layer, LOW),
        pltpu.VMEM((2, length, rows), F32),
        pltpu.VMEM((length, rows), F32),
        pltpu.VMEM((rows, model), F32),
        pltpu.VMEM((model, rows), LOW),
        pltpu.VMEM((rows, model), LOW),
        pltpu.VMEM((model, rows), LOW),
        pltpu.VMEM((HEADS // 2, 2, rows, 128), LOW),
        pltpu.VMEM((LAYERS, HEADS // 2, 2, rows, 128), LOW),
        pltpu.VMEM((8, length), F32),
        pltpu.VMEM((8, length), F32),
        pltpu.VMEM((4, SMALL_ROWS, model), F32),
        pltpu.VMEM((3, SMALL_ROWS, model), F32),
        pltpu.VMEM((levels, SMALL_ROWS, model), F32),
        *sum_buffers(3 * LAYERS, 3, model),
        *sum_buffers(HEADS // 2 * LAYERS, HEADS // 2, 384),
        pltpu.SemaphoreType.DMA((FAR_SEMS,)),
        pltpu.SemaphoreType.DMA((FAR_SEMS,)),
        pltpu.SemaphoreType.DMA((NEAR_SEMS,)),
    ]
    lo, ig, gin, gsq, small, _ = pl.pallas_call(
        functools.partial(fused_kernel, levels),
        out_shape=[
            shape(folded + (model,), LOW),
            shape(tokens.shape, LOW),
            shape((LAYERS, HEADS // 2) + folded + (384,), LOW),
            shape((LAYERS, 3) + folded + (model,), LOW),
            shape((SMALL_ROWS, model), F32),
            shape((LAYERS - 1, HEADS, length, rows), LOW),
        ],
        in_specs=[anywhere] * 11,
        out_specs=[anywhere] * 6,
        scratch_shapes=scratch,
        compiler_params=pltpu.CompilerParams(
            collective_id=0, has_side_effects=True, vmem_limit_bytes=VMEM_BYTES
        ),
    )(
        tokens,
        cell_starts,
        generate_flags,
        valid_mask,
        in_weight,
        out_weight,
        up_weight,
        down_weight,
        norm_gains,
        biases.transpose(1, 0, 2),
        out_grad,
    )
    return finish(tokens, in_weight, lo, ig, gin, gsq, small)


VMEM_BYTES = 63 * 1024 * 1024


def finish_kernel(model, *refs):
    lo_in, ig_in, gin_in, gsq_in, small = refs[:5]
    lo, ig, gin, gout, gup, gdn, gains, shifts, rms = refs[5:14]
    low_wide, wide, low_square, square, passing, in_sems, out_sems = refs[14:]
    pairs = gin_in.shape[1]
    reads, writes = [], []

    def read(src, dst):
        copy = pltpu.make_async_copy(src, dst, in_sems.at[len(reads)])
        copy.start()
        reads.append(copy)
        return copy

    def write(src, dst):
        copy = pltpu.make_async_copy(src, dst, out_sems.at[len(writes)])
        copy.start()
        writes.append(copy)

    def widen_square(slot, copy, target):
        copy.wait()
        square[slot] = low_square[slot].astype(F32)
        write(square.at[slot], target)

    reads_lo = read(lo_in, passing)
    reads_square, reads_wide = [], []
    for layer in range(LAYERS):
        for k in range(3):
            reads_square.append(read(gsq_in.at[layer, k], low_square.at[3 * layer + k]))
            if k == 0:
                for pair in range(pairs):
                    reads_wide.append(
                        read(gin_in.at[layer, pair], low_wide.at[pairs * layer + pair])
                    )
    reads_ig = read(ig_in.at[0], low_square.at[3 * LAYERS])
    for layer in range(LAYERS):
        for k in range(2):
            row = 2 * layer + k
            gains[layer, k : k + 1, :] = small[row : row + 1, :]
        for k in range(7):
            row = 2 * LAYERS + 7 * layer + k
            shifts[k, layer : layer + 1, :] = small[row : row + 1, :]
    first = 9 * LAYERS
    count = jnp.sum(small[first + 3 * LAYERS : first + 3 * LAYERS + 1, :], keepdims=True)
    line = lax.broadcasted_iota(jnp.int32, rms.shape, 0)
    place = lax.broadcasted_iota(jnp.int32, rms.shape, 1)
    squares = jnp.zeros(rms.shape, F32)
    for layer in range(LAYERS):
        for k in range(3):
            row = first + 3 * layer + k
            value = jnp.sum(small[row : row + 1, :], keepdims=True)
            squares = jnp.where((line == layer) & (place == k), value, squares)
    rms[...] = jnp.sqrt(squares / (count * model))
    reads_lo.wait()
    write(passing, lo)
    for layer in range(LAYERS):
        for k, target in enumerate((gdn, gup, gout)):
            slot = 3 * layer + k
            widen_square(slot, reads_square[slot], target.at[layer])
            if k == 0:
                for pair in range(pairs):
                    slot = pairs * layer + pair
                    reads_wide[slot].wait()
                    for part in range(3):
                        begin = model * part + 128 * pair
                        wide[layer, :, begin : begin + 128] = low_wide[
                            slot, :, 128 * part : 128 * part + 128
                        ].astype(F32)
                write(wide.at[layer], gin.at[layer])
    widen_square(3 * LAYERS, reads_ig, ig.at[0])
    for copy in writes:
        copy.wait()


def finish(tokens, in_weight, lo, ig, gin, gsq, small):
    rows, model = tokens.shape[1:]
    shape = jax.ShapeDtypeStruct
    vmem, far = pl.BlockSpec(memory_space=pltpu.VMEM), pl.BlockSpec(memory_space=pltpu.HBM)
    square = (LAYERS, model, model)
    slots = LAYERS * HEADS // 2
    outs = pl.pallas_call(
        functools.partial(finish_kernel, model),
        out_shape=[
            shape(tokens.shape, LOW),
            shape(tokens.shape, F32),
            shape(in_weight.shape, F32),
            shape(square, F32),
            shape(square, F32),
            shape(square, F32),
            shape((LAYERS, 2, model), F32),
            shape((7, LAYERS, model), F32),
            shape((LAYERS, 3), F32),
        ],
        in_specs=[far] * 4 + [vmem],
        out_specs=[far] * 6 + [vmem] * 3,
        scratch_shapes=[
            pltpu.VMEM((slots, model, 384), LOW),
            pltpu.VMEM(in_weight.shape, F32),
            pltpu.VMEM((3 * LAYERS + 1, model, model), LOW),
            pltpu.VMEM((3 * LAYERS + 1, model, model), F32),
            pltpu.VMEM(tokens.shape, LOW),
            pltpu.SemaphoreType.DMA((slots + 3 * LAYERS + 2,)),
            pltpu.SemaphoreType.DMA((4 * LAYERS + 2,)),
        ],
        compiler_params=pltpu.CompilerParams(vmem_limit_bytes=VMEM_BYTES),
    )(
        lo.reshape(tokens.shape),
        ig,
        gin.reshape(LAYERS, HEADS // 2, model, 384),
        gsq.reshape(LAYERS, 3, model, model),
        small,
    )
    lo, ig, gin, gout, gup, gdn, gains, shifts, rms = outs
    return lo, ig, gin, gout, gup, gdn, gains, shifts.transpose(1, 0, 2), rms


def solution(mesh):
    placed = (
        P("dp", "seq", None),
        P("dp", None),
        P("dp", None),
        P("dp", None),
        P(),
        P(),
        P(),
        P(),
        P(),
        P(),
        P("dp", "seq", None),
    )
    paired = mesh.shape["seq"] == 2 and mesh.shape["dp"] % 4 == 0
    return jax.shard_map(
        local_pair if paired else local,
        mesh=mesh,
        in_specs=placed,
        out_specs=(P("dp", "seq", None), P("dp", "seq", None), P(), P(), P(), P(), P(), P(), P()),
        check_vma=False,
    )
```

```python
import functools
import math

import jax
import jax.numpy as jnp
from jax import lax
from jax.experimental import pallas as pl
from jax.experimental.pallas import tpu as pltpu
from jax.sharding import PartitionSpec as P

HEADS = 8
HEAD_DIM = 64
LAYERS = 2


EPS = 1e-05
NEG = -1e30


def block_width(count):
    for option in range(1024, 255, -1):
        if count % option == 0:
            return option
    return count


def segment_ids(starts_row, positions):
    return jnp.sum((positions[:, None] >= starts_row[None, :]).astype(jnp.int32), axis=1) - 1


def norm_rows(total, gain, shift):
    mean = jnp.mean(total, axis=-1, keepdims=True)
    centred = total - mean
    spread = jnp.mean(centred * centred, axis=-1, keepdims=True)
    inverse = lax.rsqrt(spread + EPS)
    normed = centred * inverse
    return (normed * gain + shift, normed, inverse)


def norm_back(grad, normed, inverse, gain):
    scaled = grad * gain
    return inverse * (
        scaled
        - jnp.mean(scaled, axis=-1, keepdims=True)
        - normed * jnp.mean(scaled * normed, axis=-1, keepdims=True)
    )


def gelu_slope(inner):
    return (
        0.5 * (1.0 + jax.scipy.special.erf(inner * 0.7071067811865476))
        + inner * jnp.exp(-0.5 * inner * inner) * 0.3989422804014327
    )


def make_mask(query_pos, query_seg, starts_row, key_ok_row):

    def mask_for(begin, width):
        key_pos = begin + jnp.arange(width, dtype=jnp.int32)
        key_seg = segment_ids(starts_row, key_pos)
        key_good = lax.dynamic_slice_in_dim(key_ok_row, begin, width, 0) > 0
        return (query_seg[:, None] == key_seg[None, :]) & (
            key_good[None, :] | (query_pos[:, None] == key_pos[None, :])
        )

    return mask_for


def make_attend(query_heads, mask_for, scale):

    def attend(carry, piece, start):
        count = piece.shape[0]
        width = block_width(count)
        model = piece.shape[1] // 2

        def attend_one_block(step, state):
            best, total, summed = state
            begin = step * width
            block = lax.dynamic_slice_in_dim(piece, begin, width, 0)
            key_heads = block[:, :model].reshape(width, HEADS, HEAD_DIM)
            value_heads = block[:, model:].reshape(width, HEADS, HEAD_DIM)
            allowed = mask_for(start + begin, width)[None]
            scores = (
                jnp.einsum(
                    "qhd,khd->hqk", query_heads, key_heads, preferred_element_type=jnp.float32
                )
                * scale
            )
            scores = jnp.where(allowed, scores, NEG)
            new_best = jnp.maximum(best, jnp.max(scores, axis=-1))
            factor = jnp.exp(best - new_best)
            weights = jnp.where(allowed, jnp.exp(scores - new_best[:, :, None]), 0.0)
            total = total * factor + jnp.sum(weights, axis=-1)
            update = jnp.einsum(
                "hqk,khd->qhd",
                weights.astype(jnp.bfloat16),
                value_heads,
                preferred_element_type=jnp.float32,
            )
            summed = summed * factor.T[:, :, None] + update
            return (new_best, total, summed)

        return lax.fori_loop(0, count // width, attend_one_block, carry)

    return attend


def make_back(query_heads, grad_heads, log_total, delta, mask_for, scale):

    def back(carry, piece, start):
        count = piece.shape[0]
        width = block_width(count)
        model = piece.shape[1] // 2

        def back_one_block(step, state):
            query_grad, full_grad = state
            begin = step * width
            block = lax.dynamic_slice_in_dim(piece, begin, width, 0)
            key_heads = block[:, :model].reshape(width, HEADS, HEAD_DIM)
            value_heads = block[:, model:].reshape(width, HEADS, HEAD_DIM)
            allowed = mask_for(start + begin, width)[None]
            scores = (
                jnp.einsum(
                    "qhd,khd->hqk", query_heads, key_heads, preferred_element_type=jnp.float32
                )
                * scale
            )
            probs = jnp.where(allowed, jnp.exp(scores - log_total[:, :, None]), 0.0)
            prob_grad = jnp.einsum(
                "qhd,khd->hqk", grad_heads, value_heads, preferred_element_type=jnp.float32
            )
            score_grad = (probs * (prob_grad - delta[:, :, None])).astype(jnp.bfloat16)
            query_grad = (
                query_grad
                + jnp.einsum(
                    "hqk,khd->qhd", score_grad, key_heads, preferred_element_type=jnp.float32
                )
                * scale
            )
            key_grad = (
                jnp.einsum(
                    "hqk,qhd->khd", score_grad, query_heads, preferred_element_type=jnp.float32
                )
                * scale
            )
            value_grad = jnp.einsum(
                "hqk,qhd->khd",
                probs.astype(jnp.bfloat16),
                grad_heads,
                preferred_element_type=jnp.float32,
            )
            update = jnp.concatenate(
                [key_grad.reshape(width, model), value_grad.reshape(width, model)], axis=1
            )
            place = start + begin
            current = lax.dynamic_slice_in_dim(full_grad, place, width, 0)
            full_grad = lax.dynamic_update_slice_in_dim(full_grad, current + update, place, 0)
            return (query_grad, full_grad)

        return lax.fori_loop(0, count // width, back_one_block, carry)

    return back


def local(
    tokens,
    cell_starts,
    generate_flags,
    valid_mask,
    in_weight,
    out_weight,
    up_weight,
    down_weight,
    norm_gains,
    biases,
    out_grad,
):
    rows = tokens.shape[1]
    model = tokens.shape[2]
    scale = 1.0 / math.sqrt(HEAD_DIM)
    first = lax.axis_index("seq") * rows
    query_pos = first + jnp.arange(rows, dtype=jnp.int32)
    starts_row = cell_starts[0]
    key_ok_row = valid_mask[0] * (1 - generate_flags[0])
    mask_for = make_mask(query_pos, segment_ids(starts_row, query_pos), starts_row, key_ok_row)
    valid_here = lax.dynamic_slice_in_dim(valid_mask[0], first, rows, 0).astype(jnp.float32)
    stream = tokens[0].astype(jnp.float32)
    stream_low = tokens[0]
    kept = []
    squares = []
    for layer in range(LAYERS):
        bias_rows = biases[layer]
        gains_pair = norm_gains[layer]
        mixed = jnp.dot(
            stream_low, in_weight[layer], preferred_element_type=jnp.float32
        ) + jnp.concatenate([bias_rows[0], jnp.zeros((model,), jnp.float32), bias_rows[1]])
        mixed_low = mixed.astype(jnp.bfloat16)
        query_heads = mixed_low[:, :model].reshape(rows, HEADS, HEAD_DIM)
        key_value = mixed_low[:, model:]
        attend = make_attend(query_heads, mask_for, scale)
        state = (
            jnp.full((HEADS, rows), NEG, jnp.float32),
            jnp.zeros((HEADS, rows), jnp.float32),
            jnp.zeros((rows, HEADS, HEAD_DIM), jnp.float32),
        )
        gathered = key_value
        best, total, summed = attend(
            state, lax.all_gather(key_value, "seq", axis=0, tiled=True), jnp.int32(0)
        )
        attended = (summed / total.T[:, :, None]).reshape(rows, model)
        log_total = best + jnp.log(total)
        attended_low = attended.astype(jnp.bfloat16)
        branch = (
            jnp.dot(attended_low, out_weight[layer], preferred_element_type=jnp.float32)
            + bias_rows[2]
        )
        hidden, normed_one, inverse_one = norm_rows(stream + branch, gains_pair[0], bias_rows[5])
        hidden_low = hidden.astype(jnp.bfloat16)
        inner = (
            jnp.dot(hidden_low, up_weight[layer], preferred_element_type=jnp.float32) + bias_rows[3]
        )
        active_low = jax.nn.gelu(inner, approximate=False).astype(jnp.bfloat16)
        ff_out = (
            jnp.dot(active_low, down_weight[layer], preferred_element_type=jnp.float32)
            + bias_rows[4]
        )
        result, normed_two, inverse_two = norm_rows(hidden + ff_out, gains_pair[1], bias_rows[6])
        squares.append(
            jnp.stack(
                [
                    jnp.sum(valid_here * jnp.sum(part * part, axis=-1))
                    for part in (stream, branch, ff_out)
                ]
            )
        )
        kept.append(
            (
                stream_low,
                query_heads,
                gathered,
                attended,
                attended_low,
                log_total,
                normed_one,
                inverse_one,
                hidden_low,
                inner,
                active_low,
                normed_two,
                inverse_two,
            )
        )
        stream = result
        stream_low = result.astype(jnp.bfloat16)
    layer_output = stream.astype(jnp.bfloat16)[None]
    square_local = jnp.stack(squares)
    count_local = jnp.sum(valid_here)
    square_total, count_total = lax.psum((square_local, count_local), ("dp", "seq"))
    grad = out_grad[0].astype(jnp.float32)
    length = rows * lax.axis_size("seq")
    collected = [None] * LAYERS
    for layer in reversed(range(LAYERS)):
        (
            stream_low,
            query_heads,
            gathered,
            attended,
            attended_low,
            log_total,
            normed_one,
            inverse_one,
            hidden_low,
            inner,
            active_low,
            normed_two,
            inverse_two,
        ) = kept[layer]
        gains_pair = norm_gains[layer]
        gain_two = jnp.sum(grad * normed_two, axis=0)
        shift_two = jnp.sum(grad, axis=0)
        second_grad = norm_back(grad, normed_two, inverse_two, gains_pair[1])
        down_grad_low = second_grad.astype(jnp.bfloat16)
        down_bias = jnp.sum(down_grad_low.astype(jnp.float32), axis=0)
        down_matrix_grad = jnp.einsum(
            "tf,td->fd", active_low, down_grad_low, preferred_element_type=jnp.float32
        )
        active_grad = jnp.einsum(
            "td,fd->tf", down_grad_low, down_weight[layer], preferred_element_type=jnp.float32
        )
        inner_grad_low = (active_grad * gelu_slope(inner)).astype(jnp.bfloat16)
        up_bias = jnp.sum(inner_grad_low.astype(jnp.float32), axis=0)
        up_matrix_grad = jnp.einsum(
            "td,tf->df", hidden_low, inner_grad_low, preferred_element_type=jnp.float32
        )
        hidden_grad = second_grad + jnp.einsum(
            "tf,df->td", inner_grad_low, up_weight[layer], preferred_element_type=jnp.float32
        )
        gain_one = jnp.sum(hidden_grad * normed_one, axis=0)
        shift_one = jnp.sum(hidden_grad, axis=0)
        first_grad = norm_back(hidden_grad, normed_one, inverse_one, gains_pair[0])
        branch_grad_low = first_grad.astype(jnp.bfloat16)
        out_bias = jnp.sum(branch_grad_low.astype(jnp.float32), axis=0)
        out_matrix_grad = jnp.einsum(
            "td,te->de", attended_low, branch_grad_low, preferred_element_type=jnp.float32
        )
        attended_grad_low = jnp.einsum(
            "te,de->td", branch_grad_low, out_weight[layer], preferred_element_type=jnp.float32
        ).astype(jnp.bfloat16)
        grad_heads = attended_grad_low.reshape(rows, HEADS, HEAD_DIM)
        delta = jnp.sum(
            (attended_grad_low.astype(jnp.float32) * attended).reshape(rows, HEADS, HEAD_DIM),
            axis=-1,
        ).T
        back = make_back(query_heads, grad_heads, log_total, delta, mask_for, scale)
        state = (
            jnp.zeros((rows, HEADS, HEAD_DIM), jnp.float32),
            jnp.zeros((length, 2 * model), jnp.float32),
        )
        query_grad, full_grad = back(
            state, lax.all_gather(gathered, "seq", axis=0, tiled=True), jnp.int32(0)
        )
        key_value_grad = lax.psum_scatter(
            full_grad.astype(jnp.bfloat16), "seq", scatter_dimension=0, tiled=True
        ).astype(jnp.float32)
        mixed_grad_low = jnp.concatenate(
            [query_grad.reshape(rows, model), key_value_grad], axis=1
        ).astype(jnp.bfloat16)
        query_bias = jnp.sum(mixed_grad_low[:, :model].astype(jnp.float32), axis=0)
        value_bias = jnp.sum(mixed_grad_low[:, 2 * model :].astype(jnp.float32), axis=0)
        in_matrix_grad = jnp.einsum(
            "td,tm->dm", stream_low, mixed_grad_low, preferred_element_type=jnp.float32
        )
        grad = first_grad + jnp.einsum(
            "tm,dm->td", mixed_grad_low, in_weight[layer], preferred_element_type=jnp.float32
        )
        collected[layer] = (
            in_matrix_grad,
            out_matrix_grad,
            up_matrix_grad,
            down_matrix_grad,
            jnp.stack([gain_one, gain_two]),
            jnp.stack([query_bias, value_bias, out_bias, up_bias, down_bias, shift_one, shift_two]),
        )
    in_stack = jnp.stack([collected[layer][0] for layer in range(LAYERS)])
    out_stack = jnp.stack([collected[layer][1] for layer in range(LAYERS)])
    up_stack = jnp.stack([collected[layer][2] for layer in range(LAYERS)])
    down_stack = jnp.stack([collected[layer][3] for layer in range(LAYERS)])
    gains_stack = jnp.stack([collected[layer][4] for layer in range(LAYERS)])
    biases_stack = jnp.stack([collected[layer][5] for layer in range(LAYERS)])
    in_total, out_total, up_total, down_total, gains_total, biases_total = lax.psum(
        (in_stack, out_stack, up_stack, down_stack, gains_stack, biases_stack), ("dp", "seq")
    )
    stream_rms = jnp.sqrt(square_total / (count_total * model))
    return (
        layer_output,
        grad[None],
        in_total,
        out_total,
        up_total,
        down_total,
        gains_total,
        biases_total,
        stream_rms,
    )


MESH = pl.DeviceIdType.MESH
LOW = jnp.bfloat16
F32 = jnp.float32
SMALL_ROWS = 32
HOME_QUEUE = 0.5
SCALE = 1.0 / math.sqrt(HEAD_DIM)


def nn(left, right):
    return lax.dot_general(left, right, (((1,), (0,)), ((), ())), preferred_element_type=F32)


def nt(left, right):
    return lax.dot_general(left, right, (((1,), (1,)), ((), ())), preferred_element_type=F32)


def tn(left, right):
    return lax.dot_general(left, right, (((0,), (0,)), ((), ())), preferred_element_type=F32)


def column_sum(value):
    return jnp.sum(value.astype(F32), axis=0, keepdims=True)


def pad_head(rows, which):
    blank = jnp.zeros_like(rows)
    return jnp.concatenate([rows, blank] if which == 0 else [blank, rows], axis=0)


class Sems:
    def __init__(self, send, recv, near, set_size):
        self.set_size = set_size
        self.send, self.recv, self.near = send, recv, near
        self.far_used = self.near_used = 0
        self.spare = []

    def take_set(self):
        if self.spare:
            return self.spare.pop(0)
        first = self.far_used
        self.far_used += self.set_size
        return first

    def far(self, src, dst, device, index=None):
        if index is None:
            index = self.far_used
            self.far_used += 1
        return pltpu.make_async_remote_copy(
            src_ref=src,
            dst_ref=dst,
            send_sem=self.send.at[index],
            recv_sem=self.recv.at[index],
            device_id=device,
            device_id_type=MESH,
        )

    def local(self, src, dst):
        index = self.near_used
        self.near_used += 1
        return pltpu.make_async_copy(src, dst, self.near.at[index])


class Clock:
    QUEUE = 3.5

    def __init__(self):
        self.now = 0.0
        self.free = {"core": 0.0, "x": 0.0, "y": 0.0, "z": 0.0}

    def transfer(self, loads):
        end = 0.0
        for link, load in loads.items():
            begin = max(self.free[link], self.now)
            self.free[link] = begin + load
            end = max(end, self.free[link] + (0.9 if link == "core" else 2.6))
        return end

    def opens(self, loads):
        return max([self.free[link] - self.QUEUE for link in loads], default=0.0)


FAR_SEMS = 161
NEAR_SEMS = 44


def fused_kernel(
    levels,
    tok_ref,
    starts_hbm,
    flags_hbm,
    valid_hbm,
    win_hbm,
    wout_hbm,
    wup_hbm,
    wdn_hbm,
    gains_hbm,
    biases_hbm,
    og_hbm,
    lo_hbm,
    ig_hbm,
    gin_hbm,
    gsq_hbm,
    small_ref,
    kept_hbm,
    starts_ref,
    flags_ref,
    valid_ref,
    gains_ref,
    biases_ref,
    win,
    wout,
    wup,
    wdn,
    low,
    outer,
    keys,
    values,
    turned,
    query_low,
    query_t,
    weights_t,
    attended_t,
    attended_low,
    inverse_total,
    normed_one,
    normed_two,
    inverse_norm,
    hidden_low,
    active_low,
    slope_low,
    scores,
    mask,
    flow,
    grad_low_t,
    grad_low,
    query_grad_t,
    give,
    take,
    meta,
    meta_sent,
    small,
    small_in,
    small_z,
    *rest,
):
    square_sum, wide_sum = rest[:8], rest[8:16]
    send_sems, recv_sems, near_sems = rest[16:]
    rows, model = low.shape[1], low.shape[2]
    length = 2 * rows
    pairs = HEADS // 2
    d = lax.axis_index("dp")
    x = lax.axis_index("seq")
    core = lax.rem(d, 2)
    y = lax.rem(lax.div(d, 2), 2)
    z = lax.div(d, 4)
    to_core = (d + 1 - 2 * core, x)
    to_x = (d, 1 - x)
    to_y = (d + 2 - 4 * y, x)
    to_diag = (d + 1 - 2 * core, 1 - x)

    def at_z(level):
        return (d + (level - z) * 4, x)

    z_next = [lax.rem(z + step, levels) for step in range(1, levels)]
    sems = Sems(send_sems, recv_sems, near_sems, 6 + 2 * (levels - 1))
    barrier = pltpu.get_barrier_semaphore()
    peers = [to_core, to_x, to_y, to_diag] + [at_z(level) for level in z_next]
    for peer in peers:
        pl.semaphore_signal(barrier, inc=1, device_id=peer, device_id_type=MESH)

    def load(pairs_of):
        copies = [sems.local(src, dst) for src, dst in pairs_of]
        for copy in copies:
            copy.start()
        return copies

    row_loads = load(
        [(starts_hbm, starts_ref), (flags_hbm, flags_ref), (valid_hbm, valid_ref)]
    )
    shift_loads = load([(gains_hbm, gains_ref), (biases_hbm, biases_ref)])
    moved = core != x
    away_low = sems.far(tok_ref.at[0], low.at[0], to_diag)
    away_outer = sems.far(og_hbm.at[0], outer, to_diag)
    away_meta = sems.far(meta_sent, meta, to_diag)
    stay_low = sems.local(tok_ref.at[0], low.at[0])
    stay_outer = sems.local(og_hbm.at[0], outer)

    for copy in row_loads:
        copy.wait()
    position = lax.broadcasted_iota(jnp.int32, (1, length), 1)
    segment = jnp.zeros((1, length), jnp.int32) - 1
    for cell in range(starts_ref.shape[1]):
        segment = segment + (position >= starts_ref[0:1, cell : cell + 1]).astype(jnp.int32)
    good = valid_ref[...] * (1 - flags_ref[...]) > 0
    meta_sent[...] = jnp.zeros_like(meta_sent)
    meta_sent[0:1, :] = jnp.where(good, segment, -1).astype(F32)
    meta_sent[1:2, :] = segment.astype(F32)
    meta_sent[2:3, :] = valid_ref[...].astype(F32)

    pl.semaphore_wait(barrier, len(peers))

    @pl.when(moved)
    def _():
        away_meta.start()
        away_low.start()

    @pl.when(jnp.logical_not(moved))
    def _():
        stay_low.start()
        meta[...] = meta_sent[...]

    weight_loads = []
    for layer in range(LAYERS):
        weight_loads.append(
            [
                load([(win_hbm.at[layer], win.at[layer])])[0],
                load([(wout_hbm.at[layer], wout.at[layer])])[0],
                load([(wup_hbm.at[layer], wup.at[layer])])[0],
                load([(wdn_hbm.at[layer], wdn.at[layer])])[0],
            ]
        )

    small[...] = jnp.zeros_like(small)
    for copy in shift_loads:
        copy.wait()

    @pl.when(moved)
    def _():
        away_meta.wait()

    near = meta[:, pl.ds(pl.multiple_of(core * rows, 128), rows)]
    far = meta[:, pl.ds(pl.multiple_of((1 - core) * rows, 128), rows)]
    near_t, far_t = near.T, far.T
    same = lax.broadcasted_iota(jnp.int32, (rows, rows), 0) == lax.broadcasted_iota(
        jnp.int32, (rows, rows), 1
    )
    mask[0:rows, :] = jnp.where((near_t[:, 0:1] == near[1:2, :]) | same, 0.0, NEG)
    mask[rows:length, :] = jnp.where(far_t[:, 0:1] == near[1:2, :], 0.0, NEG)
    valid_column = near_t[:, 2:3]
    small[0, 24:25, :] = near[2:3, :]

    @pl.when(moved)
    def _():
        away_low.wait()
        away_outer.start()

    @pl.when(jnp.logical_not(moved))
    def _():
        stay_low.wait()
        stay_outer.start()

    def note_square(layer, which, value):
        row = 18 + 3 * layer + which
        small[0, row : row + 1, :] = column_sum(value * value * valid_column)

    staged = square_sum[0].at[3 * LAYERS - 1]
    spills = []
    flow[...] = low[0].astype(F32)
    for layer in range(LAYERS):
        bias = [biases_ref[k, layer : layer + 1, :] for k in range(7)]
        gain = [gains_ref[layer, k : k + 1, :] for k in range(2)]
        load_in, load_out, load_up, load_down = weight_loads[layer]
        load_in.wait()
        stream_low = low[layer]
        note_square(layer, 0, flow[...])
        keys[layer, 0:rows, :] = nn(stream_low, win[layer, :, model : 2 * model]).astype(LOW)
        send_keys = sems.far(
            keys.at[layer, pl.ds(0, rows)], keys.at[layer, pl.ds(rows, rows)], to_core
        )
        send_keys.start()
        values[layer, 0:rows, :] = (
            nn(stream_low, win[layer, :, 2 * model : 3 * model]) + bias[1]
        ).astype(LOW)
        send_values = sems.far(
            values.at[layer, pl.ds(0, rows)], values.at[layer, pl.ds(rows, rows)], to_core
        )
        send_values.start()
        query = nn(stream_low, win[layer, :, 0:model]) + bias[0]
        query_low[layer] = (query * (SCALE / math.log(2.0))).astype(LOW)
        query_t[layer] = query_low[layer].T
        turned[:, 0:rows] = values[layer, 0:rows, :].T
        def score(head, begin=0, end=length, layer=layer):
            pair = head // 2
            scores[head % 2, begin:end] = (
                nn(
                    keys[layer, begin:end, 128 * pair : 128 * pair + 128],
                    pad_head(query_t[layer, 64 * head : 64 * head + 64, :], head % 2),
                )
                + mask[begin:end]
            )

        score(0, 0, rows)
        send_keys.wait()
        score(0, rows, length)
        for head in range(HEADS):
            if head + 1 < HEADS:
                score(head + 1)
            if head == 0:
                send_values.wait()
                turned[:, rows:length] = values[layer, rows:length, :].T
            if layer > 0:
                spills[layer - 1][head].wait()
            block = scores[head % 2]
            best = jnp.max(block, axis=0, keepdims=True)
            weight = jnp.exp2(block - best)
            inverse = 1.0 / jnp.sum(weight, axis=0, keepdims=True)
            weight_low = weight.astype(LOW)
            weights_t[head] = weight_low
            span = slice(64 * head, 64 * head + 64)
            inverse_total[layer, head : head + 1, :] = inverse
            attended_t[layer, span, :] = nn(turned[span, :], weight_low) * inverse
            if layer + 1 < LAYERS:
                if head == 0:
                    spills.append([])
                copy = sems.local(weights_t.at[head], kept_hbm.at[layer, head])
                copy.start()
                spills[layer].append(copy)
        attended_low[layer] = attended_t[layer].T.astype(LOW)
        load_out.wait()
        branch = nn(attended_low[layer], wout[layer]) + bias[2]
        note_square(layer, 1, branch)
        total = flow[...] + branch
        centred = total - jnp.mean(total, axis=-1, keepdims=True)
        inverse = lax.rsqrt(jnp.mean(centred * centred, axis=-1, keepdims=True) + EPS)
        normed = centred * inverse
        normed_one[layer] = normed.astype(LOW)
        inverse_norm[:, 2 * layer : 2 * layer + 1] = inverse
        hidden = normed * gain[0] + bias[5]
        flow[...] = hidden
        hidden_low[layer] = hidden.astype(LOW)
        load_up.wait()
        inner = nn(hidden_low[layer], wup[layer]) + bias[3]
        share = 0.5 * (1.0 + lax.erf(inner * 0.7071067811865476))
        active_low[layer] = (inner * share).astype(LOW)
        slope_low[layer] = (
            share + inner * jnp.exp(-0.5 * inner * inner) * 0.3989422804014327
        ).astype(LOW)
        load_down.wait()
        ff_out = nn(active_low[layer], wdn[layer]) + bias[4]
        note_square(layer, 2, ff_out)
        total = flow[...] + ff_out
        centred = total - jnp.mean(total, axis=-1, keepdims=True)
        inverse = lax.rsqrt(jnp.mean(centred * centred, axis=-1, keepdims=True) + EPS)
        normed = centred * inverse
        normed_two[layer] = normed.astype(LOW)
        inverse_norm[:, 2 * layer + 1 : 2 * layer + 2] = inverse
        result = normed * gain[1] + bias[6]
        if layer + 1 < LAYERS:
            flow[...] = result
            low[layer + 1] = result.astype(LOW)
        else:
            staged[...] = result.astype(LOW).reshape(staged.shape)

    away_result = [
        sems.far(staged.at[i, j], lo_hbm.at[i, j], to_diag) for i in range(2) for j in range(2)
    ]
    stay_result = sems.local(staged, lo_hbm)
    strips = [pl.ds(rows // 4 * k, rows // 4) for k in range(4)]
    away_grad = [sems.far(outer.at[strip], ig_hbm.at[0, strip], to_diag) for strip in strips]
    stay_grad = sems.local(outer, ig_hbm.at[0])

    @pl.when(moved)
    def _():
        away_outer.wait()

    @pl.when(jnp.logical_not(moved))
    def _():
        stay_outer.wait()
        stay_result.start()

    piece = model // 8 // levels
    own_rows = pl.ds(pl.multiple_of(z * piece, piece), piece)
    clock = Clock()

    def reduce_chunk(buffers, begin, count, home):
        return loads_of(buffers, count), steps_of(buffers, begin, count, home)

    def share_of(width):
        return width // 256 * 128

    def loads_of(buffers, count):
        width = buffers[0].shape[-1]
        size = count * width / model
        part = share_of(width) / width
        first = {"x": 2.88 * part * size, "y": 2.88 * (1 - part) * size}
        second = {"x": 1.44 * (1 - part) * size, "y": 1.44 * part * size}
        core_load, z_load = {"core": 0.46 * size}, {"z": 1.35 * size}
        return [core_load, first, second, z_load, z_load, second, first, core_load]

    def steps_of(buffers, begin, count, home):
        mine, whole, take_core, take_x, take_y, take_ay, take_bx, take_z = buffers
        width = mine.shape[-1]
        some = pl.ds(begin, count)
        landed = pl.ds(begin % take_core.shape[0], count)
        split = share_of(width)
        left, right = pl.ds(0, split), pl.ds(split, width - split)
        every = slice(None)
        first = sems.take_set()

        def send(src, dst, peer, index):
            copy = sems.far(src, dst, peer, first + index)
            copy.start()
            return copy

        def send_same(at, peer, index):
            return send(whole.at[at], whole.at[at], peer, index)

        def add_into(at, value):
            mine[at] = mine[at] + value

        def finish(copies):
            for copy in copies:
                copy.wait()

        mine_core, mine_left, mine_right = (
            (some, core),
            (some, core, x, every, every, left),
            (some, core, every, y, every, right),
        )
        deep_left, deep_right = (some, core, x, y, every, left), (some, core, x, y, every, right)
        own = (some, core, x, y, own_rows)
        by_core, by_x, by_y, by_y_deep, by_x_deep, back_core, by_z = 0, 1, 2, 3, 4, 5, 6
        back_z = by_z + levels - 1

        flight = [send(mine.at[some, 1 - core], take_core.at[landed], to_core, by_core)]
        yield
        finish(flight)
        add_into(mine_core, take_core[landed])
        flight = [
            send(mine.at[some, core, 1 - x, every, every, left], take_x.at[some], to_x, by_x),
            send(mine.at[some, core, every, 1 - y, every, right], take_y.at[some], to_y, by_y),
        ]
        yield
        finish(flight)
        add_into(mine_left, take_x[some])
        add_into(mine_right, take_y[some])
        flight = [
            send(mine.at[some, core, x, 1 - y, every, left], take_ay.at[some], to_y, by_y_deep),
            send(mine.at[some, core, 1 - x, y, every, right], take_bx.at[some], to_x, by_x_deep),
        ]
        yield
        finish(flight)
        add_into(deep_left, take_ay[some])
        add_into(deep_right, take_bx[some])
        flight = [
            send(
                mine.at[some, core, x, y, pl.ds(pl.multiple_of(level * piece, piece), piece)],
                take_z.at[step, some],
                at_z(level),
                by_z + step,
            )
            for step, level in enumerate(z_next)
        ]
        yield
        finish(flight)
        total = mine[own].astype(F32)
        for step in range(levels - 1):
            total = total + take_z[step, some].astype(F32)
        whole[own[:1] + own[2:]] = total.astype(LOW)
        flight = [
            send_same(own[:1] + own[2:], at_z(level), back_z + step)
            for step, level in enumerate(z_next)
        ]
        yield
        finish(flight)
        flight = [
            send_same((some, x, y, every, left), to_y, by_y),
            send_same((some, x, y, every, right), to_x, by_x),
        ]
        yield
        finish(flight)
        flight = [
            send_same((some, x, every, every, left), to_x, by_x_deep),
            send_same((some, every, y, every, right), to_y, by_y_deep),
        ]
        yield
        finish(flight)
        flight = [send(whole.at[some], home, to_core, back_core)]
        copy = sems.local(whole.at[some], home)
        copy.start()
        homing.append(copy)
        yield
        finish(flight)
        sems.spare.append(first)

    def send_home(copies):
        for copy in copies:
            pl.when(moved)(copy.start)
            yield
        for copy in copies:
            pl.when(moved)(copy.wait)

    def reduce_small():
        for step, peer in enumerate((to_core, to_x, to_y)):
            copy = sems.far(small.at[step], small_in.at[step], peer)
            copy.start()
            yield
            copy.wait()
            small[step + 1] = small[step] + small_in[step]
        copies = [sems.far(small.at[3], small_z.at[z], at_z(level)) for level in z_next]
        for copy in copies:
            copy.start()
        small_z[z] = small[3]
        yield
        for copy in copies:
            copy.wait()
        total = small_z[0]
        for level in range(1, levels):
            total = total + small_z[level]
        small_in[0] = total
        copy = sems.local(small_in.at[0], small_ref)
        copy.start()
        homing.append(copy)

    homing = []
    active = []

    def advance(entry):
        loads = entry[2]
        if next(entry[1], True):
            active.remove(entry)
            clock.now += 0.1
        else:
            clock.now += 0.25
            entry[0] = clock.transfer(loads.pop(0))

    def begin(chunk):
        loads, steps = chunk
        entry = [0.0, steps, loads, True]
        active.append(entry)
        advance(entry)

    def begin_home(copies):
        entry = [clock.now, send_home(copies), [{"x": 1.45} for _ in copies], False]
        active.append(entry)
        return entry

    def when(entry):
        if not entry[2]:
            return entry[0]
        if not entry[3]:
            return max(clock.now, clock.free["x"] - HOME_QUEUE)
        return max(entry[0], clock.opens(entry[2][0]))

    def pump(spent):
        clock.now += spent
        while True:
            ready = [entry for entry in active if when(entry) <= clock.now]
            if not ready:
                return
            advance(max(ready, key=lambda entry: (entry[3], len(entry[2]), active.index(entry))))

    def note(row, value):
        small[0, row : row + 1, :] = value

    reloads = []
    result_home = begin_home(away_result)
    flow[...] = outer[...].astype(F32)
    for layer in reversed(range(LAYERS)):
        gain = [gains_ref[layer, k : k + 1, :] for k in range(2)]
        base = 3 * (LAYERS - 1 - layer)
        wide = pairs * (LAYERS - 1 - layer)
        mine = square_sum[0]
        folded = mine.shape[1:]
        bias_row = 4 + 7 * layer
        turned[...] = keys[layer].T
        grad = flow[...]
        normed = normed_two[layer].astype(F32)
        note(2 * layer + 1, column_sum(grad * normed))
        note(bias_row + 6, column_sum(grad))
        scaled = grad * gain[1]
        second = inverse_norm[:, 2 * layer + 1 : 2 * layer + 2] * (
            scaled
            - jnp.mean(scaled, axis=-1, keepdims=True)
            - normed * jnp.mean(scaled * normed, axis=-1, keepdims=True)
        )
        scores[0, 0:rows, :] = second
        down_low = second.astype(LOW)
        note(bias_row + 4, column_sum(down_low))
        mine[base] = tn(active_low[layer], down_low).astype(LOW).reshape(folded)
        inner_low = (nt(down_low, wdn[layer]) * slope_low[layer].astype(F32)).astype(LOW)
        note(bias_row + 3, column_sum(inner_low))
        mine[base + 1] = tn(hidden_low[layer], inner_low).astype(LOW).reshape(folded)
        pump(2.6)
        begin(
            reduce_chunk(
                square_sum,
                base,
                2,
                gsq_hbm.at[layer, pl.ds(0, 2), core],
            )
        )
        grad = scores[0, 0:rows, :] + nt(inner_low, wup[layer])
        normed = normed_one[layer].astype(F32)
        note(2 * layer, column_sum(grad * normed))
        note(bias_row + 5, column_sum(grad))
        scaled = grad * gain[0]
        flow[...] = inverse_norm[:, 2 * layer : 2 * layer + 1] * (
            scaled
            - jnp.mean(scaled, axis=-1, keepdims=True)
            - normed * jnp.mean(scaled * normed, axis=-1, keepdims=True)
        )
        branch_low = flow[...].astype(LOW)
        note(bias_row + 2, column_sum(branch_low))
        mine[base + 2] = tn(attended_low[layer], branch_low).astype(LOW).reshape(folded)
        pump(1.2)
        begin(
            reduce_chunk(square_sum, base + 2, 1, gsq_hbm.at[layer, pl.ds(2, 1), core])
        )
        attended_grad_t = nt(branch_low, wout[layer]).astype(LOW).T
        for head in range(HEADS):
            span = slice(64 * head, 64 * head + 64)
            grad_low_t[span, :] = (
                attended_grad_t[span, :].astype(F32) * inverse_total[layer, head : head + 1, :]
            ).astype(LOW)
        grad_low[...] = grad_low_t[...].T
        pump(1.0)
        gives = []

        def close_pairs(chosen, layer=layer, wide=wide, bias_row=bias_row, gives=gives):
            mine = wide_sum[0]
            parts = []
            for pair in chosen:
                side = slice(128 * pair, 128 * pair + 128)
                gives[pair].wait()
                taken = [take[layer, pair, which].astype(F32) for which in range(2)]
                three = [
                    query_grad_t[side, :].T,
                    (mask[0:rows, side] + taken[0]).astype(LOW),
                    (mask[rows:length, side] + taken[1]).astype(LOW),
                ]
                small[0, bias_row : bias_row + 1, side] = column_sum(three[0])
                small[0, bias_row + 1 : bias_row + 2, side] = column_sum(three[2])
                parts += three
            part = jnp.concatenate(parts, axis=1)
            product = tn(low[layer], part).astype(LOW)
            for k, pair in enumerate(chosen):
                slot = wide + pair
                mine[slot] = product[:, 384 * k : 384 * k + 384].reshape(mine.shape[1:])
            first, count = wide + chosen[0], len(chosen)
            home = gin_hbm.at[layer, pl.ds(chosen[0], count), core]
            pump(0.4 * count)
            begin(reduce_chunk(wide_sum, first, count, home))
            weight = jnp.concatenate(
                [
                    win[layer, :, model * k + 128 * pair : model * k + 128 * pair + 128]
                    for pair in chosen
                    for k in range(3)
                ],
                axis=1,
            )
            total = flow[...] + nt(part, weight)
            if layer > 0 or chosen[-1] < pairs - 1:
                flow[...] = total
            else:
                outer[...] = total.astype(LOW)

        first_half = lax.broadcasted_iota(jnp.int32, (1, 128), 1) < HEAD_DIM
        for head in range(HEADS):
            pair = head // 2
            span = slice(64 * head, 64 * head + 64)
            lanes = slice(128 * pair, 128 * pair + 128)
            grad_part = grad_low_t[span, :]
            delta = column_sum(grad_part.astype(F32) * attended_t[layer, span, :])
            if layer + 1 < LAYERS:
                reloads[head].wait()
            prob_grad = nn(values[layer, :, lanes], pad_head(grad_part, head % 2))
            score_grad = (weights_t[head].astype(F32) * (prob_grad - delta)).astype(LOW)
            query_grad_t[span, :] = (nn(turned[span, :], score_grad) * SCALE).astype(LOW)
            key_part = nn(score_grad, query_low[layer, :, lanes])
            value_part = nn(weights_t[head], grad_low[:, lanes])
            if head % 2 == 0:
                key_even, value_even = key_part, value_part
            else:
                key_grad = jnp.where(first_half, key_even, key_part) * math.log(2.0)
                value_grad = jnp.where(first_half, value_even, value_part)
                mask[0:rows, lanes] = key_grad[0:rows]
                mask[rows:length, lanes] = value_grad[0:rows]
                give[pair, 0] = key_grad[rows:length].astype(LOW)
                give[pair, 1] = value_grad[rows:length].astype(LOW)
                copy = sems.far(give.at[pair], take.at[layer, pair], to_core)
                copy.start()
                gives.append(copy)
            if layer > 0:
                copy = sems.local(kept_hbm.at[layer - 1, head], weights_t.at[head])
                copy.start()
                reloads.append(copy)
            pump(1.15)
            if layer > 0 and head == HEADS // 2:
                close_pairs([0, 1])
            if layer == 0 and head % 2 == 0 and head > 0:
                close_pairs([pair - 1])
        close_pairs([2, 3] if layer > 0 else [3])
        if layer == 0:
            begin(([{"core": 0.1}, {"x": 1.5}, {"y": 1.5}, {"z": 2.0}], reduce_small()))
        if layer > 0:

            while result_home in active:
                advance(result_home)

            @pl.when(jnp.logical_not(moved))
            def _():
                stay_result.wait()

        pump(0.4)

    begin_home(away_grad)

    @pl.when(jnp.logical_not(moved))
    def _():
        stay_grad.start()

    while active:
        clock.now = max(clock.now, min(when(entry) for entry in active))
        pump(0.0)
    for copy in homing:
        copy.wait()

    @pl.when(jnp.logical_not(moved))
    def _():
        stay_grad.wait()

    assert sems.far_used <= FAR_SEMS and sems.near_used <= NEAR_SEMS


def local_pair(
    tokens,
    cell_starts,
    generate_flags,
    valid_mask,
    in_weight,
    out_weight,
    up_weight,
    down_weight,
    norm_gains,
    biases,
    out_grad,
):
    rows, model = tokens.shape[1:]
    length = 2 * rows
    levels = lax.axis_size("dp") // 4
    eighth = model // 8
    folded = (2, 2, 2, eighth)

    def sum_buffers(count, shared, width):
        split = width // 256 * 128
        return [
            pltpu.VMEM((count,) + folded + (width,), LOW),
            pltpu.VMEM((count,) + folded[1:] + (width,), LOW),
            pltpu.VMEM((shared,) + folded[1:] + (width,), LOW),
            pltpu.VMEM((count, 2, eighth, split), LOW),
            pltpu.VMEM((count, 2, eighth, width - split), LOW),
            pltpu.VMEM((count, eighth, split), LOW),
            pltpu.VMEM((count, eighth, width - split), LOW),
            pltpu.VMEM((max(levels - 1, 1), count, eighth // levels, width), LOW),
        ]

    shape = jax.ShapeDtypeStruct
    anywhere = pl.BlockSpec(memory_space=pl.ANY)
    by_layer = (LAYERS, rows, model)
    scratch = [
        pltpu.VMEM(cell_starts.shape, jnp.int32),
        pltpu.VMEM(generate_flags.shape, jnp.int32),
        pltpu.VMEM(valid_mask.shape, jnp.int32),
        pltpu.VMEM(norm_gains.shape, F32),
        pltpu.VMEM((7, LAYERS, model), F32),
        pltpu.VMEM(in_weight.shape, LOW),
        pltpu.VMEM(out_weight.shape, LOW),
        pltpu.VMEM(up_weight.shape, LOW),
        pltpu.VMEM(down_weight.shape, LOW),
        pltpu.VMEM(by_layer, LOW),
        pltpu.VMEM((rows, model), LOW),
        pltpu.VMEM((LAYERS, length, model), LOW),
        pltpu.VMEM((LAYERS, length, model), LOW),
        pltpu.VMEM((model, length), LOW),
        pltpu.VMEM(by_layer, LOW),
        pltpu.VMEM((LAYERS, model, rows), LOW),
        pltpu.VMEM((HEADS, length, rows), LOW),
        pltpu.VMEM((LAYERS, model, rows), F32),
        pltpu.VMEM(by_layer, LOW),
        pltpu.VMEM((LAYERS, HEADS, rows), F32),
        pltpu.VMEM(by_layer, LOW),
        pltpu.VMEM(by_layer, LOW),
        pltpu.VMEM((rows, 2 * LAYERS), F32),
        pltpu.VMEM(by_layer, LOW),
        pltpu.VMEM(by_layer, LOW),
        pltpu.VMEM(by_layer, LOW),
        pltpu.VMEM((2, length, rows), F32),
        pltpu.VMEM((length, rows), F32),
        pltpu.VMEM((rows, model), F32),
        pltpu.VMEM((model, rows), LOW),
        pltpu.VMEM((rows, model), LOW),
        pltpu.VMEM((model, rows), LOW),
        pltpu.VMEM((HEADS // 2, 2, rows, 128), LOW),
        pltpu.VMEM((LAYERS, HEADS // 2, 2, rows, 128), LOW),
        pltpu.VMEM((8, length), F32),
        pltpu.VMEM((8, length), F32),
        pltpu.VMEM((4, SMALL_ROWS, model), F32),
        pltpu.VMEM((3, SMALL_ROWS, model), F32),
        pltpu.VMEM((levels, SMALL_ROWS, model), F32),
        *sum_buffers(3 * LAYERS, 3, model),
        *sum_buffers(HEADS // 2 * LAYERS, HEADS // 2, 384),
        pltpu.SemaphoreType.DMA((FAR_SEMS,)),
        pltpu.SemaphoreType.DMA((FAR_SEMS,)),
        pltpu.SemaphoreType.DMA((NEAR_SEMS,)),
    ]
    lo, ig, gin, gsq, small, _ = pl.pallas_call(
        functools.partial(fused_kernel, levels),
        out_shape=[
            shape(folded + (model,), LOW),
            shape(tokens.shape, LOW),
            shape((LAYERS, HEADS // 2) + folded + (384,), LOW),
            shape((LAYERS, 3) + folded + (model,), LOW),
            shape((SMALL_ROWS, model), F32),
            shape((LAYERS - 1, HEADS, length, rows), LOW),
        ],
        in_specs=[anywhere] * 11,
        out_specs=[anywhere] * 6,
        scratch_shapes=scratch,
        compiler_params=pltpu.CompilerParams(
            collective_id=0, has_side_effects=True, vmem_limit_bytes=VMEM_BYTES
        ),
    )(
        tokens,
        cell_starts,
        generate_flags,
        valid_mask,
        in_weight,
        out_weight,
        up_weight,
        down_weight,
        norm_gains,
        biases.transpose(1, 0, 2),
        out_grad,
    )
    return finish(tokens, in_weight, lo, ig, gin, gsq, small)


VMEM_BYTES = 63 * 1024 * 1024


def finish_kernel(model, *refs):
    lo_in, ig_in, gin_in, gsq_in, small = refs[:5]
    lo, ig, gin, gout, gup, gdn, gains, shifts, rms = refs[5:14]
    low_wide, wide, low_square, square, passing, in_sems, out_sems = refs[14:]
    pairs = gin_in.shape[1]
    reads, writes = [], []

    def read(src, dst):
        copy = pltpu.make_async_copy(src, dst, in_sems.at[len(reads)])
        copy.start()
        reads.append(copy)
        return copy

    def write(src, dst):
        copy = pltpu.make_async_copy(src, dst, out_sems.at[len(writes)])
        copy.start()
        writes.append(copy)

    def widen_square(slot, copy, target):
        copy.wait()
        square[slot] = low_square[slot].astype(F32)
        write(square.at[slot], target)

    reads_lo = read(lo_in, passing)
    reads_square, reads_wide = [], []
    for layer in range(LAYERS):
        for k in range(3):
            reads_square.append(read(gsq_in.at[layer, k], low_square.at[3 * layer + k]))
            if k == 0:
                for pair in range(pairs):
                    reads_wide.append(
                        read(gin_in.at[layer, pair], low_wide.at[pairs * layer + pair])
                    )
    reads_ig = read(ig_in.at[0], low_square.at[3 * LAYERS])
    for layer in range(LAYERS):
        for k in range(2):
            row = 2 * layer + k
            gains[layer, k : k + 1, :] = small[row : row + 1, :]
        for k in range(7):
            row = 2 * LAYERS + 7 * layer + k
            shifts[k, layer : layer + 1, :] = small[row : row + 1, :]
    first = 9 * LAYERS
    count = jnp.sum(small[first + 3 * LAYERS : first + 3 * LAYERS + 1, :], keepdims=True)
    line = lax.broadcasted_iota(jnp.int32, rms.shape, 0)
    place = lax.broadcasted_iota(jnp.int32, rms.shape, 1)
    squares = jnp.zeros(rms.shape, F32)
    for layer in range(LAYERS):
        for k in range(3):
            row = first + 3 * layer + k
            value = jnp.sum(small[row : row + 1, :], keepdims=True)
            squares = jnp.where((line == layer) & (place == k), value, squares)
    rms[...] = jnp.sqrt(squares / (count * model))
    reads_lo.wait()
    write(passing, lo)
    for layer in range(LAYERS):
        for k, target in enumerate((gdn, gup, gout)):
            slot = 3 * layer + k
            widen_square(slot, reads_square[slot], target.at[layer])
            if k == 0:
                for pair in range(pairs):
                    slot = pairs * layer + pair
                    reads_wide[slot].wait()
                    for part in range(3):
                        begin = model * part + 128 * pair
                        wide[layer, :, begin : begin + 128] = low_wide[
                            slot, :, 128 * part : 128 * part + 128
                        ].astype(F32)
                write(wide.at[layer], gin.at[layer])
    widen_square(3 * LAYERS, reads_ig, ig.at[0])
    for copy in writes:
        copy.wait()


def finish(tokens, in_weight, lo, ig, gin, gsq, small):
    rows, model = tokens.shape[1:]
    shape = jax.ShapeDtypeStruct
    vmem, far = pl.BlockSpec(memory_space=pltpu.VMEM), pl.BlockSpec(memory_space=pltpu.HBM)
    square = (LAYERS, model, model)
    slots = LAYERS * HEADS // 2
    outs = pl.pallas_call(
        functools.partial(finish_kernel, model),
        out_shape=[
            shape(tokens.shape, LOW),
            shape(tokens.shape, F32),
            shape(in_weight.shape, F32),
            shape(square, F32),
            shape(square, F32),
            shape(square, F32),
            shape((LAYERS, 2, model), F32),
            shape((7, LAYERS, model), F32),
            shape((LAYERS, 3), F32),
        ],
        in_specs=[far] * 4 + [vmem],
        out_specs=[far] * 6 + [vmem] * 3,
        scratch_shapes=[
            pltpu.VMEM((slots, model, 384), LOW),
            pltpu.VMEM(in_weight.shape, F32),
            pltpu.VMEM((3 * LAYERS + 1, model, model), LOW),
            pltpu.VMEM((3 * LAYERS + 1, model, model), F32),
            pltpu.VMEM(tokens.shape, LOW),
            pltpu.SemaphoreType.DMA((slots + 3 * LAYERS + 2,)),
            pltpu.SemaphoreType.DMA((4 * LAYERS + 2,)),
        ],
        compiler_params=pltpu.CompilerParams(vmem_limit_bytes=VMEM_BYTES),
    )(
        lo.reshape(tokens.shape),
        ig,
        gin.reshape(LAYERS, HEADS // 2, model, 384),
        gsq.reshape(LAYERS, 3, model, model),
        small,
    )
    lo, ig, gin, gout, gup, gdn, gains, shifts, rms = outs
    return lo, ig, gin, gout, gup, gdn, gains, shifts.transpose(1, 0, 2), rms


def solution(mesh):
    placed = (
        P("dp", "seq", None),
        P("dp", None),
        P("dp", None),
        P("dp", None),
        P(),
        P(),
        P(),
        P(),
        P(),
        P(),
        P("dp", "seq", None),
    )
    paired = mesh.shape["seq"] == 2 and mesh.shape["dp"] % 4 == 0
    return jax.shard_map(
        local_pair if paired else local,
        mesh=mesh,
        in_specs=placed,
        out_specs=(P("dp", "seq", None), P("dp", "seq", None), P(), P(), P(), P(), P(), P(), P()),
        check_vma=False,
    )
```
